128 devices in a mesh: section: 2 (over core), dp: 64 (over x, z, y).
Axes of the slice: x: 4, y: 4, z: 4, core: 2. Of those that a mesh axis runs over, the one named last changes fastest.
Arguments:
- frames: bfloat16 [131072, 512], P('dp'), may hold values from -6 to 6
- cotangent: bfloat16 [131072, 512], P('dp'), may hold values from -6 to 6
- lengths: int32 [256, 4], P('dp'), may hold values from 1 to 256, 512 in all within a row
- bw_ids: int32 [256, 4], P('dp'), may hold values from 0 to 3
- conv_weight: float32 [2, 7, 512], P('section'), may hold values from -2 to 2
- conv_bias: float32 [2, 512], P('section'), may hold values from -4 to 4
- scale_table: float32 [2, 4, 512], P('section'), may hold values from 0.1 to 1.9
- shift_table: float32 [2, 4, 512], P('section'), may hold values from -3 to 3
- w_up: bfloat16 [2, 512, 1536], P('section'), may hold values from -0.25 to 0.25
- b_up: float32 [2, 1536], P('section'), may hold values from -3 to 3
- w_down: bfloat16 [2, 1536, 512], P('section'), may hold values from -0.15625 to 0.15625
- b_down: float32 [2, 512], P('section'), may hold values from -3 to 3
- layer_scale: float32 [2, 512], P('section'), may hold values from 0.5 to 1.5
Outputs:
- acts: bfloat16 [2, 131072, 512], P('section', 'dp')
- in_grad: float32 [2, 131072, 512], P('section', 'dp')
- g_conv_weight: float32 [2, 7, 512], P('section')
- g_conv_bias: float32 [2, 512], P('section')
- g_scale_table: float32 [2, 4, 512], P('section')
- g_shift_table: float32 [2, 4, 512], P('section')
- g_w_up: float32 [2, 512, 1536], P('section')
- g_b_up: float32 [2, 1536], P('section')
- g_w_down: float32 [2, 1536, 512], P('section')
- g_b_down: float32 [2, 512], P('section')
- g_layer_scale: float32 [2, 512], P('section')
The draws below stay inside these ranges and needn't reach their ends.
Inputs may be any that keep to these rules, and one draw needn't show every extreme that they name: Each row holds the lengths of the 4 clips of one micro-batch of one device, in order, summing to 512; the largest of each row is 256.
All inputs are finite; a program needn't handle non-finite values.
Results may differ from the reference program's by a relative error of at most 0.0074.
Values may be sent and summed in bfloat16 or wider, within the bound.
A program may use at most 192 MiB of HBM per device.

```python
import math
import jax
import jax.numpy as jnp
import numpy as np
from jax import lax

D = 512
FF = 1536
BANDS = 4
KERNEL = 7
MICRO = 4
CLIPS = 4
SPAN = 512
ROWS = 256
TOKENS = 131072
N_DP = 64


def with_ends(entries, own_key, least, top_value):
    extent = entries.shape
    index_at = [jax.random.randint(jax.random.fold_in(own_key, axis), (), 0, extent[axis]) for axis in range(len(extent))]
    entries = entries.at[tuple(index_at)].set(least)
    longest = extent.index(max(extent))
    index_at[longest] = (index_at[longest] + 1) % extent[longest]
    return entries.at[tuple(index_at)].set(top_value)


def shard_levels(rng, dims, split, smallest, top_value):
    def one(dim, blocks):
        heights = jax.random.uniform(jax.random.fold_in(jax.random.fold_in(rng, 6), dim), (blocks,), jnp.float32, smallest / len(split), top_value / len(split))
        return jnp.repeat(jnp.exp(heights), dims[dim] // blocks).reshape((-1,) + (1,) * (len(dims) - dim - 1))

    level = one(*split[0])
    for cut in split[1:]:
        level = level * one(*cut)
    return level


def profile(amount, total, limit, slope):
    portions = [(1 << 20) // math.isqrt(grade ** slope) + 1 for grade in range(2, amount + 1)]
    surplus, given = total - limit - (amount - 1), [1] * (amount - 1)
    while surplus > 0:
        free = [i for i in range(amount - 1) if given[i] < limit]
        whole, budget = sum([portions[i] for i in free]), surplus
        for i in free:
            addition = min(limit - given[i], max(1, budget * portions[i] // whole), surplus)
            given[i] = given[i] + addition
            surplus = surplus - addition
    return np.array([limit] + given)


def ragged_sizes(rng, number_of, total, reach, skew):
    if number_of == 2:
        one = jax.random.randint(rng, (), max(1, total - reach), min(reach, total - 1) + 1)
        return jnp.stack([one, total - one])
    tallies = jnp.asarray(profile(number_of, total, reach, skew), jnp.int32)
    pairs = (number_of - 1) // 2
    giver, receiver = tallies[1:1 + 2 * pairs:2], tallies[2:2 + 2 * pairs:2]
    slack = jnp.minimum(giver - 1, reach - receiver)
    passed = jax.random.randint(jax.random.fold_in(rng, 1), (pairs,), 0, 1 << 20) % (slack + 1)
    tallies = tallies.at[1:1 + 2 * pairs:2].set(giver - passed).at[2:2 + 2 * pairs:2].set(receiver + passed)
    return tallies[jax.random.permutation(jax.random.fold_in(rng, 2), number_of)]


def normal_values(own_key, shape, width, limit, cuts=(), kind=jnp.bfloat16):
    drawn = width * jax.random.normal(own_key, shape, jnp.float32)
    if cuts:
        drawn = drawn * shard_levels(own_key, shape, cuts, -0.22, 0.18)
    return jnp.clip(drawn, -limit, limit).astype(kind)


def setup_inputs(seed: int = 0) -> dict:
    seeds = jax.random.split(jax.random.key(seed), 14)
    return {
        "frames": normal_values(seeds[0], (TOKENS, D), 1.0, 6.0, ((0, 64),)),
        "cotangent": normal_values(seeds[1], (TOKENS, D), 1.0, 6.0, ((0, 64),)),
        "lengths": jax.vmap(lambda own: ragged_sizes(own, CLIPS, SPAN, SPAN // 2, 2))(jax.random.split(seeds[2], ROWS)).reshape((ROWS, CLIPS)).astype(jnp.int32),
        "bw_ids": with_ends(jax.random.randint(seeds[3], (ROWS, CLIPS), 0, BANDS), jax.random.fold_in(seeds[3], 1), 0, BANDS - 1).astype(jnp.int32),
        "conv_weight": normal_values(seeds[4], (2, KERNEL, D), KERNEL ** -0.5, 2.0, ((0, 2),), jnp.float32),
        "conv_bias": normal_values(seeds[5], (2, D), 1.0, 4.0, ((0, 2),), jnp.float32),
        "scale_table": jnp.clip(1.0 + 0.18 * jax.random.normal(seeds[6], (2, BANDS, D), jnp.float32), 0.1, 1.9),
        "shift_table": normal_values(seeds[7], (2, BANDS, D), 0.5, 3.0, ((0, 2),), jnp.float32),
        "w_up": normal_values(seeds[8], (2, D, FF), D ** -0.5, 0.25, ((0, 2),)),
        "b_up": normal_values(seeds[9], (2, FF), 0.5, 3.0, ((0, 2),), jnp.float32),
        "w_down": normal_values(seeds[10], (2, FF, D), FF ** -0.5, 0.15625, ((0, 2),)),
        "b_down": normal_values(seeds[11], (2, D), 0.5, 3.0, ((0, 2),), jnp.float32),
        "layer_scale": jnp.clip(0.5 + 1.0 * jax.random.uniform(seeds[12], (2, D), jnp.float32) ** shard_levels(seeds[12], (2, D), ((0, 2),), -0.2, 0.2), 0.5, 1.5),
    }


@jax.custom_vjp
def low(v):
    return lax.optimization_barrier(v.astype(jnp.bfloat16)).astype(jnp.float32)

@jax.custom_vjp
def low_back(v):
    return v

def low_keep(v):
    return (low(v), None)

def low_pass(kept, grad):
    return (grad,)

def back_keep(v):
    return (v, None)

def back_low(kept, grad):
    return (low(grad),)
low.defvjp(low_keep, low_pass)
low_back.defvjp(back_keep, back_low)

def frame_tables(row_lengths, row_ids):
    ends = jnp.cumsum(row_lengths, axis=-1)
    position = jnp.arange(SPAN, dtype=jnp.int32)
    segment = lax.optimization_barrier(jnp.sum((position[:, None] >= ends[..., None, :]).astype(jnp.int32), axis=-1))
    seg_hot = (segment[..., None] == jnp.arange(CLIPS, dtype=jnp.int32)).astype(jnp.float32)
    clip_hot = (row_ids[..., None] == jnp.arange(BANDS, dtype=jnp.int32)).astype(jnp.float32)
    band_hot = jnp.einsum('...tc,...ck->...tk', seg_hot, clip_hot, precision=lax.Precision.HIGHEST)
    return (segment, band_hot)

def prepare(inputs, segment, band_hot, taps, conv_b, scale_tab, shift_tab):
    length = inputs.shape[-2]
    lead = inputs.ndim - 2
    padded = jnp.pad(inputs, [(0, 0)] * lead + [(3, 3), (0, 0)])
    seg_pad = jnp.pad(segment, [(0, 0)] * lead + [(3, 3)], constant_values=-1)
    hidden = conv_b + jnp.zeros_like(inputs)
    for offset in range(KERNEL):
        moved = lax.slice_in_dim(padded, offset, offset + length, axis=lead)
        moved_seg = lax.slice_in_dim(seg_pad, offset, offset + length, axis=lead)
        hidden = hidden + jnp.where((moved_seg == segment)[..., None], moved, 0.0) * taps[offset]
    center = hidden - lax.optimization_barrier(jnp.mean(hidden, axis=-1, keepdims=True))
    spread = lax.optimization_barrier(jnp.mean(center * center, axis=-1, keepdims=True))
    normed = center * lax.rsqrt(spread + 1e-06)
    scale = jnp.einsum('...tk,kd->...td', band_hot, scale_tab, precision=lax.Precision.HIGHEST)
    shift = jnp.einsum('...tk,kd->...td', band_hot, shift_tab, precision=lax.Precision.HIGHEST)
    return normed * scale + shift

def apply_block(inputs, segment, band_hot, weights):
    taps, conv_b, scale_tab, shift_tab, up_w, up_b, down_w, down_b, gamma = weights
    adapted = low(prepare(inputs, segment, band_hot, taps, conv_b, scale_tab, shift_tab))
    up_val = low_back(jnp.einsum('...td,df->...tf', adapted, up_w, precision=lax.Precision.HIGHEST) + up_b)
    gelu_val = low(jax.nn.gelu(up_val, approximate=False))
    down_val = low_back(jnp.einsum('...tf,fd->...td', gelu_val, down_w, precision=lax.Precision.HIGHEST) + down_b)
    return inputs + gamma * down_val

def reference(frames, cotangent, lengths, bw_ids, conv_weight, conv_bias, scale_table, shift_table, w_up, b_up, w_down, b_down, layer_scale):
    params = tuple((p.astype(jnp.float32) for p in (conv_weight, conv_bias, scale_table, shift_table, w_up, b_up, w_down, b_down, layer_scale)))
    frames_g = frames.astype(jnp.float32).reshape(N_DP, MICRO, SPAN, D)
    cot_g = cotangent.astype(jnp.float32).reshape(N_DP, MICRO, SPAN, D)
    len_g = lengths.reshape(N_DP, MICRO, CLIPS)
    ids_g = bw_ids.reshape(N_DP, MICRO, CLIPS)

    def group_step(totals, pieces):
        block_x, block_cot, block_len, block_ids = pieces
        segment, band_hot = frame_tables(block_len, block_ids)

        def forward(inputs, extra, weights):
            lower = tuple((w[0] for w in weights))
            upper = tuple((w[1] for w in weights))
            first = low(apply_block(inputs, segment, band_hot, lower))
            return (first, apply_block(low_back(first + extra), segment, band_hot, upper))
        extra_zero = jnp.zeros((MICRO, SPAN, D), jnp.float32)
        (first, second), pullback = jax.vjp(forward, block_x, extra_zero, params)
        grad_x, grad_e, grad_w = pullback((jnp.zeros_like(first), block_cot))
        totals = jax.tree.map(jnp.add, totals, grad_w)
        return (totals, (first, second, grad_x, grad_e))
    start = tuple((jnp.zeros_like(p) for p in params))
    totals, (first, second, grad_x, grad_e) = lax.scan(group_step, start, (frames_g, cot_g, len_g, ids_g))
    acts = jnp.stack([first.reshape(TOKENS, D), second.reshape(TOKENS, D)]).astype(jnp.bfloat16)
    in_grad = jnp.stack([grad_x.reshape(TOKENS, D), grad_e.reshape(TOKENS, D)])
    return (acts, in_grad, totals[0], totals[1], totals[2], totals[3], totals[4], totals[5], totals[6], totals[7], totals[8])
```

```python
import functools
import math

import jax
import jax.numpy as jnp
import numpy as np
from jax import lax
from jax.experimental import pallas as pl
from jax.experimental.pallas import tpu as pltpu
from jax.sharding import PartitionSpec as P

BF = jnp.bfloat16
F32 = jnp.float32
MESH = pl.DeviceIdType.MESH
MIB = 2**20

SPAN = 512
D = 512
FF = 1536
ROWS = 2
M = ROWS * SPAN
HALO = 8
PADDED = SPAN + 2 * HALO
STEP = 64
TILE = 256
GRADS = 2 * FF
SMALL = 32
EXP_SCALE = -0.5 * math.log2(math.e)
PDF_SCALE = 1.0 / math.sqrt(2.0 * math.pi)
ERF_SCALE = 1.0 / math.sqrt(2.0)
TAPS, CBIAS, SCALE, SHIFT, DBIAS, GAMMA, UBIAS = 0, 7, 8, 12, 16, 17, 18
SMALL_ROWS = 21
OFFSETS = (0, 1, 2, 4, 5, 6)


def at(start, size):
    return slice(start, start + size) if isinstance(start, int) else pl.ds(start, size)


def times(index, size):
    return index * size if isinstance(index, int) else pl.multiple_of(index * size, size)


def over_rows(value):
    return jnp.sum(value.reshape(value.shape[0] // 8, 8, value.shape[1]), axis=0)


def dot(a, b, dims):
    return lax.dot_general(a, b, (dims, ((), ())), preferred_element_type=F32)


def clip_tables(first, lengths, ids, masks, hot):
    for r in range(ROWS):
        row = first + r
        ends = [lengths[row, 0]]
        for c in (1, 2):
            ends.append(ends[-1] + lengths[row, c])
        band_of = [ids[row, c] for c in range(4)]

        def segment(frame):
            return sum((frame >= end).astype(jnp.int32) for end in ends)

        @pl.loop(0, SPAN // STEP, unroll=2)
        def _(i):
            frame = lax.broadcasted_iota(jnp.int32, (STEP, 128), 0) + i * STEP
            lane = lax.broadcasted_iota(jnp.int32, (STEP, 128), 1)
            here = segment(frame)
            for q, k in enumerate(OFFSETS):
                there = frame + (k - 3)
                same = (segment(there) == here) & (there >= 0) & (there < SPAN)
                masks[r, q, at(times(i, STEP), STEP), :] = jnp.where(same, 1.0, 0.0)
            band = jnp.where(here == 2, band_of[2], band_of[3])
            band = jnp.where(here == 1, band_of[1], band)
            band = jnp.where(here == 0, band_of[0], band)
            one = (lane == band) | (lane == band + 4)
            hot[at(r * SPAN + times(i, STEP), STEP), :] = jnp.where(one, 1.0, 0.0).astype(BF)


def band_table(small, table):
    table[...] = jnp.zeros_like(table)
    for half, first in enumerate((SCALE, SHIFT)):
        whole = small[first : first + 4, :]
        upper = whole.astype(BF).astype(F32)
        both = jnp.concatenate([upper, whole - upper], axis=0)
        table[0:8, half * D : (half + 1) * D] = both.astype(BF)


def conv_norm(x, padded, masks, hot, table, small, normed, rstd_out, adapted):
    for r in range(ROWS):
        for j in range(4):
            padded[r, j, 0:HALO] = jnp.zeros((HALO, 128), F32)
            padded[r, j, HALO + SPAN :] = jnp.zeros((HALO, 128), F32)
            padded[r, j, HALO : HALO + SPAN] = x[r * SPAN : (r + 1) * SPAN, 128 * j : 128 * (j + 1)].astype(F32)

        @pl.loop(0, SPAN // STEP, unroll=8)
        def _(i):
            here = at(times(i, STEP), STEP)
            hidden = []
            for j in range(4):
                c = slice(128 * j, 128 * (j + 1))
                total = small[CBIAS : CBIAS + 1, c] + padded[r, j, at(times(i, STEP) + HALO, STEP), :] * small[3:4, c]
                for q, k in enumerate(OFFSETS):
                    moved = padded[r, j, pl.ds(i * STEP + (HALO + k - 3), STEP), :]
                    total = total + moved * masks[r, q, here, :] * small[k : k + 1, c]
                hidden.append(total)
            mean = jnp.sum(hidden[0] + hidden[1] + hidden[2] + hidden[3], axis=1, keepdims=True) * (1.0 / D)
            center = [h - mean for h in hidden]
            square = [c * c for c in center]
            spread = jnp.sum(square[0] + square[1] + square[2] + square[3], axis=1, keepdims=True) * (1.0 / D)
            rstd = lax.rsqrt(spread + 1e-6)
            rows = at(r * SPAN + times(i, STEP), STEP)
            tables = dot(hot[rows, :], table[...], ((1,), (0,)))
            rstd_out[rows, :] = jnp.broadcast_to(rstd, (STEP, 128))
            for j in range(4):
                c = slice(128 * j, 128 * (j + 1))
                n = center[j] * rstd
                normed[rows, c] = n
                adapted[rows, c] = (n * tables[:, c] + tables[:, D + 128 * j : D + 128 * (j + 1)]).astype(BF)


def up_gelu(adapted, w_up, small, g, slope):
    for i in range(M // TILE):
        rows = at(i * TILE, TILE)
        for c in range(FF // TILE):
            cols = at(c * TILE, TILE)
            bias = small[UBIAS + c // 2 : UBIAS + c // 2 + 1, at((c % 2) * TILE, TILE)]
            u = dot(adapted[rows, :], w_up[:, cols], ((1,), (0,))) + bias
            pdf = jnp.exp2((u * EXP_SCALE) * u) * PDF_SCALE
            cdf = 0.5 + 0.5 * lax.erf(u * ERF_SCALE)
            g[rows, cols] = (u * cdf).astype(BF)
            slope[rows, cols] = (cdf + u * pdf).astype(BF)


def down(x, g, w_down, small, out, upstream, v_out, g_gamma):
    for i in range(M // TILE):
        rows = at(i * TILE, TILE)
        for c in range(2):
            cols = at(c * TILE, TILE)
            v = dot(g[rows, :], w_down[:, cols], ((1,), (0,))) + small[DBIAS : DBIAS + 1, cols]
            out[rows, cols] = (x[rows, cols].astype(F32) + small[GAMMA : GAMMA + 1, cols] * v).astype(BF)
            if v_out is not None:
                v_out[rows, cols] = v.astype(BF)
            if upstream is not None:
                g_gamma[:, cols] += over_rows(upstream[rows, cols].astype(F32) * v)


def down_back(upstream, w_down, small, slope, dv_out, du_out, g_dbias, g_ubias, v, g_gamma):
    for i in range(M // TILE):
        rows = at(i * TILE, TILE)
        dy = upstream[rows, :].astype(F32)
        dv = small[GAMMA : GAMMA + 1, :] * dy
        g_dbias[...] += over_rows(dv)
        if v is not None:
            g_gamma[...] += over_rows(dy * v[rows, :].astype(F32))
        dv = dv.astype(BF)
        dv_out[rows, :] = dv
        for c in range(FF // TILE):
            cols = at(c * TILE, TILE)
            du = dot(dv, w_down[cols, :], ((1,), (1,))) * slope[rows, cols].astype(F32)
            du_out[rows, cols] = du.astype(BF)
            g_ubias[:, cols] += over_rows(du)


def down_grad(g, dv, out):
    for c in range(FF // TILE):
        cols = at(c * TILE, TILE)
        out[cols, :] = dot(g[:, cols], dv[...], ((0,), (0,))).astype(BF)


def up_grad(adapted, du, out):
    for c in range(FF // TILE):
        place = (at(FF + (c // 2) * D, D), at((c % 2) * TILE, TILE))
        out[place] = dot(adapted[...], du[:, at(c * TILE, TILE)], ((0,), (0,))).astype(BF)


def norm_back(du, w_up, hot, table, normed, rstd, d_hidden, g_table):
    half = 512
    for i in range(M // half):
        rows = at(i * half, half)
        da = dot(du[rows, :], w_up[...], ((1,), (1,)))
        n = normed[rows, :]
        dan = da * n
        ones = hot[rows, 0:16]
        g_table[:, 0:D] += dot(ones, dan.astype(BF), ((0,), (0,)))[0:8]
        g_table[:, D:] += dot(ones, da.astype(BF), ((0,), (0,)))[0:8]
        scale = dot(hot[rows, :], table[:, 0:D], ((1,), (0,)))
        dn = da * scale
        mean = jnp.sum(dn, axis=1, keepdims=True) * (1.0 / D)
        along = jnp.sum(dan * scale, axis=1, keepdims=True) * (1.0 / D)
        dh = (dn - mean - n * along) * rstd[rows, 0:1]
        r, first = i * half // SPAN, i * half % SPAN
        for j in range(4):
            d_hidden[r, j, at(HALO + first, half), :] = dh[:, 128 * j : 128 * (j + 1)]


def conv_back(x, upstream, d_hidden, masks, small, g_taps, g_cbias, out):
    for r in range(ROWS):
        for j in range(4):
            d_hidden[r, j, 0:HALO] = jnp.zeros((HALO, 128), F32)
            d_hidden[r, j, HALO + SPAN :] = jnp.zeros((HALO, 128), F32)

        @pl.loop(0, SPAN // STEP, unroll=2)
        def _(i):
            rows = at(r * SPAN + times(i, STEP), STEP)
            here = at(times(i, STEP), STEP)
            for j in range(4):
                c = slice(128 * j, 128 * (j + 1))
                value = x[rows, c].astype(F32)
                dh = d_hidden[r, j, at(times(i, STEP) + HALO, STEP), :]
                total = upstream[rows, c].astype(F32) + dh * small[3:4, c]
                g_cbias[:, c] += over_rows(dh)
                g_taps[3, :, c] += over_rows(value * dh)
                for q, k in enumerate(OFFSETS):
                    part = d_hidden[r, j, pl.ds(i * STEP + (HALO + k - 3), STEP), :] * masks[r, q, here, :]
                    total = total + part * small[6 - k : 7 - k, c]
                    g_taps[6 - k, :, c] += over_rows(value * part)
                out[rows, c] = total.astype(out.dtype)


def small_grads(out, g_taps, g_cbias, g_table, g_dbias, g_gamma, g_ubias):
    def whole(value):
        return jnp.sum(value, axis=0, keepdims=True)

    rows = [whole(g_taps[k]) for k in range(7)] + [whole(g_cbias[...])]
    rows += [g_table[0:4, 0:D], g_table[0:4, D:], whole(g_dbias[...]), whole(g_gamma[...])]
    rows += [whole(g_ubias[:, k * D : (k + 1) * D]) for k in range(3)]
    rows.append(jnp.zeros((SMALL - SMALL_ROWS, D), F32))
    out[...] = jnp.concatenate(rows, axis=0)


def compute_kernel(
    lengths, ids, frames, cotangent, own_small, far_small, own_up, far_up, own_down, far_down,
    acts_out, grad_out, weight_out, small_out,
    x0, cot, small, w_up, w_down, acts, grads, weight_grads, small_sums,
    padded, masks, hot, table, normed, rstd, adapted, g, slope, v0, dv, du, d_hidden,
    g_table, g_taps, g_cbias, g_dbias, g_ubias, g_gamma, in_sems, out_sems,
):
    section = lax.axis_index("section")
    mine = pl.ds(pl.multiple_of(section * M, M), M)
    loads = [
        pltpu.make_async_copy(frames.at[mine], x0, in_sems.at[0]),
        pltpu.make_async_copy(cotangent.at[mine], cot, in_sems.at[1]),
        pltpu.make_async_copy(own_small, small.at[section], in_sems.at[2]),
        pltpu.make_async_copy(far_small, small.at[1 - section], in_sems.at[3]),
        pltpu.make_async_copy(own_up, w_up.at[section], in_sems.at[4]),
        pltpu.make_async_copy(far_up, w_up.at[1 - section], in_sems.at[5]),
        pltpu.make_async_copy(own_down, w_down.at[section], in_sems.at[6]),
        pltpu.make_async_copy(far_down, w_down.at[1 - section], in_sems.at[7]),
    ]
    for load in loads:
        load.start()
    stores = []

    def store(src, dst):
        copy = pltpu.make_async_copy(src, dst, out_sems.at[len(stores)])
        copy.start()
        stores.append(copy)

    clip_tables(section * ROWS, lengths, ids, masks, hot)
    for ref in (g_table, g_taps, g_cbias, g_dbias, g_ubias, g_gamma):
        ref[...] = jnp.zeros_like(ref)
    for i in (0, 2, 3):
        loads[i].wait()
    for b in range(2):
        band_table(small.at[b], table.at[b])
    for b, x in ((0, x0), (1, acts.at[0])):
        conv_norm(x, padded, masks, hot, table.at[b], small.at[b], normed.at[b], rstd.at[b], adapted.at[b])
        if b == 0:
            for i in (4, 5, 6, 7, 1):
                loads[i].wait()
        up_gelu(adapted.at[b], w_up.at[b], small.at[b], g.at[b], slope.at[b])
        if b == 0:
            down(x, g.at[b], w_down.at[b], small.at[b], acts.at[0], None, v0, None)
        else:
            down(x, g.at[b], w_down.at[b], small.at[b], acts.at[1], cot, None, g_gamma.at[1])
        store(acts.at[b], acts_out.at[b])
    for b, x, dy in ((1, acts.at[0], cot), (0, x0, grads.at[1])):
        v = v0 if b == 0 else None
        down_back(
            dy, w_down.at[b], small.at[b], slope.at[b], dv, du, g_dbias.at[b], g_ubias.at[b], v, g_gamma.at[b]
        )
        down_grad(g.at[b], dv, weight_grads.at[b])
        up_grad(adapted.at[b], du, weight_grads.at[b])
        store(weight_grads.at[b], weight_out.at[b])
        norm_back(du, w_up.at[b], hot, table.at[b], normed.at[b], rstd.at[b], d_hidden, g_table.at[b])
        conv_back(x, dy, d_hidden, masks, small.at[b], g_taps.at[b], g_cbias.at[b], grads.at[b])
        store(grads.at[b], grad_out.at[b])
        small_grads(
            small_sums.at[b], g_taps.at[b], g_cbias.at[b], g_table.at[b], g_dbias.at[b], g_gamma.at[b], g_ubias.at[b]
        )
    store(small_sums, small_out)
    for copy in stores:
        copy.wait()


def compute(lengths, ids, *arrays):
    smem = pl.BlockSpec(memory_space=pltpu.SMEM)
    hbm = pl.BlockSpec(memory_space=pl.ANY)
    return pl.pallas_call(
        compute_kernel,
        out_shape=[
            jax.ShapeDtypeStruct((2, M, D), BF),
            jax.ShapeDtypeStruct((2, M, D), BF),
            jax.ShapeDtypeStruct((2, GRADS, D), BF),
            jax.ShapeDtypeStruct((2, SMALL, D), F32),
        ],
        in_specs=[smem, smem] + [hbm] * 8,
        out_specs=[hbm] * 4,
        scratch_shapes=[
            pltpu.VMEM((M, D), BF),
            pltpu.VMEM((M, D), BF),
            pltpu.VMEM((2, 24, D), F32),
            pltpu.VMEM((2, D, FF), BF),
            pltpu.VMEM((2, FF, D), BF),
            pltpu.VMEM((2, M, D), BF),
            pltpu.VMEM((2, M, D), BF),
            pltpu.VMEM((2, GRADS, D), BF),
            pltpu.VMEM((2, SMALL, D), F32),
            pltpu.VMEM((ROWS, 4, PADDED, 128), F32),
            pltpu.VMEM((ROWS, 6, SPAN, 128), F32),
            pltpu.VMEM((M, 128), BF),
            pltpu.VMEM((2, 128, 2 * D), BF),
            pltpu.VMEM((2, M, D), F32),
            pltpu.VMEM((2, M, 128), F32),
            pltpu.VMEM((2, M, D), BF),
            pltpu.VMEM((2, M, FF), BF),
            pltpu.VMEM((2, M, FF), BF),
            pltpu.VMEM((M, D), BF),
            pltpu.VMEM((M, D), BF),
            pltpu.VMEM((M, FF), BF),
            pltpu.VMEM((ROWS, 4, PADDED, 128), F32),
            pltpu.VMEM((2, 8, 2 * D), F32),
            pltpu.VMEM((2, 7, 8, D), F32),
            pltpu.VMEM((2, 8, D), F32),
            pltpu.VMEM((2, 8, D), F32),
            pltpu.VMEM((2, 8, FF), F32),
            pltpu.VMEM((2, 8, D), F32),
            pltpu.SemaphoreType.DMA((8,)),
            pltpu.SemaphoreType.DMA((8,)),
        ],
        compiler_params=pltpu.CompilerParams(vmem_limit_bytes=62 * MIB),
        cost_estimate=pl.CostEstimate(flops=24 * M * D * FF, bytes_accessed=24 * MIB, transcendentals=4 * M * FF),
    )(lengths, ids, *arrays)


PARTS = 3
PART_ROWS = GRADS // PARTS


def reduce_kernel(
    acts, grads, weight_grads, small_sums,
    acts_all, grads_all, weight_all, small_all,
    own, far, pair, got1, got2, got3, sum1, sum2, small_own, small_far, small_pair, small_got, small_sum,
    load_sems, pair_send, pair_recv, send, recv, back_send, back_recv, small_send, small_recv,
):
    section = lax.axis_index("section")
    dp = lax.axis_index("dp")
    coords = (dp // 16, (dp // 4) % 4, dp % 4)
    strides = (16, 4, 1)

    def peer(axis, distance):
        moved = lax.rem(coords[axis] + distance, 4)
        return {"dp": dp + (moved - coords[axis]) * strides[axis], "section": section}

    other = {"dp": dp, "section": 1 - section}

    loads = [
        pltpu.make_async_copy(weight_grads.at[1 - section], far, load_sems.at[0]),
        pltpu.make_async_copy(weight_grads.at[section], own, load_sems.at[1]),
        pltpu.make_async_copy(small_sums.at[1 - section], small_far, load_sems.at[2]),
        pltpu.make_async_copy(small_sums.at[section], small_own, load_sems.at[3]),
        pltpu.make_async_copy(acts.at[section], acts_all.at[pl.ds(pl.multiple_of(section * M, M), M)], load_sems.at[4]),
        pltpu.make_async_copy(grads.at[section], grads_all.at[pl.ds(pl.multiple_of(section * M, M), M)], load_sems.at[5]),
    ]
    for load in loads:
        load.start()

    barrier = pltpu.get_barrier_semaphore()
    pl.semaphore_signal(barrier, inc=1, device_id=other, device_id_type=MESH)
    for axis in range(3):
        for distance in (1, 2, 3):
            pl.semaphore_signal(barrier, inc=1, device_id=peer(axis, distance), device_id_type=MESH)
    pl.semaphore_wait(barrier, 10)

    def copy(src, dst, send_sem, recv_sem, device):
        made = pltpu.make_async_remote_copy(
            src_ref=src, dst_ref=dst, send_sem=send_sem, recv_sem=recv_sem, device_id=device, device_id_type=MESH
        )
        made.start()
        return made

    waits = []
    loads[0].wait()
    pairs = []
    for p in range(PARTS):
        rows = at(p * PART_ROWS, PART_ROWS)
        pairs.append(copy(far.at[rows], pair.at[rows], pair_send.at[p], pair_recv.at[p], other))
    loads[2].wait()
    pairs.append(copy(small_far, small_pair, pair_send.at[3], pair_recv.at[3], other))
    place = pl.ds(pl.multiple_of(section * M, M), M)
    pairs.append(copy(acts.at[1 - section], acts_all.at[place], pair_send.at[4], pair_recv.at[4], other))
    pairs.append(copy(grads.at[1 - section], grads_all.at[place], pair_send.at[5], pair_recv.at[5], other))
    loads[1].wait()
    loads[3].wait()

    def block(p, stage):
        first, size = p * PART_ROWS, PART_ROWS
        for s in range(stage):
            size //= 4
            first = first + coords[(p + s) % 3] * size
        return first, size

    def spread(p, stage, source, got):
        axis = (p + stage) % 3
        size = PART_ROWS // 4 ** (stage + 1)
        sent = []
        for distance in (1, 2, 3):
            to = lax.rem(coords[axis] + distance, 4)
            i = (p * 3 + stage) * 3 + distance - 1
            sent.append(
                copy(
                    source.at[pl.ds(pl.multiple_of(to * size, size), size)],
                    got.at[p, distance - 1],
                    send.at[i],
                    recv.at[i],
                    peer(axis, distance),
                )
            )
        return sent

    def total(p, stage, source, got):
        size = PART_ROWS // 4 ** (stage + 1)
        kept = source[pl.ds(pl.multiple_of(coords[(p + stage) % 3] * size, size), size), :].astype(F32)
        for d in range(3):
            kept = kept + got[p, d].astype(F32)
        return kept

    small_waits = []

    def small_spread(stage, axis, source_of, dst_of):
        sent = []
        for distance in (1, 2, 3):
            i = stage * 3 + distance - 1
            to = lax.rem(coords[axis] + distance, 4)
            sent.append(copy(source_of(to), dst_of(distance), small_send.at[i], small_recv.at[i], peer(axis, distance)))
        return sent

    flights = {}
    for p in range(PARTS):
        pairs[p].wait()
        rows = at(p * PART_ROWS, PART_ROWS)
        own[rows, :] = (own[rows, :].astype(F32) + pair[rows, :].astype(F32)).astype(BF)
        flights[p] = spread(p, 0, own.at[rows], got1)
    pairs[3].wait()
    small_own[...] += small_pair[...]

    def quarter(index):
        return pl.ds(pl.multiple_of(index * 8, 8), 8)

    small_flight = small_spread(0, 0, lambda to: small_own.at[quarter(to)], lambda d: small_got.at[0, d - 1])

    for p in range(PARTS):
        for sent in flights[p]:
            sent.wait()
        rows = at(p * PART_ROWS, PART_ROWS)
        sum1[p] = total(p, 0, own.at[rows], got1).astype(BF)
        flights[p] = spread(p, 1, sum1.at[p], got2)
    for sent in small_flight:
        sent.wait()
    small_sum[0] = small_own[quarter(coords[0]), :] + small_got[0, 0] + small_got[0, 1] + small_got[0, 2]
    small_flight = small_spread(1, 1, lambda to: small_sum.at[0], lambda d: small_got.at[1, d - 1])
    for p in range(PARTS):
        for sent in flights[p]:
            sent.wait()
        sum2[p] = total(p, 1, sum1.at[p], got2).astype(BF)
        flights[p] = spread(p, 2, sum2.at[p], got3)
    for sent in small_flight:
        sent.wait()
    small_sum[1] = small_sum[0] + small_got[1, 0] + small_got[1, 1] + small_got[1, 2]
    small_flight = small_spread(2, 2, lambda to: small_sum.at[1], lambda d: small_got.at[2, d - 1])

    def gather(p, stage):
        axis = (p + stage) % 3
        first, size = block(p, stage + 1)
        rows = pl.ds(pl.multiple_of(first, size), size)
        sent = []
        for distance in (1, 2, 3):
            i = (p * 3 + stage) * 3 + distance - 1
            sent.append(copy(weight_all.at[rows], weight_all.at[rows], back_send.at[i], back_recv.at[i], peer(axis, distance)))
        return sent

    for p in range(PARTS):
        for sent in flights[p]:
            sent.wait()
        first, size = block(p, 3)
        weight_all[pl.ds(pl.multiple_of(first, size), size), :] = total(p, 2, sum2.at[p], got3).astype(BF)
        flights[p] = gather(p, 2)
    for sent in small_flight:
        sent.wait()
    small_all[quarter(coords[0]), :] = small_sum[1] + small_got[2, 0] + small_got[2, 1] + small_got[2, 2]
    small_flight = small_spread(
        3, 0, lambda to: small_all.at[quarter(coords[0])], lambda d: small_all.at[quarter(coords[0])]
    )
    for stage in (1, 0):
        for p in range(PARTS):
            for sent in flights[p]:
                sent.wait()
            flights[p] = gather(p, stage)
    for p in range(PARTS):
        for sent in flights[p]:
            sent.wait()
    for sent in small_flight:
        sent.wait()
    pairs[4].wait()
    pairs[5].wait()
    loads[4].wait()
    loads[5].wait()


def reduce(acts, grads, weight_grads, small_sums):
    vmem = pl.BlockSpec(memory_space=pltpu.VMEM)
    hbm = pl.BlockSpec(memory_space=pl.ANY)
    quarter = PART_ROWS // 4
    return pl.pallas_call(
        reduce_kernel,
        out_shape=[
            jax.ShapeDtypeStruct((2 * M, D), BF),
            jax.ShapeDtypeStruct((2 * M, D), BF),
            jax.ShapeDtypeStruct((GRADS, D), BF),
            jax.ShapeDtypeStruct((SMALL, D), F32),
        ],
        in_specs=[hbm] * 4,
        out_specs=[hbm, hbm, vmem, vmem],
        scratch_shapes=[
            pltpu.VMEM((GRADS, D), BF),
            pltpu.VMEM((GRADS, D), BF),
            pltpu.VMEM((GRADS, D), BF),
            pltpu.VMEM((PARTS, 3, quarter, D), BF),
            pltpu.VMEM((PARTS, 3, quarter // 4, D), BF),
            pltpu.VMEM((PARTS, 3, quarter // 16, D), BF),
            pltpu.VMEM((PARTS, quarter, D), BF),
            pltpu.VMEM((PARTS, quarter // 4, D), BF),
            pltpu.VMEM((SMALL, D), F32),
            pltpu.VMEM((SMALL, D), F32),
            pltpu.VMEM((SMALL, D), F32),
            pltpu.VMEM((3, 3, 8, D), F32),
            pltpu.VMEM((2, 8, D), F32),
            pltpu.SemaphoreType.DMA((6,)),
            pltpu.SemaphoreType.DMA((6,)),
            pltpu.SemaphoreType.DMA((6,)),
            pltpu.SemaphoreType.DMA((27,)),
            pltpu.SemaphoreType.DMA((27,)),
            pltpu.SemaphoreType.DMA((27,)),
            pltpu.SemaphoreType.DMA((27,)),
            pltpu.SemaphoreType.DMA((12,)),
            pltpu.SemaphoreType.DMA((12,)),
        ],
        compiler_params=pltpu.CompilerParams(collective_id=0, has_side_effects=True, vmem_limit_bytes=40 * MIB),
    )(acts, grads, weight_grads, small_sums)


def shards(
    frames, cotangent, lengths, bw_ids, conv_weight, conv_bias, scale_table, shift_table,
    w_up, b_up, w_down, b_down, layer_scale,
):
    own_small = jnp.concatenate(
        [conv_weight[0], conv_bias, scale_table[0], shift_table[0], b_down, layer_scale, b_up.reshape(3, D),
         jnp.zeros((24 - SMALL_ROWS, D), F32)]
    )
    swap = [(0, 1), (1, 0)]
    far_small = lax.ppermute(own_small, "section", swap)
    far_up = lax.ppermute(w_up[0], "section", swap)
    far_down = lax.ppermute(w_down[0], "section", swap)
    acts, grads, weight_grads, small_sums = compute(
        lengths, bw_ids, frames, cotangent, own_small, far_small, w_up[0], far_up, w_down[0], far_down
    )
    acts, grads, weights, small = reduce(acts, grads, weight_grads, small_sums)
    g_down = weights[:FF].astype(F32)
    g_up = jnp.concatenate([weights[FF + k * D : FF + (k + 1) * D] for k in range(3)], axis=1).astype(F32)
    return (
        acts[None],
        grads.astype(F32)[None],
        small[None, TAPS : TAPS + 7],
        small[CBIAS : CBIAS + 1],
        small[None, SCALE : SCALE + 4],
        small[None, SHIFT : SHIFT + 4],
        g_up[None],
        small[UBIAS : UBIAS + 3].reshape(1, FF),
        g_down[None],
        small[DBIAS : DBIAS + 1],
        small[GAMMA : GAMMA + 1],
    )


def solution(mesh):
    rows = P("dp", None)
    matrix, vector = P("section", None, None), P("section", None)
    in_specs = (rows,) * 4 + (matrix, vector, matrix, matrix, matrix, vector, matrix, vector, vector)
    stacked = P("section", "dp", None)
    out_specs = (stacked, stacked, matrix, vector, matrix, matrix, matrix, vector, matrix, vector, vector)
    return jax.shard_map(shards, mesh=mesh, in_specs=in_specs, out_specs=out_specs, check_vma=False)
```

```python
import functools
import math

import jax
import jax.numpy as jnp
import numpy as np
from jax import lax
from jax.experimental import pallas as pl
from jax.experimental.pallas import tpu as pltpu
from jax.sharding import PartitionSpec as P

BF = jnp.bfloat16
F32 = jnp.float32
MESH = pl.DeviceIdType.MESH
MIB = 2**20

SPAN = 512
D = 512
FF = 1536
ROWS = 2
M = ROWS * SPAN
HALO = 8
PADDED = SPAN + 2 * HALO
STEP = 64
TILE = 256
GRADS = 2 * FF
SMALL = 32
EXP_SCALE = -0.5 * math.log2(math.e)
PDF_SCALE = 1.0 / math.sqrt(2.0 * math.pi)
ERF_SCALE = 1.0 / math.sqrt(2.0)
TAPS, CBIAS, SCALE, SHIFT, DBIAS, GAMMA, UBIAS = 0, 7, 8, 12, 16, 17, 18
SMALL_ROWS = 21
OFFSETS = (0, 1, 2, 4, 5, 6)


def at(start, size):
    return slice(start, start + size) if isinstance(start, int) else pl.ds(start, size)


def times(index, size):
    return index * size if isinstance(index, int) else pl.multiple_of(index * size, size)


def over_rows(value):
    return jnp.sum(value.reshape(value.shape[0] // 8, 8, value.shape[1]), axis=0)


def dot(a, b, dims):
    return lax.dot_general(a, b, (dims, ((), ())), preferred_element_type=F32)


def clip_tables(first, lengths, ids, masks, hot):
    for r in range(ROWS):
        row = first + r
        ends = [lengths[row, 0]]
        for c in (1, 2):
            ends.append(ends[-1] + lengths[row, c])
        band_of = [ids[row, c] for c in range(4)]

        def segment(frame):
            return sum((frame >= end).astype(jnp.int32) for end in ends)

        @pl.loop(0, SPAN // STEP, unroll=2)
        def _(i):
            frame = lax.broadcasted_iota(jnp.int32, (STEP, 128), 0) + i * STEP
            lane = lax.broadcasted_iota(jnp.int32, (STEP, 128), 1)
            here = segment(frame)
            for q, k in enumerate(OFFSETS):
                there = frame + (k - 3)
                same = (segment(there) == here) & (there >= 0) & (there < SPAN)
                masks[r, q, at(times(i, STEP), STEP), :] = jnp.where(same, 1.0, 0.0)
            band = jnp.where(here == 2, band_of[2], band_of[3])
            band = jnp.where(here == 1, band_of[1], band)
            band = jnp.where(here == 0, band_of[0], band)
            one = (lane == band) | (lane == band + 4)
            hot[at(r * SPAN + times(i, STEP), STEP), :] = jnp.where(one, 1.0, 0.0).astype(BF)


def band_table(small, table):
    table[...] = jnp.zeros_like(table)
    for half, first in enumerate((SCALE, SHIFT)):
        whole = small[first : first + 4, :]
        upper = whole.astype(BF).astype(F32)
        both = jnp.concatenate([upper, whole - upper], axis=0)
        table[0:8, half * D : (half + 1) * D] = both.astype(BF)


def conv_norm(x, padded, masks, hot, table, small, normed, rstd_out, adapted):
    for r in range(ROWS):
        for j in range(4):
            padded[r, j, 0:HALO] = jnp.zeros((HALO, 128), F32)
            padded[r, j, HALO + SPAN :] = jnp.zeros((HALO, 128), F32)
            padded[r, j, HALO : HALO + SPAN] = x[r * SPAN : (r + 1) * SPAN, 128 * j : 128 * (j + 1)].astype(F32)

        @pl.loop(0, SPAN // STEP, unroll=8)
        def _(i):
            here = at(times(i, STEP), STEP)
            hidden = []
            for j in range(4):
                c = slice(128 * j, 128 * (j + 1))
                total = small[CBIAS : CBIAS + 1, c] + padded[r, j, at(times(i, STEP) + HALO, STEP), :] * small[3:4, c]
                for q, k in enumerate(OFFSETS):
                    moved = padded[r, j, pl.ds(i * STEP + (HALO + k - 3), STEP), :]
                    total = total + moved * masks[r, q, here, :] * small[k : k + 1, c]
                hidden.append(total)
            mean = jnp.sum(hidden[0] + hidden[1] + hidden[2] + hidden[3], axis=1, keepdims=True) * (1.0 / D)
            center = [h - mean for h in hidden]
            square = [c * c for c in center]
            spread = jnp.sum(square[0] + square[1] + square[2] + square[3], axis=1, keepdims=True) * (1.0 / D)
            rstd = lax.rsqrt(spread + 1e-6)
            rows = at(r * SPAN + times(i, STEP), STEP)
            tables = dot(hot[rows, :], table[...], ((1,), (0,)))
            rstd_out[rows, :] = jnp.broadcast_to(rstd, (STEP, 128))
            for j in range(4):
                c = slice(128 * j, 128 * (j + 1))
                n = center[j] * rstd
                normed[rows, c] = n
                adapted[rows, c] = (n * tables[:, c] + tables[:, D + 128 * j : D + 128 * (j + 1)]).astype(BF)


def up_gelu(adapted, w_up, small, g, slope):
    for i in range(M // TILE):
        rows = at(i * TILE, TILE)
        for c in range(FF // TILE):
            cols = at(c * TILE, TILE)
            bias = small[UBIAS + c // 2 : UBIAS + c // 2 + 1, at((c % 2) * TILE, TILE)]
            u = dot(adapted[rows, :], w_up[:, cols], ((1,), (0,))) + bias
            pdf = jnp.exp2((u * EXP_SCALE) * u) * PDF_SCALE
            cdf = 0.5 + 0.5 * lax.erf(u * ERF_SCALE)
            g[rows, cols] = (u * cdf).astype(BF)
            slope[rows, cols] = (cdf + u * pdf).astype(BF)


def down(x, g, w_down, small, out, upstream, v_out, g_gamma):
    for i in range(M // TILE):
        rows = at(i * TILE, TILE)
        for c in range(2):
            cols = at(c * TILE, TILE)
            v = dot(g[rows, :], w_down[:, cols], ((1,), (0,))) + small[DBIAS : DBIAS + 1, cols]
            out[rows, cols] = (x[rows, cols].astype(F32) + small[GAMMA : GAMMA + 1, cols] * v).astype(BF)
            if v_out is not None:
                v_out[rows, cols] = v.astype(BF)
            if upstream is not None:
                g_gamma[:, cols] += over_rows(upstream[rows, cols].astype(F32) * v)


def down_back(upstream, w_down, small, slope, dv_out, g_dbias, g_ubias, v, g_gamma):
    for i in range(M // TILE):
        rows = at(i * TILE, TILE)
        dy = upstream[rows, :].astype(F32)
        dv = small[GAMMA : GAMMA + 1, :] * dy
        g_dbias[...] += over_rows(dv)
        if v is not None:
            g_gamma[...] += over_rows(dy * v[rows, :].astype(F32))
        dv = dv.astype(BF)
        dv_out[rows, :] = dv
        for c in range(FF // TILE):
            cols = at(c * TILE, TILE)
            du = dot(dv, w_down[cols, :], ((1,), (1,))) * slope[rows, cols].astype(F32)
            slope[rows, cols] = du.astype(BF)
            g_ubias[:, cols] += over_rows(du)


def down_grad(g, dv, out):
    for c in range(FF // TILE):
        cols = at(c * TILE, TILE)
        out[cols, :] = dot(g[:, cols], dv[...], ((0,), (0,))).astype(BF)


def up_grad(adapted, du, out):
    for c in range(FF // TILE):
        place = (at(FF + (c // 2) * D, D), at((c % 2) * TILE, TILE))
        out[place] = dot(adapted[...], du[:, at(c * TILE, TILE)], ((0,), (0,))).astype(BF)


def norm_back(du, w_up, hot, table, normed, rstd, d_hidden, g_table):
    half = TILE
    for i in range(M // half):
        rows = at(i * half, half)
        da = dot(du[rows, :], w_up[...], ((1,), (1,)))
        n = normed[rows, :]
        dan = da * n
        ones = hot[rows, 0:16]
        g_table[:, 0:D] += dot(ones, dan.astype(BF), ((0,), (0,)))[0:8]
        g_table[:, D:] += dot(ones, da.astype(BF), ((0,), (0,)))[0:8]
        scale = dot(hot[rows, :], table[:, 0:D], ((1,), (0,)))
        dn = da * scale
        mean = jnp.sum(dn, axis=1, keepdims=True) * (1.0 / D)
        along = jnp.sum(dan * scale, axis=1, keepdims=True) * (1.0 / D)
        dh = (dn - mean - n * along) * rstd[rows, 0:1]
        r, first = i * half // SPAN, i * half % SPAN
        for j in range(4):
            d_hidden[r, j, at(HALO + first, half), :] = dh[:, 128 * j : 128 * (j + 1)]


def conv_back(x, upstream, d_hidden, masks, small, g_taps, g_cbias, out):
    for r in range(ROWS):
        for j in range(4):
            d_hidden[r, j, 0:HALO] = jnp.zeros((HALO, 128), F32)
            d_hidden[r, j, HALO + SPAN :] = jnp.zeros((HALO, 128), F32)

        @pl.loop(0, SPAN // STEP, unroll=2)
        def _(i):
            rows = at(r * SPAN + times(i, STEP), STEP)
            here = at(times(i, STEP), STEP)
            for j in range(4):
                c = slice(128 * j, 128 * (j + 1))
                value = x[rows, c].astype(F32)
                dh = d_hidden[r, j, at(times(i, STEP) + HALO, STEP), :]
                total = upstream[rows, c].astype(F32) + dh * small[3:4, c]
                g_cbias[:, c] += over_rows(dh)
                g_taps[3, :, c] += over_rows(value * dh)
                for q, k in enumerate(OFFSETS):
                    part = d_hidden[r, j, pl.ds(i * STEP + (HALO + k - 3), STEP), :] * masks[r, q, here, :]
                    total = total + part * small[6 - k : 7 - k, c]
                    g_taps[6 - k, :, c] += over_rows(value * part)
                out[rows, c] = total.astype(out.dtype)


def small_grads(out, g_taps, g_cbias, g_table, g_dbias, g_gamma, g_ubias):
    def whole(value):
        return jnp.sum(value, axis=0, keepdims=True)

    rows = [whole(g_taps[k]) for k in range(7)] + [whole(g_cbias[...])]
    rows += [g_table[0:4, 0:D], g_table[0:4, D:], whole(g_dbias[...]), whole(g_gamma[...])]
    rows += [whole(g_ubias[:, k * D : (k + 1) * D]) for k in range(3)]
    rows.append(jnp.zeros((SMALL - SMALL_ROWS, D), F32))
    out[...] = jnp.concatenate(rows, axis=0)


PARTS = 3
PART_ROWS = GRADS // PARTS
STRIDES = (16, 4, 1)


def train_kernel(
    lengths, ids, conv_weight, conv_bias, scale_table, shift_table, b_down, layer_scale, b_up,
    frames, cotangent, own_up, own_down,
    acts_all, grads_all, weight_all, small_all,
    x0, cot, small, w_up, w_down, acts, grads, weight_grads, small_sums,
    padded, masks, hot, table, normed, rstd, adapted, g, slope, v0, dv,
    g_table, g_taps, g_cbias, g_dbias, g_ubias, g_gamma,
    pair, got1, got2, got3, sum1, sum2, small_pair, small_got, small_sum,
    load_sems, store_sems, swap_send, swap_recv, pair_send, pair_recv, row_send, row_recv,
    send, recv, back_send, back_recv, small_send, small_recv,
):
    section = lax.axis_index("section")
    dp = lax.axis_index("dp")
    coords = (dp // 16, (dp // 4) % 4, dp % 4)
    other = {"dp": dp, "section": 1 - section}
    mine = pl.ds(pl.multiple_of(section * M, M), M)

    def along(axis, distance):
        return lax.rem(coords[axis] + distance, 4)

    def peer(axis, distance):
        return {"dp": dp + (along(axis, distance) - coords[axis]) * STRIDES[axis], "section": section}

    def remote(src, dst, send_sem, recv_sem, device):
        return pltpu.make_async_remote_copy(
            src_ref=src, dst_ref=dst, send_sem=send_sem, recv_sem=recv_sem, device_id=device, device_id_type=MESH
        )

    barrier = pltpu.get_barrier_semaphore()
    pl.semaphore_signal(barrier, inc=1, device_id=other, device_id_type=MESH)
    for axis in range(3):
        for distance in (1, 2, 3):
            pl.semaphore_signal(barrier, inc=1, device_id=peer(axis, distance), device_id_type=MESH)
    loads = [
        pltpu.make_async_copy(frames.at[mine], x0, load_sems.at[0]),
        pltpu.make_async_copy(own_up, w_up.at[section], load_sems.at[1]),
        pltpu.make_async_copy(own_down, w_down.at[section], load_sems.at[2]),
        pltpu.make_async_copy(cotangent.at[mine], cot, load_sems.at[3]),
    ]
    for load in loads:
        load.start()
    rows = [conv_weight[0], conv_bias[...], scale_table[0], shift_table[0], b_down[...], layer_scale[...]]
    rows += [b_up[:, k * D : (k + 1) * D] for k in range(3)] + [jnp.zeros((24 - SMALL_ROWS, D), F32)]
    small[section] = jnp.concatenate(rows, axis=0)
    pl.semaphore_wait(barrier, 10)
    swaps = [
        remote(small.at[section], small.at[section], swap_send.at[0], swap_recv.at[0], other),
        remote(own_up, w_up.at[section], swap_send.at[1], swap_recv.at[1], other),
        remote(own_down, w_down.at[section], swap_send.at[2], swap_recv.at[2], other),
    ]
    for swap in swaps:
        swap.start()

    def to_owner(b, i, rows):
        return remote(weight_grads.at[b, rows], pair.at[rows], pair_send.at[i], pair_recv.at[i], other)

    def kept_rows(b, kind, source, target):
        return pltpu.make_async_copy(source, target.at[mine], store_sems.at[2 * kind + b])

    def sent_rows(b, kind, source, target):
        i = 2 * kind + b
        return remote(source, target.at[mine], row_send.at[i], row_recv.at[i], other)

    def start_rows(b, *what):
        @pl.when(section == b)
        def _():
            kept_rows(b, *what).start()

        @pl.when(section != b)
        def _():
            sent_rows(b, *what).start()

    def finish_rows(b, *what):
        @pl.when(section == b)
        def _():
            kept_rows(b, *what).wait()
            sent_rows(b, *what).wait_recv()

        @pl.when(section != b)
        def _():
            sent_rows(b, *what).wait_send()

    def block(p, stage):
        first, size = p * PART_ROWS, PART_ROWS
        for s in range(stage):
            size //= 4
            first = first + coords[(p + s) % 3] * size
        return pl.ds(pl.multiple_of(first, size), size)

    def scatter(b, p, stage):
        axis = (p + stage) % 3
        size = PART_ROWS // 4 ** (stage + 1)
        source = (weight_grads.at[b, at(p * PART_ROWS, PART_ROWS)], sum1.at[p], sum2.at[p])[stage]
        got = (got1, got2, got3)[stage]
        made = []
        for distance in (1, 2, 3):
            i = (p * 3 + stage) * 3 + distance - 1
            part = pl.ds(pl.multiple_of(along(axis, distance) * size, size), size)
            made.append(remote(source.at[part], got.at[p, distance - 1], send.at[i], recv.at[i], peer(axis, distance)))
        return made

    def gather(p, stage):
        axis = (p + stage) % 3
        rows = block(p, stage + 1)
        made = []
        for distance in (1, 2, 3):
            i = (p * 3 + stage) * 3 + distance - 1
            made.append(remote(pair.at[rows], pair.at[rows], back_send.at[i], back_recv.at[i], peer(axis, distance)))
        return made

    def start(copies):
        for copy in copies:
            copy.start()

    def arrived(copies):
        for copy in copies:
            copy.wait_recv()

    def total(b, p, stage):
        axis = (p + stage) % 3
        size = PART_ROWS // 4 ** (stage + 1)
        part = pl.ds(pl.multiple_of(coords[axis] * size, size), size)
        got = (got1, got2, got3)[stage]
        if stage == 0:
            kept = weight_grads[b, pl.ds(pl.multiple_of(p * PART_ROWS + coords[axis] * size, size), size), :]
        else:
            kept = (sum1, sum2)[stage - 1][p, part, :]
        kept = kept.astype(F32)
        for d in range(3):
            kept = kept + got[p, d].astype(F32)
        return kept.astype(BF)

    def step(b, p, k):
        if k == 0:
            for i in range(4):
                rows = at(p * PART_ROWS + i * TILE, TILE)
                weight_grads[b, rows, :] = (weight_grads[b, rows, :].astype(F32) + pair[rows, :].astype(F32)).astype(BF)
            start(scatter(b, p, 0))
        elif k in (1, 2):
            arrived(scatter(b, p, k - 1))
            (sum1, sum2)[k - 1][p] = total(b, p, k - 1)
            start(scatter(b, p, k))
        elif k == 3:
            arrived(scatter(b, p, 2))
            pair[block(p, 3), :] = total(b, p, 2)
            start(gather(p, 2))
        elif k in (4, 5):
            arrived(gather(p, 6 - k))
            start(gather(p, 5 - k))
        else:
            arrived(gather(p, 0))
            keep(p).start()

    def keep(p):
        rows = at(p * PART_ROWS, PART_ROWS)
        return pltpu.make_async_copy(pair.at[rows], weight_all.at[rows], store_sems.at[4 + p])

    def steps(b, *todo):
        @pl.when(section == b)
        def _():
            for p, k in todo:
                step(b, p, k)

    PIECES = (at(0, 1024), at(1024, 512), at(1536, 512), at(2048, 1024))

    def pieces(b, *todo):
        @pl.when(section != b)
        def _():
            for i in todo:
                to_owner(b, i, PIECES[i]).start()

    def pieces_in(b, *todo):
        @pl.when(section == b)
        def _():
            for i in todo:
                to_owner(b, i, PIECES[i]).wait_recv()

    clip_tables(section * ROWS, lengths, ids, masks, hot)
    for ref in (g_table, g_taps, g_cbias, g_dbias, g_ubias, g_gamma):
        ref[...] = jnp.zeros_like(ref)
    swaps[0].wait_recv()
    for b in range(2):
        band_table(small.at[b], table.at[b])
    loads[0].wait()
    conv_norm(x0, padded, masks, hot, table.at[0], small.at[0], normed.at[0], rstd.at[0], adapted.at[0])
    loads[1].wait()
    swaps[1].wait_recv()
    up_gelu(adapted.at[0], w_up.at[0], small.at[0], g.at[0], slope.at[0])
    loads[2].wait()
    swaps[2].wait_recv()
    down(x0, g.at[0], w_down.at[0], small.at[0], acts.at[0], None, v0, None)
    start_rows(0, 0, acts.at[0], acts_all)
    conv_norm(acts.at[0], padded, masks, hot, table.at[1], small.at[1], normed.at[1], rstd.at[1], adapted.at[1])
    up_gelu(adapted.at[1], w_up.at[1], small.at[1], g.at[1], slope.at[1])
    loads[3].wait()

    down_back(cot, w_down.at[1], small.at[1], slope.at[1], dv, g_dbias.at[1], g_ubias.at[1], None, None)
    down_grad(g.at[1], dv, weight_grads.at[1])
    pieces(1, 0, 1)
    up_grad(adapted.at[1], slope.at[1], weight_grads.at[1])
    pieces(1, 2, 3)
    pieces_in(1, 0)
    steps(1, (0, 0))
    norm_back(slope.at[1], w_up.at[1], hot, table.at[1], normed.at[1], rstd.at[1], padded, g_table.at[1])
    pieces_in(1, 1, 2, 3)
    steps(1, (1, 0), (2, 0))
    conv_back(acts.at[0], cot, padded, masks, small.at[1], g_taps.at[1], g_cbias.at[1], grads.at[1])
    start_rows(1, 1, grads.at[1], grads_all)
    down_back(grads.at[1], w_down.at[0], small.at[0], slope.at[0], dv, g_dbias.at[0], g_ubias.at[0], v0, g_gamma.at[0])
    steps(1, (0, 1))
    down_grad(g.at[0], dv, weight_grads.at[0])
    pieces(0, 0, 1)
    steps(1, (1, 1), (2, 1), (0, 2))
    up_grad(adapted.at[0], slope.at[0], weight_grads.at[0])
    pieces(0, 2, 3)
    pieces_in(0, 0)
    steps(0, (0, 0))
    pieces_in(0, 1, 2)
    steps(0, (1, 0))
    pieces_in(0, 3)
    steps(0, (2, 0))
    steps(1, (1, 2), (2, 2), (0, 3))
    norm_back(slope.at[0], w_up.at[0], hot, table.at[0], normed.at[0], rstd.at[0], padded, g_table.at[0])
    steps(1, (1, 3), (2, 3), (0, 4))
    conv_back(x0, grads.at[1], padded, masks, small.at[0], g_taps.at[0], g_cbias.at[0], grads.at[0])
    start_rows(0, 1, grads.at[0], grads_all)
    steps(1, (1, 4), (2, 4), (0, 5))
    steps(0, (0, 1))
    down(acts.at[0], g.at[1], w_down.at[1], small.at[1], acts.at[1], cot, None, g_gamma.at[1])
    start_rows(1, 0, acts.at[1], acts_all)
    for b in range(2):
        small_grads(
            small_sums.at[b], g_taps.at[b], g_cbias.at[b], g_table.at[b], g_dbias.at[b], g_gamma.at[b], g_ubias.at[b]
        )

    small_far = remote(small_sums.at[1 - section], small_pair, pair_send.at[4], pair_recv.at[4], other)
    small_far.start()
    steps(1, (1, 5), (2, 5))
    steps(0, (1, 1), (2, 1), (0, 2))

    def quarter(index):
        return pl.ds(pl.multiple_of(index * 8, 8), 8)

    def small_copies(stage):
        made = []
        axis = (0, 1, 2, 0)[stage]
        for distance in (1, 2, 3):
            i = stage * 3 + distance - 1
            if stage == 0:
                src, dst = small_pair.at[quarter(along(axis, distance))], small_got.at[0, distance - 1]
            elif stage == 3:
                src = dst = small_all.at[quarter(coords[0])]
            else:
                src, dst = small_sum.at[stage - 1], small_got.at[stage, distance - 1]
            made.append(remote(src, dst, small_send.at[i], small_recv.at[i], peer(axis, distance)))
        return made

    def small_total(stage, kept):
        return kept + small_got[stage, 0] + small_got[stage, 1] + small_got[stage, 2]

    small_far.wait_recv()
    small_pair[...] += small_sums[section]
    start(small_copies(0))
    steps(0, (1, 2), (2, 2), (0, 3))
    arrived(small_copies(0))
    small_sum[0] = small_total(0, small_pair[quarter(coords[0]), :])
    start(small_copies(1))
    steps(0, (1, 3), (2, 3), (0, 4))
    arrived(small_copies(1))
    small_sum[1] = small_total(1, small_sum[0])
    start(small_copies(2))
    steps(0, (1, 4), (2, 4), (0, 5))
    arrived(small_copies(2))
    small_all[quarter(coords[0]), :] = small_total(2, small_sum[1])
    start(small_copies(3))
    steps(0, (1, 5), (2, 5))
    steps(1, (0, 6), (1, 6), (2, 6))
    arrived(small_copies(3))
    steps(0, (0, 6), (1, 6), (2, 6))

    for swap in swaps:
        swap.wait_send()
    for b in range(2):
        finish_rows(b, 0, acts.at[b], acts_all)
        finish_rows(b, 1, grads.at[b], grads_all)

        @pl.when(section != b)
        def _():
            for i in range(4):
                to_owner(b, i, PIECES[i]).wait_send()

        @pl.when(section == b)
        def _():
            for p in range(PARTS):
                for stage in range(3):
                    for copy in scatter(b, p, stage) + gather(p, stage):
                        copy.wait_send()
                keep(p).wait()

    small_far.wait_send()
    for stage in range(4):
        for copy in small_copies(stage):
            copy.wait_send()


def train(*arrays):
    smem = pl.BlockSpec(memory_space=pltpu.SMEM)
    vmem = pl.BlockSpec(memory_space=pltpu.VMEM)
    hbm = pl.BlockSpec(memory_space=pl.ANY)
    quarter = PART_ROWS // 4
    return pl.pallas_call(
        train_kernel,
        out_shape=[
            jax.ShapeDtypeStruct((2 * M, D), BF),
            jax.ShapeDtypeStruct((2 * M, D), BF),
            jax.ShapeDtypeStruct((GRADS, D), BF),
            jax.ShapeDtypeStruct((SMALL, D), F32),
        ],
        in_specs=[smem, smem] + [vmem] * 7 + [hbm] * 4,
        out_specs=[hbm, hbm, hbm, vmem],
        scratch_shapes=[
            pltpu.VMEM((M, D), BF),
            pltpu.VMEM((M, D), BF),
            pltpu.VMEM((2, 24, D), F32),
            pltpu.VMEM((2, D, FF), BF),
            pltpu.VMEM((2, FF, D), BF),
            pltpu.VMEM((2, M, D), BF),
            pltpu.VMEM((2, M, D), BF),
            pltpu.VMEM((2, GRADS, D), BF),
            pltpu.VMEM((2, SMALL, D), F32),
            pltpu.VMEM((ROWS, 4, PADDED, 128), F32),
            pltpu.VMEM((ROWS, 6, SPAN, 128), F32),
            pltpu.VMEM((M, 128), BF),
            pltpu.VMEM((2, 128, 2 * D), BF),
            pltpu.VMEM((2, M, D), F32),
            pltpu.VMEM((2, M, 128), F32),
            pltpu.VMEM((2, M, D), BF),
            pltpu.VMEM((2, M, FF), BF),
            pltpu.VMEM((2, M, FF), BF),
            pltpu.VMEM((M, D), BF),
            pltpu.VMEM((M, D), BF),
            pltpu.VMEM((2, 8, 2 * D), F32),
            pltpu.VMEM((2, 7, 8, D), F32),
            pltpu.VMEM((2, 8, D), F32),
            pltpu.VMEM((2, 8, D), F32),
            pltpu.VMEM((2, 8, FF), F32),
            pltpu.VMEM((2, 8, D), F32),
            pltpu.VMEM((GRADS, D), BF),
            pltpu.VMEM((PARTS, 3, quarter, D), BF),
            pltpu.VMEM((PARTS, 3, quarter // 4, D), BF),
            pltpu.VMEM((PARTS, 3, quarter // 16, D), BF),
            pltpu.VMEM((PARTS, quarter, D), BF),
            pltpu.VMEM((PARTS, quarter // 4, D), BF),
            pltpu.VMEM((SMALL, D), F32),
            pltpu.VMEM((3, 3, 8, D), F32),
            pltpu.VMEM((2, 8, D), F32),
        ]
        + [pltpu.SemaphoreType.DMA((n,)) for n in (4, 7, 3, 3, 5, 5, 4, 4, 27, 27, 27, 27, 12, 12)],
        compiler_params=pltpu.CompilerParams(collective_id=0, has_side_effects=True, vmem_limit_bytes=63 * MIB),
        cost_estimate=pl.CostEstimate(flops=24 * M * D * FF, bytes_accessed=24 * MIB, transcendentals=4 * M * FF),
    )(*arrays)


def shards(
    frames, cotangent, lengths, bw_ids, conv_weight, conv_bias, scale_table, shift_table,
    w_up, b_up, w_down, b_down, layer_scale,
):
    acts, grads, weights, small = train(
        lengths, bw_ids, conv_weight, conv_bias, scale_table, shift_table, b_down, layer_scale, b_up,
        frames, cotangent, w_up[0], w_down[0],
    )
    g_down = weights[:FF].astype(F32)
    g_up = jnp.concatenate([weights[FF + k * D : FF + (k + 1) * D] for k in range(3)], axis=1).astype(F32)
    return (
        acts[None],
        grads.astype(F32)[None],
        small[None, TAPS : TAPS + 7],
        small[CBIAS : CBIAS + 1],
        small[None, SCALE : SCALE + 4],
        small[None, SHIFT : SHIFT + 4],
        g_up[None],
        small[UBIAS : UBIAS + 3].reshape(1, FF),
        g_down[None],
        small[DBIAS : DBIAS + 1],
        small[GAMMA : GAMMA + 1],
    )


def solution(mesh):
    rows = P("dp", None)
    matrix, vector = P("section", None, None), P("section", None)
    in_specs = (rows,) * 4 + (matrix, vector, matrix, matrix, matrix, vector, matrix, vector, vector)
    stacked = P("section", "dp", None)
    out_specs = (stacked, stacked, matrix, vector, matrix, matrix, matrix, vector, matrix, vector, vector)
    return jax.shard_map(shards, mesh=mesh, in_specs=in_specs, out_specs=out_specs, check_vma=False)
```

```python
import functools
import math

import jax
import jax.numpy as jnp
import numpy as np
from jax import lax
from jax.experimental import pallas as pl
from jax.experimental.pallas import tpu as pltpu
from jax.sharding import PartitionSpec as P

BF = jnp.bfloat16
F32 = jnp.float32
MESH = pl.DeviceIdType.MESH
MIB = 2**20

SPAN = 512
D = 512
FF = 1536
ROWS = 2
M = ROWS * SPAN
HALO = 8
PADDED = SPAN + 2 * HALO
STEP = 64
TILE = 256
GRADS = 2 * FF
SMALL = 32
EXP_SCALE = -0.5 * math.log2(math.e)
PDF_SCALE = 1.0 / math.sqrt(2.0 * math.pi)
ERF_SCALE = 1.0 / math.sqrt(2.0)
TAPS, CBIAS, SCALE, SHIFT, DBIAS, GAMMA, UBIAS = 0, 7, 8, 12, 16, 17, 18
SMALL_ROWS = 21
OFFSETS = (0, 1, 2, 4, 5, 6)


def at(start, size):
    return slice(start, start + size) if isinstance(start, int) else pl.ds(start, size)


def times(index, size):
    return index * size if isinstance(index, int) else pl.multiple_of(index * size, size)


def over_rows(value):
    return jnp.sum(value.reshape(value.shape[0] // 8, 8, value.shape[1]), axis=0)


def dot(a, b, dims):
    return lax.dot_general(a, b, (dims, ((), ())), preferred_element_type=F32)


def clip_tables(first, lengths, ids, masks, hot):
    for r in range(ROWS):
        row = first + r
        ends = [lengths[row, 0]]
        for c in (1, 2):
            ends.append(ends[-1] + lengths[row, c])
        band_of = [ids[row, c] for c in range(4)]

        def segment(frame):
            return sum((frame >= end).astype(jnp.int32) for end in ends)

        @pl.loop(0, SPAN // STEP, unroll=2)
        def _(i):
            frame = lax.broadcasted_iota(jnp.int32, (STEP, 128), 0) + i * STEP
            lane = lax.broadcasted_iota(jnp.int32, (STEP, 128), 1)
            here = segment(frame)
            for q, k in enumerate(OFFSETS):
                there = frame + (k - 3)
                same = (segment(there) == here) & (there >= 0) & (there < SPAN)
                masks[r, q, at(times(i, STEP), STEP), :] = jnp.where(same, 1.0, 0.0)
            band = jnp.where(here == 2, band_of[2], band_of[3])
            band = jnp.where(here == 1, band_of[1], band)
            band = jnp.where(here == 0, band_of[0], band)
            one = (lane == band) | (lane == band + 4)
            hot[at(r * SPAN + times(i, STEP), STEP), :] = jnp.where(one, 1.0, 0.0).astype(BF)


def band_table(small, table):
    table[...] = jnp.zeros_like(table)
    for half, first in enumerate((SCALE, SHIFT)):
        whole = small[first : first + 4, :]
        upper = whole.astype(BF).astype(F32)
        both = jnp.concatenate([upper, whole - upper], axis=0)
        table[0:8, half * D : (half + 1) * D] = both.astype(BF)


def conv_norm(x, padded, masks, hot, table, small, normed, rstd_out, adapted):
    for r in range(ROWS):
        for j in range(4):
            padded[r, j, 0:HALO] = jnp.zeros((HALO, 128), F32)
            padded[r, j, HALO + SPAN :] = jnp.zeros((HALO, 128), F32)
            padded[r, j, HALO : HALO + SPAN] = x[r * SPAN : (r + 1) * SPAN, 128 * j : 128 * (j + 1)].astype(F32)

        @pl.loop(0, SPAN // STEP, unroll=8)
        def _(i):
            here = at(times(i, STEP), STEP)
            hidden = []
            for j in range(4):
                c = slice(128 * j, 128 * (j + 1))
                total = small[CBIAS : CBIAS + 1, c] + padded[r, j, at(times(i, STEP) + HALO, STEP), :] * small[3:4, c]
                for q, k in enumerate(OFFSETS):
                    moved = padded[r, j, pl.ds(i * STEP + (HALO + k - 3), STEP), :]
                    total = total + moved * masks[r, q, here, :] * small[k : k + 1, c]
                hidden.append(total)
            mean = jnp.sum(hidden[0] + hidden[1] + hidden[2] + hidden[3], axis=1, keepdims=True) * (1.0 / D)
            center = [h - mean for h in hidden]
            square = [c * c for c in center]
            spread = jnp.sum(square[0] + square[1] + square[2] + square[3], axis=1, keepdims=True) * (1.0 / D)
            rstd = lax.rsqrt(spread + 1e-6)
            rows = at(r * SPAN + times(i, STEP), STEP)
            tables = dot(hot[rows, :], table[...], ((1,), (0,)))
            rstd_out[rows, :] = jnp.broadcast_to(rstd, (STEP, 128))
            for j in range(4):
                c = slice(128 * j, 128 * (j + 1))
                n = center[j] * rstd
                normed[rows, c] = n
                adapted[rows, c] = (n * tables[:, c] + tables[:, D + 128 * j : D + 128 * (j + 1)]).astype(BF)


def up_gelu(adapted, w_up, small, g, slope):
    for i in range(M // TILE):
        rows = at(i * TILE, TILE)
        for c in range(FF // TILE):
            cols = at(c * TILE, TILE)
            bias = small[UBIAS + c // 2 : UBIAS + c // 2 + 1, at((c % 2) * TILE, TILE)]
            u = dot(adapted[rows, :], w_up[:, cols], ((1,), (0,))) + bias
            pdf = jnp.exp2((u * EXP_SCALE) * u) * PDF_SCALE
            cdf = 0.5 + 0.5 * lax.erf(u * ERF_SCALE)
            g[rows, cols] = (u * cdf).astype(BF)
            slope[rows, cols] = (cdf + u * pdf).astype(BF)


def down(x, g, w_down, small, out, upstream, v_out, g_gamma, tiles=range(M // TILE)):
    for i in tiles:
        rows = at(i * TILE, TILE)
        for c in range(2):
            cols = at(c * TILE, TILE)
            v = dot(g[rows, :], w_down[:, cols], ((1,), (0,))) + small[DBIAS : DBIAS + 1, cols]
            out[rows, cols] = (x[rows, cols].astype(F32) + small[GAMMA : GAMMA + 1, cols] * v).astype(BF)
            if v_out is not None:
                v_out[rows, cols] = v.astype(BF)
            if upstream is not None:
                g_gamma[:, cols] += over_rows(upstream[rows, cols].astype(F32) * v)


def down_back(upstream, w_down, small, slope, dv_out, g_dbias, g_ubias, v, g_gamma):
    for i in range(M // TILE):
        rows = at(i * TILE, TILE)
        dy = upstream[rows, :].astype(F32)
        dv = small[GAMMA : GAMMA + 1, :] * dy
        g_dbias[...] += over_rows(dv)
        if v is not None:
            g_gamma[...] += over_rows(dy * v[rows, :].astype(F32))
        dv = dv.astype(BF)
        dv_out[rows, :] = dv
        for c in range(FF // TILE):
            cols = at(c * TILE, TILE)
            du = dot(dv, w_down[cols, :], ((1,), (1,))) * slope[rows, cols].astype(F32)
            slope[rows, cols] = du.astype(BF)
            g_ubias[:, cols] += over_rows(du)


def down_grad(g, dv, out):
    for c in range(FF // TILE):
        cols = at(c * TILE, TILE)
        out[cols, :] = dot(g[:, cols], dv[...], ((0,), (0,))).astype(BF)


def up_grad(adapted, du, out):
    for c in range(FF // TILE):
        place = (at(FF + (c // 2) * D, D), at((c % 2) * TILE, TILE))
        out[place] = dot(adapted[...], du[:, at(c * TILE, TILE)], ((0,), (0,))).astype(BF)


def norm_back(du, w_up, hot, table, normed, rstd, d_hidden, g_table, tiles=range(M // TILE)):
    for i in tiles:
        rows = at(i * TILE, TILE)
        da = dot(du[rows, :], w_up[...], ((1,), (1,)))
        n = normed[rows, :]
        dan = da * n
        ones = hot[rows, 0:16]
        g_table[:, 0:D] += dot(ones, dan.astype(BF), ((0,), (0,)))[0:8]
        g_table[:, D:] += dot(ones, da.astype(BF), ((0,), (0,)))[0:8]
        scale = dot(hot[rows, :], table[:, 0:D], ((1,), (0,)))
        dn = da * scale
        mean = jnp.sum(dn, axis=1, keepdims=True) * (1.0 / D)
        along = jnp.sum(dan * scale, axis=1, keepdims=True) * (1.0 / D)
        dh = (dn - mean - n * along) * rstd[rows, 0:1]
        r, first = i * TILE // SPAN, i * TILE % SPAN
        for j in range(4):
            d_hidden[r, j, at(HALO + first, TILE), :] = dh[:, 128 * j : 128 * (j + 1)]


def conv_back(x, upstream, d_hidden, masks, small, g_taps, g_cbias, out, which=range(ROWS)):
    for r in which:
        for j in range(4):
            d_hidden[r, j, 0:HALO] = jnp.zeros((HALO, 128), F32)
            d_hidden[r, j, HALO + SPAN :] = jnp.zeros((HALO, 128), F32)

        @pl.loop(0, SPAN // STEP, unroll=2)
        def _(i):
            rows = at(r * SPAN + times(i, STEP), STEP)
            here = at(times(i, STEP), STEP)
            for j in range(4):
                c = slice(128 * j, 128 * (j + 1))
                value = x[rows, c].astype(F32)
                dh = d_hidden[r, j, at(times(i, STEP) + HALO, STEP), :]
                total = upstream[rows, c].astype(F32) + dh * small[3:4, c]
                g_cbias[:, c] += over_rows(dh)
                g_taps[3, :, c] += over_rows(value * dh)
                for q, k in enumerate(OFFSETS):
                    part = d_hidden[r, j, pl.ds(i * STEP + (HALO + k - 3), STEP), :] * masks[r, q, here, :]
                    total = total + part * small[6 - k : 7 - k, c]
                    g_taps[6 - k, :, c] += over_rows(value * part)
                out[rows, c] = total.astype(out.dtype)


def small_grads(out, g_taps, g_cbias, g_table, g_dbias, g_gamma, g_ubias):
    def whole(value):
        return jnp.sum(value, axis=0, keepdims=True)

    rows = [whole(g_taps[k]) for k in range(7)] + [whole(g_cbias[...])]
    rows += [g_table[0:4, 0:D], g_table[0:4, D:], whole(g_dbias[...]), whole(g_gamma[...])]
    rows += [whole(g_ubias[:, k * D : (k + 1) * D]) for k in range(3)]
    rows.append(jnp.zeros((SMALL - SMALL_ROWS, D), F32))
    out[...] = jnp.concatenate(rows, axis=0)


PARTS = 3
PART_ROWS = FF // PARTS
QUARTER = PART_ROWS // 4
PIECE = (16, 256)
STRIDES = (16, 4, 1)


def train_kernel(
    lengths, ids, conv_weight, conv_bias, scale_table, shift_table, b_down, layer_scale, b_up,
    frames, cotangent, own_up, own_down,
    acts_all, grads_all, weight_all, small_all,
    x0, cot, small, w_up, w_down, acts, grads, weight_grads, small_sums,
    padded, masks, hot, table, normed, rstd, adapted, g, slope, v0, dv,
    g_table, g_taps, g_cbias, g_dbias, g_ubias, g_gamma,
    pair, line_got, plane_got, line_sum, small_got, small_sum, plane_small,
    load_sems, store_sems, swap_send, swap_recv, pair_send, pair_recv, row_send, row_recv,
    line_send, line_recv, plane_send, plane_recv, plane_back_send, plane_back_recv, line_back_send, line_back_recv,
    small_send, small_recv,
):
    section = lax.axis_index("section")
    dp = lax.axis_index("dp")
    coords = (dp // 16, (dp // 4) % 4, dp % 4)
    other = {"dp": dp, "section": 1 - section}
    mine = pl.ds(pl.multiple_of(section * M, M), M)

    def along(axis, distance):
        return lax.rem(coords[axis] + distance, 4)

    def peer(axis, distance):
        return {"dp": dp + (along(axis, distance) - coords[axis]) * STRIDES[axis], "section": section}

    def plane_peer(p, u, v):
        first, second = (p + 1) % 3, (p + 2) % 3
        moved = (along(first, u) - coords[first]) * STRIDES[first]
        return {"dp": dp + moved + (along(second, v) - coords[second]) * STRIDES[second], "section": section}

    plane = [(u, v) for u in range(4) for v in range(4) if u or v]

    def remote(src, dst, send_sem, recv_sem, device):
        return pltpu.make_async_remote_copy(
            src_ref=src, dst_ref=dst, send_sem=send_sem, recv_sem=recv_sem, device_id=device, device_id_type=MESH
        )

    barrier = pltpu.get_barrier_semaphore()
    pl.semaphore_signal(barrier, inc=1, device_id=other, device_id_type=MESH)
    for axis in range(3):
        for distance in (1, 2, 3):
            pl.semaphore_signal(barrier, inc=1, device_id=peer(axis, distance), device_id_type=MESH)
            if axis == 0:
                crossed = dict(peer(axis, distance), section=1 - section)
                pl.semaphore_signal(barrier, inc=1, device_id=crossed, device_id_type=MESH)
        for u, v in plane:
            if u and v:
                pl.semaphore_signal(barrier, inc=1, device_id=plane_peer(axis, u, v), device_id_type=MESH)
    loads = [
        pltpu.make_async_copy(frames.at[mine], x0, load_sems.at[0]),
        pltpu.make_async_copy(own_up, w_up.at[section], load_sems.at[1]),
        pltpu.make_async_copy(own_down, w_down.at[section], load_sems.at[2]),
        pltpu.make_async_copy(cotangent.at[mine], cot, load_sems.at[3]),
    ]
    for load in loads:
        load.start()
    rows = [conv_weight[k] for k in range(7)] + [conv_bias[...], scale_table[0], shift_table[0], b_down[...], layer_scale[...]]
    rows += [b_up[:, k * D : (k + 1) * D] for k in range(3)] + [jnp.zeros((24 - SMALL_ROWS, D), F32)]
    small[section] = jnp.concatenate(rows, axis=0)
    pl.semaphore_wait(barrier, 40)
    swaps = [
        remote(small.at[section], small.at[section], swap_send.at[0], swap_recv.at[0], other),
        remote(own_up, w_up.at[section], swap_send.at[1], swap_recv.at[1], other),
        remote(own_down, w_down.at[section], swap_send.at[2], swap_recv.at[2], other),
    ]
    for swap in swaps:
        swap.start()

    def part_rows(h, p):
        return at(h * FF + p * PART_ROWS, PART_ROWS)

    def to_owner(b, h, p):
        rows, i = part_rows(h, p), h * PARTS + p
        return remote(weight_grads.at[b, rows], pair.at[rows], pair_send.at[i], pair_recv.at[i], other)

    def kept_rows(b, kind, source, target):
        return pltpu.make_async_copy(source, target.at[mine], store_sems.at[2 * kind + b])

    def sent_rows(b, kind, source, target):
        i = 2 * kind + b
        return remote(source, target.at[mine], row_send.at[i], row_recv.at[i], other)

    def start_rows(b, *what):
        @pl.when(section == b)
        def _():
            kept_rows(b, *what).start()

        @pl.when(section != b)
        def _():
            sent_rows(b, *what).start()

    def finish_rows(b, *what):
        @pl.when(section == b)
        def _():
            kept_rows(b, *what).wait()
            sent_rows(b, *what).wait_recv()

        @pl.when(section != b)
        def _():
            sent_rows(b, *what).wait_send()

    def quarter(h, p, distance):
        first = h * FF + p * PART_ROWS + along(p, distance) * QUARTER
        return pl.ds(pl.multiple_of(first, QUARTER), QUARTER)

    def piece(ref, first, p, u, v):
        i, j = along((p + 1) % 3, u), along((p + 2) % 3, v)
        rows = pl.ds(pl.multiple_of(first + i * 32 + (j // 2) * 16, 16), 16)
        return ref.at[rows, pl.ds(pl.multiple_of(lax.rem(j, 2) * 256, 256), 256)]

    def line(b, h, p):
        made = []
        for distance in (1, 2, 3):
            i = (h * PARTS + p) * 3 + distance - 1
            src, dst = weight_grads.at[b, quarter(h, p, distance)], line_got.at[h, p, distance - 1]
            made.append(remote(src, dst, line_send.at[i], line_recv.at[i], peer(p, distance)))
        return made

    def line_back(h, p):
        made = []
        for distance in (1, 2, 3):
            i = (h * PARTS + p) * 3 + distance - 1
            kept = pair.at[quarter(h, p, 0)]
            made.append(remote(kept, kept, line_back_send.at[i], line_back_recv.at[i], peer(p, distance)))
        return made

    def spread(h, p):
        i = h * PARTS + p
        made = []
        for j, (u, v) in enumerate(plane):
            src = piece(line_sum.at[h, p], 0, p, u, v)
            made.append(remote(src, plane_got.at[h, p, j], plane_send.at[i], plane_recv.at[i], plane_peer(p, u, v)))
        return made

    def own_piece(h, p):
        return piece(pair, h * FF + p * PART_ROWS + coords[p] * QUARTER, p, 0, 0)

    def spread_back(h, p):
        i = h * PARTS + p
        kept = own_piece(h, p)
        return [remote(kept, kept, plane_back_send.at[i], plane_back_recv.at[i], plane_peer(p, u, v)) for u, v in plane]

    def fifteen(h, p, sems):
        return pltpu.make_async_copy(plane_got.at[h, p], plane_got.at[h, p], sems.at[h * PARTS + p])

    def start(copies):
        for copy in copies:
            copy.start()

    def arrived(copies):
        for copy in copies:
            copy.wait_recv()

    def keep(h, p):
        rows = part_rows(h, p)
        return pltpu.make_async_copy(pair.at[rows], weight_all.at[rows], store_sems.at[4 + h * PARTS + p])

    def step(b, h, p, k):
        if k == 0:
            to_owner(b, h, p).wait_recv()
            for i in range(2):
                rows = at(h * FF + p * PART_ROWS + i * TILE, TILE)
                weight_grads[b, rows, :] = (weight_grads[b, rows, :].astype(F32) + pair[rows, :].astype(F32)).astype(BF)
            start(line(b, h, p))
        elif k == 1:
            arrived(line(b, h, p))
            total = weight_grads[b, quarter(h, p, 0), :].astype(F32)
            for d in range(3):
                total = total + line_got[h, p, d].astype(F32)
            line_sum[h, p] = total.astype(BF)
            start(spread(h, p))
        elif k == 2:
            fifteen(h, p, plane_recv).wait()
            total = piece(line_sum.at[h, p], 0, p, 0, 0)[...].astype(F32)
            for j in range(15):
                total = total + plane_got[h, p, j].astype(F32)
            own_piece(h, p)[...] = total.astype(BF)
            start(spread_back(h, p))
        elif k == 3:
            fifteen(h, p, plane_back_recv).wait()
            start(line_back(h, p))
        else:
            arrived(line_back(h, p))
            keep(h, p).start()

    def steps(b, *todo):
        @pl.when(section == b)
        def _():
            for h, k in todo:
                for p in range(PARTS):
                    step(b, h, p, k)

    def hand_over(b, h):
        @pl.when(section != b)
        def _():
            for p in range(PARTS):
                to_owner(b, h, p).start()

    clip_tables(section * ROWS, lengths, ids, masks, hot)
    for ref in (g_table, g_taps, g_cbias, g_dbias, g_ubias, g_gamma):
        ref[...] = jnp.zeros_like(ref)
    swaps[0].wait_recv()
    for b in range(2):
        band_table(small.at[b], table.at[b])
    loads[0].wait()
    conv_norm(x0, padded, masks, hot, table.at[0], small.at[0], normed.at[0], rstd.at[0], adapted.at[0])
    loads[1].wait()
    swaps[1].wait_recv()
    up_gelu(adapted.at[0], w_up.at[0], small.at[0], g.at[0], slope.at[0])
    loads[2].wait()
    swaps[2].wait_recv()
    down(x0, g.at[0], w_down.at[0], small.at[0], acts.at[0], None, v0, None)
    start_rows(0, 0, acts.at[0], acts_all)
    conv_norm(acts.at[0], padded, masks, hot, table.at[1], small.at[1], normed.at[1], rstd.at[1], adapted.at[1])
    up_gelu(adapted.at[1], w_up.at[1], small.at[1], g.at[1], slope.at[1])
    loads[3].wait()

    down_back(cot, w_down.at[1], small.at[1], slope.at[1], dv, g_dbias.at[1], g_ubias.at[1], None, None)
    down_grad(g.at[1], dv, weight_grads.at[1])
    hand_over(1, 0)
    up_grad(adapted.at[1], slope.at[1], weight_grads.at[1])
    hand_over(1, 1)
    steps(1, (0, 0))
    norm_back(slope.at[1], w_up.at[1], hot, table.at[1], normed.at[1], rstd.at[1], padded, g_table.at[1])
    steps(1, (1, 0))
    conv_back(acts.at[0], cot, padded, masks, small.at[1], g_taps.at[1], g_cbias.at[1], grads.at[1])
    start_rows(1, 1, grads.at[1], grads_all)
    down_back(grads.at[1], w_down.at[0], small.at[0], slope.at[0], dv, g_dbias.at[0], g_ubias.at[0], v0, g_gamma.at[0])
    down_grad(g.at[0], dv, weight_grads.at[0])
    hand_over(0, 0)
    up_grad(adapted.at[0], slope.at[0], weight_grads.at[0])
    hand_over(0, 1)
    steps(0, (0, 0))
    steps(1, (0, 1), (1, 1))
    for i in range(2):
        norm_back(
            slope.at[0], w_up.at[0], hot, table.at[0], normed.at[0], rstd.at[0], padded, g_table.at[0],
            (2 * i, 2 * i + 1),
        )
        if i == 0:
            steps(0, (1, 0))
    for i in range(2):
        conv_back(
            x0, grads.at[1], padded, masks, small.at[0], g_taps.at[0], g_cbias.at[0], grads.at[0], (i,)
        )
    start_rows(0, 1, grads.at[0], grads_all)
    steps(0, (0, 1))
    steps(1, (0, 2), (1, 2))
    for i in range(2):
        down(
            acts.at[0], g.at[1], w_down.at[1], small.at[1], acts.at[1], cot, None, g_gamma.at[1], (2 * i, 2 * i + 1)
        )
        if i == 0:
            steps(0, (1, 1))
    start_rows(1, 0, acts.at[1], acts_all)
    for b in range(2):
        small_grads(
            small_sums.at[b], g_taps.at[b], g_cbias.at[b], g_table.at[b], g_dbias.at[b], g_gamma.at[b], g_ubias.at[b]
        )

    def eighth(index):
        return pl.ds(pl.multiple_of(index * 8, 8), 8)

    def small_out():
        made = []
        for i in range(1, 8):
            distance, crossed = i // 2, i % 2
            b = section if not crossed else 1 - section
            to = dict(peer(0, distance), section=b)
            src = small_sums.at[b, eighth(along(0, distance))]
            made.append(remote(src, small_got.at[i - 1], small_send.at[i - 1], small_recv.at[i - 1], to))
        return made

    def small_plane():
        return [
            remote(small_sum, plane_small.at[j], small_send.at[7], small_recv.at[7], plane_peer(0, u, v))
            for j, (u, v) in enumerate(plane)
        ]

    def small_plane_wait(sems):
        return pltpu.make_async_copy(plane_small, plane_small, sems.at[7])

    def small_back():
        kept = small_all.at[eighth(coords[0])]
        return [remote(kept, kept, small_send.at[7 + d], small_recv.at[7 + d], peer(0, d)) for d in (1, 2, 3)]

    start(small_out())
    steps(0, (0, 2))
    arrived(small_out())
    total = small_sums[section, eighth(coords[0]), :]
    for i in range(7):
        total = total + small_got[i]
    small_sum[...] = total
    start(small_plane())
    steps(0, (1, 2))
    steps(1, (0, 3), (1, 3))
    small_plane_wait(small_recv).wait()
    total = small_sum[...]
    for j in range(15):
        total = total + plane_small[j]
    small_all[eighth(coords[0]), :] = total
    start(small_back())
    steps(0, (0, 3), (1, 3))
    for b in range(2):
        steps(b, (0, 4), (1, 4))
    arrived(small_back())

    for swap in swaps:
        swap.wait_send()
    for b in range(2):
        finish_rows(b, 0, acts.at[b], acts_all)
        finish_rows(b, 1, grads.at[b], grads_all)

        @pl.when(section != b)
        def _():
            for h in range(2):
                for p in range(PARTS):
                    to_owner(b, h, p).wait_send()

        @pl.when(section == b)
        def _():
            for h in range(2):
                for p in range(PARTS):
                    for copy in line(b, h, p) + line_back(h, p):
                        copy.wait_send()
                    fifteen(h, p, plane_send).wait()
                    fifteen(h, p, plane_back_send).wait()
                    keep(h, p).wait()

    for copy in small_out() + small_back():
        copy.wait_send()
    small_plane_wait(small_send).wait()


def train(*arrays):
    smem = pl.BlockSpec(memory_space=pltpu.SMEM)
    vmem = pl.BlockSpec(memory_space=pltpu.VMEM)
    hbm = pl.BlockSpec(memory_space=pl.ANY)
    return pl.pallas_call(
        train_kernel,
        out_shape=[
            jax.ShapeDtypeStruct((2 * M, D), BF),
            jax.ShapeDtypeStruct((2 * M, D), BF),
            jax.ShapeDtypeStruct((GRADS, D), BF),
            jax.ShapeDtypeStruct((SMALL, D), F32),
        ],
        in_specs=[smem, smem] + [vmem] * 7 + [hbm] * 4,
        out_specs=[hbm, hbm, hbm, vmem],
        scratch_shapes=[
            pltpu.VMEM((M, D), BF),
            pltpu.VMEM((M, D), BF),
            pltpu.VMEM((2, 24, D), F32),
            pltpu.VMEM((2, D, FF), BF),
            pltpu.VMEM((2, FF, D), BF),
            pltpu.VMEM((2, M, D), BF),
            pltpu.VMEM((2, M, D), BF),
            pltpu.VMEM((2, GRADS, D), BF),
            pltpu.VMEM((2, SMALL, D), F32),
            pltpu.VMEM((ROWS, 4, PADDED, 128), F32),
            pltpu.VMEM((ROWS, 6, SPAN, 128), F32),
            pltpu.VMEM((M, 128), BF),
            pltpu.VMEM((2, 128, 2 * D), BF),
            pltpu.VMEM((2, M, D), F32),
            pltpu.VMEM((2, M, 128), F32),
            pltpu.VMEM((2, M, D), BF),
            pltpu.VMEM((2, M, FF), BF),
            pltpu.VMEM((2, M, FF), BF),
            pltpu.VMEM((M, D), BF),
            pltpu.VMEM((M, D), BF),
            pltpu.VMEM((2, 8, 2 * D), F32),
            pltpu.VMEM((2, 7, 8, D), F32),
            pltpu.VMEM((2, 8, D), F32),
            pltpu.VMEM((2, 8, D), F32),
            pltpu.VMEM((2, 8, FF), F32),
            pltpu.VMEM((2, 8, D), F32),
            pltpu.VMEM((GRADS, D), BF),
            pltpu.VMEM((2, PARTS, 3, QUARTER, D), BF),
            pltpu.VMEM((2, PARTS, 15) + PIECE, BF),
            pltpu.VMEM((2, PARTS, QUARTER, D), BF),
            pltpu.VMEM((7, 8, D), F32),
            pltpu.VMEM((8, D), F32),
            pltpu.VMEM((15, 8, D), F32),
        ]
        + [pltpu.SemaphoreType.DMA((n,)) for n in (4, 10, 3, 3, 6, 6, 4, 4, 18, 18, 6, 6, 6, 6, 18, 18, 11, 11)],
        compiler_params=pltpu.CompilerParams(collective_id=0, has_side_effects=True, vmem_limit_bytes=63 * MIB),
        cost_estimate=pl.CostEstimate(flops=24 * M * D * FF, bytes_accessed=24 * MIB, transcendentals=4 * M * FF),
    )(*arrays)


def finish_kernel(
    acts, grads, weights, small,
    acts_out, grads_out, g_taps, g_cbias, g_scale, g_shift, g_up, g_ubias, g_down, g_dbias, g_gamma,
    held, half_grads, half_weights, full_grads, full_weights, load_sems, store_sems,
):
    whole = pltpu.make_async_copy(acts, held, load_sems.at[10])
    held_out = pltpu.make_async_copy(held, acts_out.at[0], store_sems.at[10])
    loads = []
    for i in range(4):
        rows = at(i * D, D)
        loads.append(pltpu.make_async_copy(grads.at[rows], half_grads.at[rows], load_sems.at[i]))
    for i in range(6):
        rows = at(i * D, D)
        loads.append(pltpu.make_async_copy(weights.at[rows], half_weights.at[rows], load_sems.at[4 + i]))
    whole.start()
    for load in loads:
        load.start()
    g_taps[...] = jnp.concatenate([small[TAPS + k : TAPS + k + 1, :][None] for k in range(7)], axis=0)
    g_cbias[...] = small[CBIAS : CBIAS + 1, :]
    g_scale[0] = small[SCALE : SCALE + 4, :]
    g_shift[0] = small[SHIFT : SHIFT + 4, :]
    g_dbias[...] = small[DBIAS : DBIAS + 1, :]
    g_gamma[...] = small[GAMMA : GAMMA + 1, :]
    for k in range(3):
        g_ubias[:, at(k * D, D)] = small[UBIAS + k : UBIAS + k + 1, :]
    whole.wait()
    held_out.start()
    stores = [held_out]
    for i in range(10):
        rows = at((i if i < 4 else i - 4) * D, D)
        loads[i].wait()
        if i < 4:
            full_grads[rows, :] = half_grads[rows, :].astype(F32)
            copy = pltpu.make_async_copy(full_grads.at[rows], grads_out.at[0, rows], store_sems.at[i])
        else:
            full_weights[rows, :] = half_weights[rows, :].astype(F32)
            target = g_down.at[0, rows] if i < 7 else g_up.at[0, :, at((i - 7) * D, D)]
            copy = pltpu.make_async_copy(full_weights.at[rows], target, store_sems.at[i])
        copy.start()
        stores.append(copy)
    for copy in stores:
        copy.wait()


def finish(acts, grads, weights, small):
    vmem = pl.BlockSpec(memory_space=pltpu.VMEM)
    hbm = pl.BlockSpec(memory_space=pl.ANY)

    def out(*shape, kind=F32):
        return jax.ShapeDtypeStruct(shape, kind)

    return pl.pallas_call(
        finish_kernel,
        out_shape=[
            out(1, 2 * M, D, kind=BF), out(1, 2 * M, D), out(7, 1, D), out(1, D), out(1, 4, D), out(1, 4, D),
            out(1, D, FF), out(1, FF), out(1, FF, D), out(1, D), out(1, D),
        ],
        in_specs=[hbm, hbm, hbm, vmem],
        out_specs=[hbm, hbm, vmem, vmem, vmem, vmem, hbm, vmem, hbm, vmem, vmem],
        scratch_shapes=[
            pltpu.VMEM((2 * M, D), BF),
            pltpu.VMEM((2 * M, D), BF),
            pltpu.VMEM((GRADS, D), BF),
            pltpu.VMEM((2 * M, D), F32),
            pltpu.VMEM((GRADS, D), F32),
            pltpu.SemaphoreType.DMA((11,)),
            pltpu.SemaphoreType.DMA((11,)),
        ],
        compiler_params=pltpu.CompilerParams(vmem_limit_bytes=60 * MIB),
    )(acts, grads, weights, small)


def shards(
    frames, cotangent, lengths, bw_ids, conv_weight, conv_bias, scale_table, shift_table,
    w_up, b_up, w_down, b_down, layer_scale,
):
    acts, grads, weights, small = train(
        lengths, bw_ids, jnp.transpose(conv_weight, (1, 0, 2)), conv_bias, scale_table, shift_table, b_down, layer_scale, b_up,
        frames, cotangent, w_up[0], w_down[0],
    )
    outs = list(finish(acts, grads, weights, small))
    outs[2] = jnp.transpose(outs[2], (1, 0, 2))
    return tuple(outs)


def solution(mesh):
    rows = P("dp", None)
    matrix, vector = P("section", None, None), P("section", None)
    in_specs = (rows,) * 4 + (matrix, vector, matrix, matrix, matrix, vector, matrix, vector, vector)
    stacked = P("section", "dp", None)
    out_specs = (stacked, stacked, matrix, vector, matrix, matrix, matrix, vector, matrix, vector, vector)
    return jax.shard_map(shards, mesh=mesh, in_specs=in_specs, out_specs=out_specs, check_vma=False)
```

```python
import functools
import math

import jax
import jax.numpy as jnp
import numpy as np
from jax import lax
from jax.experimental import pallas as pl
from jax.experimental.pallas import tpu as pltpu
from jax.sharding import PartitionSpec as P

BF = jnp.bfloat16
F32 = jnp.float32
MESH = pl.DeviceIdType.MESH
MIB = 2**20

SPAN = 512
D = 512
FF = 1536
ROWS = 2
M = ROWS * SPAN
HALO = 8
PADDED = SPAN + 2 * HALO
STEP = 64
TILE = 256
GRADS = 2 * FF
SMALL = 32
EXP_SCALE = -0.5 * math.log2(math.e)
PDF_SCALE = 1.0 / math.sqrt(2.0 * math.pi)
ERF_SCALE = 1.0 / math.sqrt(2.0)
TAPS, CBIAS, SCALE, SHIFT, DBIAS, GAMMA, UBIAS = 0, 7, 8, 12, 16, 17, 18
SMALL_ROWS = 21
OFFSETS = (0, 1, 2, 4, 5, 6)


def at(start, size):
    return slice(start, start + size) if isinstance(start, int) else pl.ds(start, size)


def times(index, size):
    return index * size if isinstance(index, int) else pl.multiple_of(index * size, size)


def over_rows(value):
    return jnp.sum(value.reshape(value.shape[0] // 8, 8, value.shape[1]), axis=0)


def dot(a, b, dims):
    return lax.dot_general(a, b, (dims, ((), ())), preferred_element_type=F32)


def clip_tables(first, lengths, ids, clip_of, masks, hot):
    for r in range(ROWS):
        row = first + r
        ends = [lengths[row, 0]]
        for c in (1, 2):
            ends.append(ends[-1] + lengths[row, c])
        band_of = [ids[row, c] for c in range(4)]
        clip_of[0:HALO] = jnp.full((HALO, 128), -1.0, F32)
        clip_of[HALO + SPAN :] = jnp.full((HALO, 128), -1.0, F32)
        lane = lax.broadcasted_iota(jnp.int32, (STEP, 128), 1)
        for i in range(SPAN // STEP):
            frame = lax.broadcasted_iota(jnp.int32, (STEP, 128), 0) + i * STEP
            late = [frame >= end for end in ends]
            clip = jnp.where(late[0], 1.0, 0.0) + jnp.where(late[1], 1.0, 0.0) + jnp.where(late[2], 1.0, 0.0)
            clip_of[at(HALO + i * STEP, STEP), :] = clip
            band = jnp.where(late[0], band_of[1], band_of[0])
            band = jnp.where(late[1], band_of[2], band)
            band = jnp.where(late[2], band_of[3], band)
            one = (lane == band) | (lane == band + 4)
            hot[at(r * SPAN + i * STEP, STEP), :] = jnp.where(one, 1.0, 0.0).astype(BF)
        for i in range(SPAN // STEP):
            here = clip_of[at(HALO + i * STEP, STEP), :]
            for q, k in enumerate(OFFSETS):
                there = clip_of[at(HALO + i * STEP + k - 3, STEP), :]
                masks[r, q, at(i * STEP, STEP), :] = jnp.where(there == here, 1.0, 0.0)


def band_table(small, table):
    table[...] = jnp.zeros_like(table)
    for half, first in enumerate((SCALE, SHIFT)):
        whole = small[first : first + 4, :]
        upper = whole.astype(BF).astype(F32)
        both = jnp.concatenate([upper, whole - upper], axis=0)
        table[0:8, half * D : (half + 1) * D] = both.astype(BF)


def weave(*lists):
    order = [((i + 0.5) / len(steps), n, step) for n, steps in enumerate(lists) for i, step in enumerate(steps)]
    for _, _, step in sorted(order, key=lambda entry: entry[:2]):
        step()


def conv_norm(r, x, padded, masks, hot, table, small, normed, rstd_out, adapted):
    def widen():
        for j in range(4):
            padded[r, j, 0:HALO] = jnp.zeros((HALO, 128), F32)
            padded[r, j, HALO + SPAN :] = jnp.zeros((HALO, 128), F32)
            padded[r, j, HALO : HALO + SPAN] = x[r * SPAN : (r + 1) * SPAN, 128 * j : 128 * (j + 1)].astype(F32)

    def tile(i):
        here = at(i * STEP, STEP)
        hidden = []
        for j in range(4):
            c = slice(128 * j, 128 * (j + 1))
            total = small[CBIAS : CBIAS + 1, c] + padded[r, j, at(i * STEP + HALO, STEP), :] * small[3:4, c]
            for q, k in enumerate(OFFSETS):
                moved = padded[r, j, at(i * STEP + (HALO + k - 3), STEP), :]
                total = total + moved * masks[r, q, here, :] * small[k : k + 1, c]
            hidden.append(total)
        mean = jnp.sum(hidden[0] + hidden[1] + hidden[2] + hidden[3], axis=1, keepdims=True) * (1.0 / D)
        center = [h - mean for h in hidden]
        square = [c * c for c in center]
        spread = jnp.sum(square[0] + square[1] + square[2] + square[3], axis=1, keepdims=True) * (1.0 / D)
        rstd = lax.rsqrt(spread + 1e-6)
        rows = at(r * SPAN + i * STEP, STEP)
        tables = dot(hot[rows, :], table[...], ((1,), (0,)))
        rstd_out[rows, :] = jnp.broadcast_to(rstd, (STEP, 128))
        for j in range(4):
            c = slice(128 * j, 128 * (j + 1))
            n = center[j] * rstd
            normed[rows, c] = n
            adapted[rows, c] = (n * tables[:, c] + tables[:, D + 128 * j : D + 128 * (j + 1)]).astype(BF)

    return [widen] + [functools.partial(tile, i) for i in range(SPAN // STEP)]


def up_gelu(r, adapted, w_up, small, g, slope):
    def tile(i, c):
        rows, cols = at(i * TILE, TILE), at(c * TILE, TILE)
        bias = small[UBIAS + c // 2 : UBIAS + c // 2 + 1, at((c % 2) * TILE, TILE)]
        u = dot(adapted[rows, :], w_up[:, cols], ((1,), (0,))) + bias
        pdf = jnp.exp2((u * EXP_SCALE) * u) * PDF_SCALE
        cdf = 0.5 + 0.5 * lax.erf(u * ERF_SCALE)
        g[rows, cols] = (u * cdf).astype(BF)
        slope[rows, cols] = (cdf + u * pdf).astype(BF)

    return [functools.partial(tile, i, c) for i in (2 * r, 2 * r + 1) for c in range(FF // TILE)]


def down(r, x, g, w_down, small, out, upstream, v_out, g_gamma):
    def tile(i, c):
        rows, cols = at(i * TILE, TILE), at(c * TILE, TILE)
        v = dot(g[rows, :], w_down[:, cols], ((1,), (0,))) + small[DBIAS : DBIAS + 1, cols]
        out[rows, cols] = (x[rows, cols].astype(F32) + small[GAMMA : GAMMA + 1, cols] * v).astype(BF)
        if v_out is not None:
            v_out[rows, cols] = v.astype(BF)
        if upstream is not None:
            g_gamma[:, cols] += over_rows(upstream[rows, cols].astype(F32) * v)

    return [functools.partial(tile, i, c) for i in (2 * r, 2 * r + 1) for c in range(2)]


def down_back(r, upstream, w_down, small, slope, dv_out, g_dbias, g_ubias, v, g_gamma):
    def scaled(i):
        rows = at(i * TILE, TILE)
        dy = upstream[rows, :].astype(F32)
        dv = small[GAMMA : GAMMA + 1, :] * dy
        g_dbias[...] += over_rows(dv)
        if v is not None:
            g_gamma[...] += over_rows(dy * v[rows, :].astype(F32))
        dv_out[rows, :] = dv.astype(BF)

    def tile(i, c):
        rows, cols = at(i * TILE, TILE), at(c * TILE, TILE)
        du = dot(dv_out[rows, :], w_down[cols, :], ((1,), (1,))) * slope[rows, cols].astype(F32)
        slope[rows, cols] = du.astype(BF)
        g_ubias[:, cols] += over_rows(du)

    steps = []
    for i in (2 * r, 2 * r + 1):
        steps.append(functools.partial(scaled, i))
        steps += [functools.partial(tile, i, c) for c in range(FF // TILE)]
    return steps


def down_grad(g, dv, out, tiles=range(FF // TILE)):
    for c in tiles:
        cols = at(c * TILE, TILE)
        out[cols, :] = dot(g[:, cols], dv[...], ((0,), (0,))).astype(BF)


def up_grad(adapted, du, out, tiles=range(FF // TILE)):
    for c in tiles:
        place = (at((c // 2) * D, D), at((c % 2) * TILE, TILE))
        out[place] = dot(adapted[...], du[:, at(c * TILE, TILE)], ((0,), (0,))).astype(BF)


def norm_back(r, du, w_up, hot, table, normed, rstd, d_hidden, g_table):
    def tile(i):
        rows = at(i * TILE, TILE)
        da = dot(du[rows, :], w_up[...], ((1,), (1,)))
        n = normed[rows, :]
        dan = da * n
        ones = hot[rows, 0:16]
        g_table[:, 0:D] += dot(ones, dan.astype(BF), ((0,), (0,)))[0:8]
        g_table[:, D:] += dot(ones, da.astype(BF), ((0,), (0,)))[0:8]
        scale = dot(hot[rows, :], table[:, 0:D], ((1,), (0,)))
        dn = da * scale
        mean = jnp.sum(dn, axis=1, keepdims=True) * (1.0 / D)
        along = jnp.sum(dan * scale, axis=1, keepdims=True) * (1.0 / D)
        dh = (dn - mean - n * along) * rstd[rows, 0:1]
        first = i * TILE % SPAN
        for j in range(4):
            d_hidden[r, j, at(HALO + first, TILE), :] = dh[:, 128 * j : 128 * (j + 1)]

    return [functools.partial(tile, i) for i in (2 * r, 2 * r + 1)]


def conv_back(r, x, upstream, d_hidden, masks, small, g_taps, g_cbias, out):
    def edges():
        for j in range(4):
            d_hidden[r, j, 0:HALO] = jnp.zeros((HALO, 128), F32)
            d_hidden[r, j, HALO + SPAN :] = jnp.zeros((HALO, 128), F32)

    def tile(i):
        rows = at(r * SPAN + i * STEP, STEP)
        here = at(i * STEP, STEP)
        for j in range(4):
            c = slice(128 * j, 128 * (j + 1))
            value = x[rows, c].astype(F32)
            dh = d_hidden[r, j, at(i * STEP + HALO, STEP), :]
            total = upstream[rows, c].astype(F32) + dh * small[3:4, c]
            g_cbias[:, c] += over_rows(dh)
            g_taps[3, :, c] += over_rows(value * dh)
            for q, k in enumerate(OFFSETS):
                part = d_hidden[r, j, at(i * STEP + (HALO + k - 3), STEP), :] * masks[r, q, here, :]
                total = total + part * small[6 - k : 7 - k, c]
                g_taps[6 - k, :, c] += over_rows(value * part)
            out[rows, c] = total.astype(out.dtype)

    return [edges] + [functools.partial(tile, i) for i in range(SPAN // STEP)]


def small_grads(out, g_taps, g_cbias, g_table, g_dbias, g_gamma, g_ubias):
    def whole(value):
        return jnp.sum(value, axis=0, keepdims=True)

    rows = [whole(g_taps[k]) for k in range(7)] + [whole(g_cbias[...])]
    rows += [g_table[0:4, 0:D], g_table[0:4, D:], whole(g_dbias[...]), whole(g_gamma[...])]
    rows += [whole(g_ubias[:, k * D : (k + 1) * D]) for k in range(3)]
    rows.append(jnp.zeros((SMALL - SMALL_ROWS, D), F32))
    out[...] = jnp.concatenate(rows, axis=0)


PARTS = 3
PART_ROWS = FF // PARTS
QUARTER = PART_ROWS // 4
PIECE = (16, 256)
STRIDES = (16, 4, 1)
LAST = ("first+", "first-", "second+", "second-", "own", "pass+", "pass-")


def train_kernel(
    lengths, ids, conv_weight, conv_bias, scale_table, shift_table, b_down, layer_scale, b_up,
    frames, cotangent, own_up, own_down,
    acts_all, grads_all, weight_all, small_all,
    h_taps, h_cbias, h_scale, h_shift, h_dbias, h_gamma, h_ubias,
    x0, cot, small, w_up, w_down, acts, grads, weight_grads, small_sums,
    padded, masks, hot, table, normed, rstd, adapted, g, slope,
    g_table, g_taps, g_cbias, g_dbias, g_ubias, g_gamma,
    pair, final, line_got, plane_got, line_sum, small_got, small_sum, plane_small, small_held,
    load_sems, store_sems, swap_send, swap_recv, pair_send, pair_recv, row_send, row_recv,
    line_send, line_recv, plane_send, plane_recv, plane_back_send, plane_back_recv, line_back_send, line_back_recv,
    small_send, small_recv,
):
    section = lax.axis_index("section")
    dp = lax.axis_index("dp")
    coords = (dp // 16, (dp // 4) % 4, dp % 4)
    other = {"dp": dp, "section": 1 - section}
    mine = pl.ds(pl.multiple_of(section * M, M), M)
    v0, dv = acts.at[1], grads.at[0]

    ring = [[lax.rem(coords[axis] + distance, 4) for distance in range(4)] for axis in range(3)]
    step = [[(ring[axis][d] - coords[axis]) * STRIDES[axis] for d in range(4)] for axis in range(3)]
    line_dp = [[dp + step[axis][d] for d in range(4)] for axis in range(3)]

    def along(axis, distance):
        return ring[axis][distance]

    def peer(axis, distance):
        return {"dp": line_dp[axis][distance], "section": section}

    def crossed(axis, distance):
        return {"dp": line_dp[axis][distance], "section": 1 - section}

    plane_dp = [[[line_dp[(p + 1) % 3][u] + step[(p + 2) % 3][v] for v in range(4)] for u in range(4)] for p in range(3)]

    def plane_peer(p, u, v):
        return {"dp": plane_dp[p][u][v], "section": section}

    plane = [(u, v) for u in range(4) for v in range(4) if u or v]

    def remote(src, dst, send_sem, recv_sem, device):
        return pltpu.make_async_remote_copy(
            src_ref=src, dst_ref=dst, send_sem=send_sem, recv_sem=recv_sem, device_id=device, device_id_type=MESH
        )

    loads = [
        pltpu.make_async_copy(frames.at[mine], x0, load_sems.at[0]),
        pltpu.make_async_copy(own_up, w_up.at[section], load_sems.at[1]),
        pltpu.make_async_copy(own_down, w_down.at[section], load_sems.at[2]),
        pltpu.make_async_copy(cotangent.at[mine], cot, load_sems.at[3]),
    ]
    given = (conv_weight, conv_bias, scale_table, shift_table, b_down, layer_scale, b_up)
    packs = [
        pltpu.make_async_copy(src, dst, load_sems.at[4 + i])
        for i, (src, dst) in enumerate(zip(given, (h_taps, h_cbias, h_scale, h_shift, h_dbias, h_gamma, h_ubias)))
    ]
    for load in packs + loads:
        load.start()
    barrier = pltpu.get_barrier_semaphore()
    pl.semaphore_signal(barrier, inc=1, device_id=other, device_id_type=MESH)
    for axis in range(3):
        for distance in (1, 2, 3):
            pl.semaphore_signal(barrier, inc=1, device_id=peer(axis, distance), device_id_type=MESH)
            pl.semaphore_signal(barrier, inc=1, device_id=crossed(axis, distance), device_id_type=MESH)
        for u, v in plane:
            if u and v:
                pl.semaphore_signal(barrier, inc=1, device_id=plane_peer(axis, u, v), device_id_type=MESH)
    for load in packs:
        load.wait()
    rows = [h_taps[k] for k in range(7)] + [h_cbias[...], h_scale[0], h_shift[0], h_dbias[...], h_gamma[...]]
    rows += [h_ubias[:, k * D : (k + 1) * D] for k in range(3)] + [jnp.zeros((24 - SMALL_ROWS, D), F32)]
    small[section] = jnp.concatenate(rows, axis=0)
    pl.semaphore_wait(barrier, 46)
    swaps = [
        remote(small.at[section], small.at[section], swap_send.at[0], swap_recv.at[0], other),
        remote(own_up, w_up.at[section], swap_send.at[1], swap_recv.at[1], other),
        remote(own_down, w_down.at[section], swap_send.at[2], swap_recv.at[2], other),
    ]
    for swap in swaps:
        swap.start()

    def part_rows(p):
        return at(p * PART_ROWS, PART_ROWS)

    def to_adder(b, h, p):
        rows, i = part_rows(p), h * PARTS + p
        return remote(weight_grads.at[b, h, rows], pair.at[h, rows], pair_send.at[i], pair_recv.at[i], other)

    def kept_rows(b, kind, source, target):
        return pltpu.make_async_copy(source, target.at[mine], store_sems.at[2 * kind + b])

    def sent_rows(b, kind, source, target):
        i = 2 * kind + b
        return remote(source, target.at[mine], row_send.at[i], row_recv.at[i], other)

    def start_rows(b, *what):
        @pl.when(section == b)
        def _():
            kept_rows(b, *what).start()

        @pl.when(section != b)
        def _():
            sent_rows(b, *what).start()

    def finish_rows(b, *what):
        @pl.when(section == b)
        def _():
            kept_rows(b, *what).wait()
            sent_rows(b, *what).wait_recv()

        @pl.when(section != b)
        def _():
            sent_rows(b, *what).wait_send()

    def quarter(p, distance):
        first = p * PART_ROWS + along(p, distance) * QUARTER
        return pl.ds(pl.multiple_of(first, QUARTER), QUARTER)

    def piece(first, p, u, v):
        i, j = along((p + 1) % 3, u), along((p + 2) % 3, v)
        rows = pl.ds(pl.multiple_of(first + i * 32 + (j // 2) * 16, 16), 16)
        return rows, pl.ds(pl.multiple_of(lax.rem(j, 2) * 256, 256), 256)

    def own_piece(p):
        return piece(p * PART_ROWS + coords[p] * QUARTER, p, 0, 0)

    def line(b, h, p):
        made = []
        for distance in (1, 2, 3):
            i = (h * PARTS + p) * 3 + distance - 1
            src, dst = weight_grads.at[b, h, quarter(p, distance)], line_got.at[h, p, distance - 1]
            made.append(remote(src, dst, line_send.at[i], line_recv.at[i], peer(p, distance)))
        return made

    HALVES = (at(0, 256), at(256, 256))

    def last(p, name):
        i = LAST.index(name) + p * len(LAST)
        if name == "own":
            rows = quarter(p, 0)
            src, dst, to = pair.at[:, rows], final.at[:, rows], other
        elif name in ("pass+", "pass-"):
            away, half, towards = (3, 0, 1) if name == "pass+" else (1, 1, 3)
            src = dst = final.at[:, quarter(p, away), HALVES[half]]
            to = peer(p, towards)
        else:
            towards = 1 if name[-1] == "+" else 3
            half = {"first+": 0, "second+": 1, "first-": 1, "second-": 0}[name]
            rows = quarter(p, 0)
            src, dst, to = pair.at[:, rows, HALVES[half]], final.at[:, rows, HALVES[half]], crossed(p, towards)
        return remote(src, dst, line_back_send.at[i], line_back_recv.at[i], to)

    def spread(p):
        made = []
        for j, (u, v) in enumerate(plane):
            rows, cols = piece(0, p, u, v)
            src = line_sum.at[:, p, rows, cols]
            made.append(remote(src, plane_got.at[p, j], plane_send.at[p], plane_recv.at[p], plane_peer(p, u, v)))
        return made

    def spread_back(p):
        rows, cols = own_piece(p)
        kept = pair.at[:, rows, cols]
        return [remote(kept, kept, plane_back_send.at[p], plane_back_recv.at[p], plane_peer(p, u, v)) for u, v in plane]

    def fifteen(p, sems):
        return pltpu.make_async_copy(plane_got.at[p], plane_got.at[p], sems.at[p])

    def start(copies):
        for copy in copies:
            copy.start()

    def arrived(copies):
        for copy in copies:
            copy.wait_recv()

    def keep(p):
        rows = part_rows(p)
        return pltpu.make_async_copy(final.at[:, rows], weight_all.at[:, rows], store_sems.at[4 + p])

    def add_pair(b, h, p):
        to_adder(b, h, p).wait_recv()
        rows = part_rows(p)
        weight_grads[b, h, rows, :] = weight_grads[b, h, rows, :] + pair[h, rows, :]
        start(line(b, h, p))

    def add_line(b, p):
        for h in range(2):
            arrived(line(b, h, p))
            total = weight_grads[b, h, quarter(p, 0), :].astype(F32)
            for d in range(3):
                total = total + line_got[h, p, d].astype(F32)
            line_sum[h, p] = total.astype(BF)
        start(spread(p))

    def add_plane(p):
        fifteen(p, plane_recv).wait()
        rows, cols = piece(0, p, 0, 0)
        total = line_sum[:, p, rows, cols].astype(F32)
        for j in range(15):
            total = total + plane_got[p, j].astype(F32)
        rows, cols = own_piece(p)
        pair[:, rows, cols] = total.astype(BF)
        start(spread_back(p))

    def send_line(p):
        fifteen(p, plane_back_recv).wait()
        start([last(p, name) for name in LAST[:5]])

    def pass_on(p):
        for sign in "+-":
            last(p, "first" + sign).wait_recv()
            last(p, "pass" + sign).start()

    def store_part(p):
        arrived([last(p, name) for name in LAST[2:]])
        keep(p).start()

    def adder(b, act, *todo):
        @pl.when(section != b)
        def _():
            for what in todo:
                act(*what)

    every = [(p,) for p in range(PARTS)]

    def hand_over(b, h, parts=range(PARTS)):
        @pl.when(section == b)
        def _():
            for p in parts:
                to_adder(b, h, p).start()

    clip_tables(section * ROWS, lengths, ids, padded.at[0, 0], masks, hot)
    for ref in (g_table, g_taps, g_cbias, g_dbias, g_ubias, g_gamma):
        ref[...] = jnp.zeros_like(ref)
    def needs(b, *parts):
        @pl.when(section == b)
        def _():
            for i in parts:
                if i:
                    loads[i].wait()

        @pl.when(section != b)
        def _():
            for i in parts:
                swaps[i].wait_recv()

    needs(0, 0)
    band_table(small.at[0], table.at[0])
    loads[0].wait()

    def norms(b, r, x):
        return conv_norm(
            r, x, padded, masks, hot, table.at[b], small.at[b], normed.at[b], rstd.at[b], adapted.at[b]
        )

    def ups(b, r):
        return up_gelu(r, adapted.at[b], w_up.at[b], small.at[b], g.at[b], slope.at[b])

    def downs(b, r):
        if b == 0:
            return down(r, x0, g.at[0], w_down.at[0], small.at[0], acts.at[0], None, v0, None)
        return down(r, acts.at[0], g.at[1], w_down.at[1], small.at[1], acts.at[1], cot, None, g_gamma.at[1])

    def down_backs(b, r):
        dy, v = ((grads.at[1], v0), (cot, None))[b]
        return down_back(
            r, dy, w_down.at[b], small.at[b], slope.at[b], dv, g_dbias.at[b], g_ubias.at[b], v, g_gamma.at[b]
        )

    def norm_backs(b, r):
        return norm_back(
            r, slope.at[b], w_up.at[b], hot, table.at[b], normed.at[b], rstd.at[b], padded, g_table.at[b]
        )

    def conv_backs(b, r):
        x, dy = ((x0, grads.at[1]), (acts.at[0], cot))[b]
        return conv_back(r, x, dy, padded, masks, small.at[b], g_taps.at[b], g_cbias.at[b], grads.at[b])

    weave(norms(0, 0, x0))
    needs(0, 1)
    weave(norms(0, 1, x0), ups(0, 0))
    needs(0, 2)
    weave(ups(0, 1), downs(0, 0))
    needs(1, 0, 1, 2)
    band_table(small.at[1], table.at[1])
    loads[3].wait()
    weave(downs(0, 1), norms(1, 0, acts.at[0]))
    start_rows(0, 0, acts.at[0], acts_all)
    weave(norms(1, 1, acts.at[0]), ups(1, 0))
    weave(ups(1, 1), down_backs(1, 0))

    weave(down_backs(1, 1))
    down_grad(g.at[1], dv, weight_grads.at[1, 0])
    hand_over(1, 0)
    up_grad(adapted.at[1], slope.at[1], weight_grads.at[1, 1])
    hand_over(1, 1)
    weave(norm_backs(1, 0))
    weave(norm_backs(1, 1), conv_backs(1, 0))
    adder(1, add_pair, *[(1, 0, p) for p in range(PARTS)])
    weave(conv_backs(1, 1), down_backs(0, 0))
    start_rows(1, 1, grads.at[1], grads_all)
    adder(1, add_pair, *[(1, 1, p) for p in range(PARTS)])
    weave(down_backs(0, 1))
    for p in range(PARTS):
        down_grad(g.at[0], dv, weight_grads.at[0, 0], (2 * p, 2 * p + 1))
        hand_over(0, 0, (p,))
    for p in range(PARTS):
        up_grad(adapted.at[0], slope.at[0], weight_grads.at[0, 1], (2 * p, 2 * p + 1))
        hand_over(0, 1, (p,))
        adder(0, add_pair, (0, 0, p))
    adder(0, add_pair, *[(0, 1, p) for p in range(PARTS)])
    adder(1, add_line, *[(1, p) for p in range(PARTS)])
    weave(norm_backs(0, 0))
    weave(norm_backs(0, 1), conv_backs(0, 0))
    adder(1, add_plane, *every)
    weave(conv_backs(0, 1), downs(1, 0), downs(1, 1))
    start_rows(0, 1, grads.at[0], grads_all)
    start_rows(1, 0, acts.at[1], acts_all)
    for b in range(2):
        small_grads(
            small_sums.at[b], g_taps.at[b], g_cbias.at[b], g_table.at[b], g_dbias.at[b], g_gamma.at[b], g_ubias.at[b]
        )

    def eighth(index):
        return pl.ds(pl.multiple_of(index * 8, 8), 8)

    def small_out():
        made = []
        for i in range(1, 8):
            distance = i // 2
            b = 1 - section if i % 2 else section
            to = crossed(0, distance) if i % 2 else peer(0, distance)
            src = small_sums.at[b, eighth(along(0, distance))]
            made.append(remote(src, small_got.at[i - 1], small_send.at[i - 1], small_recv.at[i - 1], to))
        return made

    def small_plane():
        return [
            remote(small_sum, plane_small.at[j], small_send.at[7], small_recv.at[7], plane_peer(0, u, v))
            for j, (u, v) in enumerate(plane)
        ]

    def small_plane_wait(sems):
        return pltpu.make_async_copy(plane_small, plane_small, sems.at[7])

    def small_back():
        kept = small_held.at[eighth(coords[0])]
        return [remote(kept, kept, small_send.at[7 + d], small_recv.at[7 + d], peer(0, d)) for d in (1, 2, 3)]

    start(small_out())
    adder(0, add_line, *[(0, p) for p in range(PARTS)])
    arrived(small_out())
    total = small_sums[section, eighth(coords[0]), :]
    for i in range(7):
        total = total + small_got[i]
    small_sum[...] = total
    start(small_plane())
    adder(1, send_line, *every)
    adder(0, add_plane, *every)
    small_plane_wait(small_recv).wait()
    total = small_sum[...]
    for j in range(15):
        total = total + plane_small[j]
    small_held[eighth(coords[0]), :] = total
    start(small_back())
    adder(0, pass_on, *every)
    adder(0, send_line, *every)
    arrived(small_back())
    small_keep = pltpu.make_async_copy(small_held, small_all, store_sems.at[7])
    small_keep.start()
    adder(1, pass_on, *every)
    for p in range(PARTS):
        store_part(p)

    for swap in swaps:
        swap.wait_send()
    for b in range(2):
        finish_rows(b, 0, acts.at[b], acts_all)
        finish_rows(b, 1, grads.at[b], grads_all)

        @pl.when(section == b)
        def _():
            for h in range(2):
                for p in range(PARTS):
                    to_adder(b, h, p).wait_send()

        @pl.when(section != b)
        def _():
            for h in range(2):
                for p in range(PARTS):
                    for copy in line(b, h, p):
                        copy.wait_send()

    for p in range(PARTS):
        for name in LAST:
            last(p, name).wait_send()
        fifteen(p, plane_send).wait()
        fifteen(p, plane_back_send).wait()
        keep(p).wait()
    for copy in small_out() + small_back():
        copy.wait_send()
    small_plane_wait(small_send).wait()
    small_keep.wait()


def train(*arrays):
    smem = pl.BlockSpec(memory_space=pltpu.SMEM)
    hbm = pl.BlockSpec(memory_space=pl.ANY)
    return pl.pallas_call(
        train_kernel,
        out_shape=[
            jax.ShapeDtypeStruct((2 * M, D), BF),
            jax.ShapeDtypeStruct((2 * M, D), BF),
            jax.ShapeDtypeStruct((2, FF, D), BF),
            jax.ShapeDtypeStruct((SMALL, D), F32),
        ],
        in_specs=[smem, smem] + [hbm] * 11,
        out_specs=[hbm] * 4,
        scratch_shapes=[
            pltpu.VMEM(shape, F32)
            for shape in ((7, 1, D), (1, D), (1, 4, D), (1, 4, D), (1, D), (1, D), (1, FF))
        ]
        + [
            pltpu.VMEM((M, D), BF),
            pltpu.VMEM((M, D), BF),
            pltpu.VMEM((2, 24, D), F32),
            pltpu.VMEM((2, D, FF), BF),
            pltpu.VMEM((2, FF, D), BF),
            pltpu.VMEM((2, M, D), BF),
            pltpu.VMEM((2, M, D), BF),
            pltpu.VMEM((2, 2, FF, D), BF),
            pltpu.VMEM((2, SMALL, D), F32),
            pltpu.VMEM((ROWS, 4, PADDED, 128), F32),
            pltpu.VMEM((ROWS, 6, SPAN, 128), F32),
            pltpu.VMEM((M, 128), BF),
            pltpu.VMEM((2, 128, 2 * D), BF),
            pltpu.VMEM((2, M, D), F32),
            pltpu.VMEM((2, M, 128), F32),
            pltpu.VMEM((2, M, D), BF),
            pltpu.VMEM((2, M, FF), BF),
            pltpu.VMEM((2, M, FF), BF),
            pltpu.VMEM((2, 8, 2 * D), F32),
            pltpu.VMEM((2, 7, 8, D), F32),
            pltpu.VMEM((2, 8, D), F32),
            pltpu.VMEM((2, 8, D), F32),
            pltpu.VMEM((2, 8, FF), F32),
            pltpu.VMEM((2, 8, D), F32),
            pltpu.VMEM((2, FF, D), BF),
            pltpu.VMEM((2, FF, D), BF),
            pltpu.VMEM((2, PARTS, 3, QUARTER, D), BF),
            pltpu.VMEM((PARTS, 15, 2) + PIECE, BF),
            pltpu.VMEM((2, PARTS, QUARTER, D), BF),
            pltpu.VMEM((7, 8, D), F32),
            pltpu.VMEM((8, D), F32),
            pltpu.VMEM((15, 8, D), F32),
            pltpu.VMEM((SMALL, D), F32),
        ]
        + [pltpu.SemaphoreType.DMA((n,)) for n in (11, 8, 3, 3, 6, 6, 4, 4, 18, 18, 3, 3, 3, 3, 21, 21, 11, 11)],
        compiler_params=pltpu.CompilerParams(collective_id=0, has_side_effects=True, vmem_limit_bytes=63 * MIB),
        cost_estimate=pl.CostEstimate(flops=24 * M * D * FF, bytes_accessed=24 * MIB, transcendentals=4 * M * FF),
    )(*arrays)


def finish_kernel(
    acts, grads, weights, small,
    acts_out, grads_out, g_taps, g_cbias, g_scale, g_shift, g_up, g_ubias, g_down, g_dbias, g_gamma,
    h_taps, h_cbias, h_scale, h_shift, h_ubias, h_dbias, h_gamma,
    held_small, held, half_grads, half_weights, full_grads, full_weights, load_sems, store_sems,
):
    loads = [pltpu.make_async_copy(small, held_small, load_sems.at[0])]
    for i in range(4):
        rows = at(i * D, D)
        loads.append(pltpu.make_async_copy(grads.at[rows], half_grads.at[rows], load_sems.at[1 + i]))
    for i in range(6):
        rows = at(i * D, D)
        loads.append(
            pltpu.make_async_copy(weights.at[i // 3, at(i % 3 * D, D)], half_weights.at[rows], load_sems.at[5 + i])
        )
    for i in range(4):
        rows = at(i * D, D)
        loads.append(pltpu.make_async_copy(acts.at[rows], held.at[rows], load_sems.at[11 + i]))
    for load in loads:
        load.start()
    stores = []

    def store(src, dst):
        copy = pltpu.make_async_copy(src, dst, store_sems.at[len(stores)])
        copy.start()
        stores.append(copy)

    for i in range(10):
        rows = at((i if i < 4 else i - 4) * D, D)
        loads[1 + i].wait()
        if i < 4:
            full_grads[rows, :] = half_grads[rows, :].astype(F32)
            store(full_grads.at[rows], grads_out.at[0, rows])
        else:
            full_weights[rows, :] = half_weights[rows, :].astype(F32)
            store(full_weights.at[rows], g_down.at[0, rows] if i < 7 else g_up.at[0, :, at((i - 7) * D, D)])
        if i == 0:
            loads[0].wait()
            h_taps[...] = jnp.concatenate([held_small[TAPS + k : TAPS + k + 1, :][None] for k in range(7)], axis=0)
            h_cbias[...] = held_small[CBIAS : CBIAS + 1, :]
            h_scale[0] = held_small[SCALE : SCALE + 4, :]
            h_shift[0] = held_small[SHIFT : SHIFT + 4, :]
            h_dbias[...] = held_small[DBIAS : DBIAS + 1, :]
            h_gamma[...] = held_small[GAMMA : GAMMA + 1, :]
            for k in range(3):
                h_ubias[:, at(k * D, D)] = held_small[UBIAS + k : UBIAS + k + 1, :]
            held_outs = (h_taps, h_cbias, h_scale, h_shift, h_ubias, h_dbias, h_gamma)
            for src, dst in zip(held_outs, (g_taps, g_cbias, g_scale, g_shift, g_ubias, g_dbias, g_gamma)):
                store(src, dst)
    for i in range(4):
        loads[11 + i].wait()
        rows = at(i * D, D)
        store(held.at[rows], acts_out.at[0, rows])
    for copy in stores:
        copy.wait()


def finish(acts, grads, weights, small):
    hbm = pl.BlockSpec(memory_space=pl.ANY)
    shapes = ((7, 1, D), (1, D), (1, 4, D), (1, 4, D), (1, FF), (1, D), (1, D))

    def out(*shape, kind=F32):
        return jax.ShapeDtypeStruct(shape, kind)

    return pl.pallas_call(
        finish_kernel,
        out_shape=[
            out(1, 2 * M, D, kind=BF), out(1, 2 * M, D), out(7, 1, D), out(1, D), out(1, 4, D), out(1, 4, D),
            out(1, D, FF), out(1, FF), out(1, FF, D), out(1, D), out(1, D),
        ],
        in_specs=[hbm] * 4,
        out_specs=[hbm] * 11,
        scratch_shapes=[pltpu.VMEM(shape, F32) for shape in shapes]
        + [
            pltpu.VMEM((SMALL, D), F32),
            pltpu.VMEM((2 * M, D), BF),
            pltpu.VMEM((2 * M, D), BF),
            pltpu.VMEM((GRADS, D), BF),
            pltpu.VMEM((2 * M, D), F32),
            pltpu.VMEM((GRADS, D), F32),
            pltpu.SemaphoreType.DMA((15,)),
            pltpu.SemaphoreType.DMA((21,)),
        ],
        compiler_params=pltpu.CompilerParams(vmem_limit_bytes=60 * MIB),
    )(acts, grads, weights, small)


def shards(
    frames, cotangent, lengths, bw_ids, conv_weight, conv_bias, scale_table, shift_table,
    w_up, b_up, w_down, b_down, layer_scale,
):
    acts, grads, weights, small = train(
        lengths, bw_ids, jnp.transpose(conv_weight, (1, 0, 2)), conv_bias, scale_table, shift_table, b_down, layer_scale, b_up,
        frames, cotangent, w_up[0], w_down[0],
    )
    outs = list(finish(acts, grads, weights, small))
    outs[2] = jnp.transpose(outs[2], (1, 0, 2))
    return tuple(outs)


def solution(mesh):
    rows = P("dp", None)
    matrix, vector = P("section", None, None), P("section", None)
    in_specs = (rows,) * 4 + (matrix, vector, matrix, matrix, matrix, vector, matrix, vector, vector)
    stacked = P("section", "dp", None)
    out_specs = (stacked, stacked, matrix, vector, matrix, matrix, matrix, vector, matrix, vector, vector)
    return jax.shard_map(shards, mesh=mesh, in_specs=in_specs, out_specs=out_specs, check_vma=False)
```

```python
import functools
import math

import jax
import jax.numpy as jnp
import numpy as np
from jax import lax
from jax.experimental import pallas as pl
from jax.experimental.pallas import tpu as pltpu
from jax.sharding import PartitionSpec as P

BF = jnp.bfloat16
F32 = jnp.float32
MESH = pl.DeviceIdType.MESH
MIB = 2**20

SPAN = 512
D = 512
FF = 1536
ROWS = 2
M = ROWS * SPAN
HALO = 8
PADDED = SPAN + 2 * HALO
STEP = 64
TILE = 256
GRADS = 2 * FF
SMALL = 32
EXP_SCALE = -0.5 * math.log2(math.e)
PDF_SCALE = 1.0 / math.sqrt(2.0 * math.pi)
ERF_SCALE = 1.0 / math.sqrt(2.0)
TAPS, CBIAS, SCALE, SHIFT, DBIAS, GAMMA, UBIAS = 0, 7, 8, 12, 16, 17, 18
SMALL_ROWS = 21
OFFSETS = (0, 1, 2, 4, 5, 6)


def at(start, size):
    return slice(start, start + size) if isinstance(start, int) else pl.ds(start, size)


def times(index, size):
    return index * size if isinstance(index, int) else pl.multiple_of(index * size, size)


def over_rows(value):
    return jnp.sum(value.reshape(value.shape[0] // 8, 8, value.shape[1]), axis=0)


def dot(a, b, dims):
    return lax.dot_general(a, b, (dims, ((), ())), preferred_element_type=F32)


def clip_tables(first, lengths, ids, clip_of, masks, hot):
    for r in range(ROWS):
        row = first + r
        ends = [lengths[row, 0]]
        for c in (1, 2):
            ends.append(ends[-1] + lengths[row, c])
        band_of = [ids[row, c] for c in range(4)]
        clip_of[0:HALO] = jnp.full((HALO, 128), -1.0, F32)
        clip_of[HALO + SPAN :] = jnp.full((HALO, 128), -1.0, F32)
        lane = lax.broadcasted_iota(jnp.int32, (STEP, 128), 1)
        for i in range(SPAN // STEP):
            frame = lax.broadcasted_iota(jnp.int32, (STEP, 128), 0) + i * STEP
            late = [frame >= end for end in ends]
            clip = jnp.where(late[0], 1.0, 0.0) + jnp.where(late[1], 1.0, 0.0) + jnp.where(late[2], 1.0, 0.0)
            clip_of[at(HALO + i * STEP, STEP), :] = clip
            band = jnp.where(late[0], band_of[1], band_of[0])
            band = jnp.where(late[1], band_of[2], band)
            band = jnp.where(late[2], band_of[3], band)
            one = (lane == band) | (lane == band + 4)
            hot[at(r * SPAN + i * STEP, STEP), :] = jnp.where(one, 1.0, 0.0).astype(BF)
        for i in range(SPAN // STEP):
            here = clip_of[at(HALO + i * STEP, STEP), :]
            for q, k in enumerate(OFFSETS):
                there = clip_of[at(HALO + i * STEP + k - 3, STEP), :]
                masks[r, q, at(i * STEP, STEP), :] = jnp.where(there == here, 1.0, 0.0)


def band_table(small, table):
    table[...] = jnp.zeros_like(table)
    for half, first in enumerate((SCALE, SHIFT)):
        whole = small[first : first + 4, :]
        upper = whole.astype(BF).astype(F32)
        both = jnp.concatenate([upper, whole - upper], axis=0)
        table[0:8, half * D : (half + 1) * D] = both.astype(BF)


def weave(*lists):
    order = [((i + 0.5) / len(steps), n, step) for n, steps in enumerate(lists) for i, step in enumerate(steps)]
    for _, _, step in sorted(order, key=lambda entry: entry[:2]):
        step()


def conv_norm(r, x, padded, masks, hot, table, small, normed, rstd_out, adapted):
    def widen():
        for j in range(4):
            padded[r, j, 0:HALO] = jnp.zeros((HALO, 128), F32)
            padded[r, j, HALO + SPAN :] = jnp.zeros((HALO, 128), F32)
            padded[r, j, HALO : HALO + SPAN] = x[r * SPAN : (r + 1) * SPAN, 128 * j : 128 * (j + 1)].astype(F32)

    def tile(i):
        here = at(i * STEP, STEP)
        hidden = []
        for j in range(4):
            c = slice(128 * j, 128 * (j + 1))
            total = small[CBIAS : CBIAS + 1, c] + padded[r, j, at(i * STEP + HALO, STEP), :] * small[3:4, c]
            for q, k in enumerate(OFFSETS):
                moved = padded[r, j, at(i * STEP + (HALO + k - 3), STEP), :]
                total = total + moved * masks[r, q, here, :] * small[k : k + 1, c]
            hidden.append(total)
        mean = jnp.sum(hidden[0] + hidden[1] + hidden[2] + hidden[3], axis=1, keepdims=True) * (1.0 / D)
        center = [h - mean for h in hidden]
        square = [c * c for c in center]
        spread = jnp.sum(square[0] + square[1] + square[2] + square[3], axis=1, keepdims=True) * (1.0 / D)
        rstd = lax.rsqrt(spread + 1e-6)
        rows = at(r * SPAN + i * STEP, STEP)
        tables = dot(hot[rows, :], table[...], ((1,), (0,)))
        rstd_out[rows, :] = jnp.broadcast_to(rstd, (STEP, 128))
        for j in range(4):
            c = slice(128 * j, 128 * (j + 1))
            n = center[j] * rstd
            normed[rows, c] = n
            adapted[rows, c] = (n * tables[:, c] + tables[:, D + 128 * j : D + 128 * (j + 1)]).astype(BF)

    return [widen] + [functools.partial(tile, i) for i in range(SPAN // STEP)]


def up_gelu(r, adapted, w_up, small, g, slope):
    def tile(i, c):
        rows, cols = at(i * TILE, TILE), at(c * TILE, TILE)
        bias = small[UBIAS + c // 2 : UBIAS + c // 2 + 1, at((c % 2) * TILE, TILE)]
        u = dot(adapted[rows, :], w_up[:, cols], ((1,), (0,))) + bias
        pdf = jnp.exp2((u * EXP_SCALE) * u) * PDF_SCALE
        cdf = 0.5 + 0.5 * lax.erf(u * ERF_SCALE)
        g[rows, cols] = (u * cdf).astype(BF)
        slope[rows, cols] = (cdf + u * pdf).astype(BF)

    return [functools.partial(tile, i, c) for i in (2 * r, 2 * r + 1) for c in range(FF // TILE)]


def down(r, x, g, w_down, small, out, upstream, v_out, g_gamma):
    def tile(i, c):
        rows, cols = at(i * TILE, TILE), at(c * TILE, TILE)
        v = dot(g[rows, :], w_down[:, cols], ((1,), (0,))) + small[DBIAS : DBIAS + 1, cols]
        out[rows, cols] = (x[rows, cols].astype(F32) + small[GAMMA : GAMMA + 1, cols] * v).astype(BF)
        if v_out is not None:
            v_out[rows, cols] = v.astype(BF)
        if upstream is not None:
            g_gamma[:, cols] += over_rows(upstream[rows, cols].astype(F32) * v)

    return [functools.partial(tile, i, c) for i in (2 * r, 2 * r + 1) for c in range(2)]


def down_back(r, upstream, w_down, small, slope, dv_out, g_dbias, g_ubias, v, g_gamma):
    def scaled(i):
        rows = at(i * TILE, TILE)
        dy = upstream[rows, :].astype(F32)
        dv = small[GAMMA : GAMMA + 1, :] * dy
        g_dbias[...] += over_rows(dv)
        if v is not None:
            g_gamma[...] += over_rows(dy * v[rows, :].astype(F32))
        dv_out[rows, :] = dv.astype(BF)

    def tile(i, c):
        rows, cols = at(i * TILE, TILE), at(c * TILE, TILE)
        du = dot(dv_out[rows, :], w_down[cols, :], ((1,), (1,))) * slope[rows, cols].astype(F32)
        slope[rows, cols] = du.astype(BF)
        g_ubias[:, cols] += over_rows(du)

    steps = []
    for i in (2 * r, 2 * r + 1):
        steps.append(functools.partial(scaled, i))
        steps += [functools.partial(tile, i, c) for c in range(FF // TILE)]
    return steps


def down_grad(g, dv, out, tiles=range(FF // TILE)):
    for c in tiles:
        cols = at(c * TILE, TILE)
        out[cols, :] = dot(g[:, cols], dv[...], ((0,), (0,))).astype(BF)


def up_grad(adapted, du, out, tiles=range(FF // TILE)):
    for c in tiles:
        place = (at((c // 2) * D, D), at((c % 2) * TILE, TILE))
        out[place] = dot(adapted[...], du[:, at(c * TILE, TILE)], ((0,), (0,))).astype(BF)


def norm_back(r, du, w_up, hot, table, normed, rstd, d_hidden, g_table):
    def tile(i):
        rows = at(i * TILE, TILE)
        da = dot(du[rows, :], w_up[...], ((1,), (1,)))
        n = normed[rows, :]
        dan = da * n
        ones = hot[rows, 0:16]
        g_table[:, 0:D] += dot(ones, dan.astype(BF), ((0,), (0,)))[0:8]
        g_table[:, D:] += dot(ones, da.astype(BF), ((0,), (0,)))[0:8]
        scale = dot(hot[rows, :], table[:, 0:D], ((1,), (0,)))
        dn = da * scale
        mean = jnp.sum(dn, axis=1, keepdims=True) * (1.0 / D)
        along = jnp.sum(dan * scale, axis=1, keepdims=True) * (1.0 / D)
        dh = (dn - mean - n * along) * rstd[rows, 0:1]
        first = i * TILE % SPAN
        for j in range(4):
            d_hidden[r, j, at(HALO + first, TILE), :] = dh[:, 128 * j : 128 * (j + 1)]

    return [functools.partial(tile, i) for i in (2 * r, 2 * r + 1)]


def conv_back(r, x, upstream, d_hidden, masks, small, g_taps, g_cbias, out):
    def edges():
        for j in range(4):
            d_hidden[r, j, 0:HALO] = jnp.zeros((HALO, 128), F32)
            d_hidden[r, j, HALO + SPAN :] = jnp.zeros((HALO, 128), F32)

    def tile(i):
        rows = at(r * SPAN + i * STEP, STEP)
        here = at(i * STEP, STEP)
        for j in range(4):
            c = slice(128 * j, 128 * (j + 1))
            value = x[rows, c].astype(F32)
            dh = d_hidden[r, j, at(i * STEP + HALO, STEP), :]
            total = upstream[rows, c].astype(F32) + dh * small[3:4, c]
            g_cbias[:, c] += over_rows(dh)
            g_taps[3, :, c] += over_rows(value * dh)
            for q, k in enumerate(OFFSETS):
                part = d_hidden[r, j, at(i * STEP + (HALO + k - 3), STEP), :] * masks[r, q, here, :]
                total = total + part * small[6 - k : 7 - k, c]
                g_taps[6 - k, :, c] += over_rows(value * part)
            out[rows, c] = total.astype(out.dtype)

    return [edges] + [functools.partial(tile, i) for i in range(SPAN // STEP)]


def small_grads(out, g_taps, g_cbias, g_table, g_dbias, g_gamma, g_ubias):
    def whole(value):
        return jnp.sum(value, axis=0, keepdims=True)

    rows = [whole(g_taps[k]) for k in range(7)] + [whole(g_cbias[...])]
    rows += [g_table[0:4, 0:D], g_table[0:4, D:], whole(g_dbias[...]), whole(g_gamma[...])]
    rows += [whole(g_ubias[:, k * D : (k + 1) * D]) for k in range(3)]
    rows.append(jnp.zeros((SMALL - SMALL_ROWS, D), F32))
    out[...] = jnp.concatenate(rows, axis=0)


PARTS = 3
PART_ROWS = FF // PARTS
QUARTER = PART_ROWS // 4
PIECE = (16, 256)
STRIDES = (16, 4, 1)
LAST = ("first+", "first-", "second+", "second-", "own", "pass+", "pass-")


def train_kernel(
    lengths, ids, conv_weight, conv_bias, scale_table, shift_table, b_down, layer_scale, b_up,
    frames, cotangent, own_up, own_down,
    acts_all, grads_all, weight_all, small_all,
    h_taps, h_cbias, h_scale, h_shift, h_dbias, h_gamma, h_ubias,
    x0, cot, small, w_up, w_down, acts, grads, weight_grads, small_sums,
    padded, masks, hot, table, normed, rstd, adapted, g, slope,
    g_table, g_taps, g_cbias, g_dbias, g_ubias, g_gamma,
    pair, final, line_got, plane_got, line_sum, small_got, small_sum, plane_small, small_held,
    load_sems, store_sems, swap_send, swap_recv, pair_send, pair_recv, row_send, row_recv,
    line_send, line_recv, plane_send, plane_recv, plane_back_send, plane_back_recv, line_back_send, line_back_recv,
    small_send, small_recv,
):
    section = lax.axis_index("section")
    dp = lax.axis_index("dp")
    coords = (dp // 16, (dp // 4) % 4, dp % 4)
    other = {"dp": dp, "section": 1 - section}
    mine = pl.ds(pl.multiple_of(section * M, M), M)
    v0, dv = acts.at[1], grads.at[0]

    ring = [[lax.rem(coords[axis] + distance, 4) for distance in range(4)] for axis in range(3)]
    step = [[(ring[axis][d] - coords[axis]) * STRIDES[axis] for d in range(4)] for axis in range(3)]
    line_dp = [[dp + step[axis][d] for d in range(4)] for axis in range(3)]

    def along(axis, distance):
        return ring[axis][distance]

    def peer(axis, distance):
        return {"dp": line_dp[axis][distance], "section": section}

    def crossed(axis, distance):
        return {"dp": line_dp[axis][distance], "section": 1 - section}

    plane_dp = [[[line_dp[(p + 1) % 3][u] + step[(p + 2) % 3][v] for v in range(4)] for u in range(4)] for p in range(3)]

    def plane_peer(p, u, v):
        return {"dp": plane_dp[p][u][v], "section": section}

    plane = [(u, v) for u in range(4) for v in range(4) if u or v]

    def remote(src, dst, send_sem, recv_sem, device):
        return pltpu.make_async_remote_copy(
            src_ref=src, dst_ref=dst, send_sem=send_sem, recv_sem=recv_sem, device_id=device, device_id_type=MESH
        )

    loads = [
        pltpu.make_async_copy(frames.at[mine], x0, load_sems.at[0]),
        pltpu.make_async_copy(own_up, w_up.at[section], load_sems.at[1]),
        pltpu.make_async_copy(own_down, w_down.at[section], load_sems.at[2]),
        pltpu.make_async_copy(cotangent.at[mine], cot, load_sems.at[3]),
    ]
    given = (conv_weight, conv_bias, scale_table, shift_table, b_down, layer_scale, b_up)
    packs = [
        pltpu.make_async_copy(src, dst, load_sems.at[4 + i])
        for i, (src, dst) in enumerate(zip(given, (h_taps, h_cbias, h_scale, h_shift, h_dbias, h_gamma, h_ubias)))
    ]
    for load in packs + loads:
        load.start()
    barrier = pltpu.get_barrier_semaphore()
    pl.semaphore_signal(barrier, inc=1, device_id=other, device_id_type=MESH)
    for axis in range(3):
        for distance in (1, 2, 3):
            pl.semaphore_signal(barrier, inc=1, device_id=peer(axis, distance), device_id_type=MESH)
            pl.semaphore_signal(barrier, inc=1, device_id=crossed(axis, distance), device_id_type=MESH)
        for u, v in plane:
            if u and v:
                pl.semaphore_signal(barrier, inc=1, device_id=plane_peer(axis, u, v), device_id_type=MESH)
    for load in packs:
        load.wait()
    rows = [h_taps[k] for k in range(7)] + [h_cbias[...], h_scale[0], h_shift[0], h_dbias[...], h_gamma[...]]
    rows += [h_ubias[:, k * D : (k + 1) * D] for k in range(3)] + [jnp.zeros((24 - SMALL_ROWS, D), F32)]
    small[section] = jnp.concatenate(rows, axis=0)
    pl.semaphore_wait(barrier, 46)
    swaps = [
        remote(small.at[section], small.at[section], swap_send.at[0], swap_recv.at[0], other),
        remote(own_up, w_up.at[section], swap_send.at[1], swap_recv.at[1], other),
        remote(own_down, w_down.at[section], swap_send.at[2], swap_recv.at[2], other),
    ]
    for swap in swaps:
        swap.start()

    def part_rows(p):
        return at(p * PART_ROWS, PART_ROWS)

    def to_adder(b, h, p):
        rows, i = part_rows(p), h * PARTS + p
        return remote(weight_grads.at[b, h, rows], pair.at[h, rows], pair_send.at[i], pair_recv.at[i], other)

    def kept_rows(b, kind, source, target):
        return pltpu.make_async_copy(source, target.at[mine], store_sems.at[2 * kind + b])

    def sent_rows(b, kind, source, target):
        i = 2 * kind + b
        return remote(source, target.at[mine], row_send.at[i], row_recv.at[i], other)

    def start_rows(b, *what):
        @pl.when(section == b)
        def _():
            kept_rows(b, *what).start()

        @pl.when(section != b)
        def _():
            sent_rows(b, *what).start()

    def finish_rows(b, *what):
        @pl.when(section == b)
        def _():
            kept_rows(b, *what).wait()
            sent_rows(b, *what).wait_recv()

        @pl.when(section != b)
        def _():
            sent_rows(b, *what).wait_send()

    def quarter(p, distance):
        first = p * PART_ROWS + along(p, distance) * QUARTER
        return pl.ds(pl.multiple_of(first, QUARTER), QUARTER)

    def piece(first, p, u, v):
        i, j = along((p + 1) % 3, u), along((p + 2) % 3, v)
        rows = pl.ds(pl.multiple_of(first + i * 32 + (j // 2) * 16, 16), 16)
        return rows, pl.ds(pl.multiple_of(lax.rem(j, 2) * 256, 256), 256)

    def own_piece(p):
        return piece(p * PART_ROWS + coords[p] * QUARTER, p, 0, 0)

    def line(b, h, p):
        made = []
        for distance in (1, 2, 3):
            i = (h * PARTS + p) * 3 + distance - 1
            src, dst = weight_grads.at[b, h, quarter(p, distance)], line_got.at[h, p, distance - 1]
            made.append(remote(src, dst, line_send.at[i], line_recv.at[i], peer(p, distance)))
        return made

    HALVES = (at(0, 256), at(256, 256))

    def last(p, name):
        i = LAST.index(name) + p * len(LAST)
        if name == "own":
            rows = quarter(p, 0)
            src, dst, to = pair.at[:, rows], final.at[:, rows], other
        elif name in ("pass+", "pass-"):
            away, half, towards = (3, 0, 1) if name == "pass+" else (1, 1, 3)
            src = dst = final.at[:, quarter(p, away), HALVES[half]]
            to = peer(p, towards)
        else:
            towards = 1 if name[-1] == "+" else 3
            half = {"first+": 0, "second+": 1, "first-": 1, "second-": 0}[name]
            rows = quarter(p, 0)
            src, dst, to = pair.at[:, rows, HALVES[half]], final.at[:, rows, HALVES[half]], crossed(p, towards)
        return remote(src, dst, line_back_send.at[i], line_back_recv.at[i], to)

    def spread(p):
        made = []
        for j, (u, v) in enumerate(plane):
            rows, cols = piece(0, p, u, v)
            src = line_sum.at[:, p, rows, cols]
            made.append(remote(src, plane_got.at[p, j], plane_send.at[p], plane_recv.at[p], plane_peer(p, u, v)))
        return made

    def spread_back(p):
        rows, cols = own_piece(p)
        kept = pair.at[:, rows, cols]
        return [remote(kept, kept, plane_back_send.at[p], plane_back_recv.at[p], plane_peer(p, u, v)) for u, v in plane]

    def fifteen(p, sems):
        return pltpu.make_async_copy(plane_got.at[p], plane_got.at[p], sems.at[p])

    def start(copies):
        for copy in copies:
            copy.start()

    def arrived(copies):
        for copy in copies:
            copy.wait_recv()

    def keep(p):
        rows = part_rows(p)
        return pltpu.make_async_copy(final.at[:, rows], weight_all.at[:, rows], store_sems.at[4 + p])

    def add_pair(b, h, p):
        to_adder(b, h, p).wait_recv()
        rows = part_rows(p)
        weight_grads[b, h, rows, :] = weight_grads[b, h, rows, :] + pair[h, rows, :]
        start(line(b, h, p))

    def add_line(b, p):
        for h in range(2):
            arrived(line(b, h, p))
            total = weight_grads[b, h, quarter(p, 0), :].astype(F32)
            for d in range(3):
                total = total + line_got[h, p, d].astype(F32)
            line_sum[h, p] = total.astype(BF)
        start(spread(p))

    def add_plane(p):
        fifteen(p, plane_recv).wait()
        rows, cols = piece(0, p, 0, 0)
        total = line_sum[:, p, rows, cols].astype(F32)
        for j in range(15):
            total = total + plane_got[p, j].astype(F32)
        rows, cols = own_piece(p)
        pair[:, rows, cols] = total.astype(BF)
        start(spread_back(p))

    def send_line(p):
        fifteen(p, plane_back_recv).wait()
        start([last(p, name) for name in LAST[:5]])

    def pass_on(p):
        for sign in "+-":
            last(p, "first" + sign).wait_recv()
            last(p, "pass" + sign).start()

    def store_part(p):
        arrived([last(p, name) for name in LAST[2:]])
        keep(p).start()

    def adder(b, act, *todo):
        @pl.when(section != b)
        def _():
            for what in todo:
                act(*what)

    every = [(p,) for p in range(PARTS)]

    def hand_over(b, h, parts=range(PARTS)):
        @pl.when(section == b)
        def _():
            for p in parts:
                to_adder(b, h, p).start()

    clip_tables(section * ROWS, lengths, ids, padded.at[0, 0], masks, hot)
    for ref in (g_table, g_taps, g_cbias, g_dbias, g_ubias, g_gamma):
        ref[...] = jnp.zeros_like(ref)
    def needs(b, *parts):
        @pl.when(section == b)
        def _():
            for i in parts:
                if i:
                    loads[i].wait()

        @pl.when(section != b)
        def _():
            for i in parts:
                swaps[i].wait_recv()

    needs(0, 0)
    band_table(small.at[0], table.at[0])
    loads[0].wait()

    def norms(b, r, x):
        return conv_norm(
            r, x, padded, masks, hot, table.at[b], small.at[b], normed.at[b], rstd.at[b], adapted.at[b]
        )

    def ups(b, r):
        return up_gelu(r, adapted.at[b], w_up.at[b], small.at[b], g.at[b], slope.at[b])

    def downs(b, r):
        if b == 0:
            return down(r, x0, g.at[0], w_down.at[0], small.at[0], acts.at[0], None, v0, None)
        return down(r, acts.at[0], g.at[1], w_down.at[1], small.at[1], acts.at[1], cot, None, g_gamma.at[1])

    def down_backs(b, r):
        dy, v = ((grads.at[1], v0), (cot, None))[b]
        return down_back(
            r, dy, w_down.at[b], small.at[b], slope.at[b], dv, g_dbias.at[b], g_ubias.at[b], v, g_gamma.at[b]
        )

    def norm_backs(b, r):
        return norm_back(
            r, slope.at[b], w_up.at[b], hot, table.at[b], normed.at[b], rstd.at[b], padded, g_table.at[b]
        )

    def conv_backs(b, r):
        x, dy = ((x0, grads.at[1]), (acts.at[0], cot))[b]
        return conv_back(r, x, dy, padded, masks, small.at[b], g_taps.at[b], g_cbias.at[b], grads.at[b])

    weave(norms(0, 0, x0))
    needs(0, 1)
    weave(norms(0, 1, x0), ups(0, 0))
    needs(0, 2)
    weave(ups(0, 1), downs(0, 0))
    needs(1, 0, 1, 2)
    band_table(small.at[1], table.at[1])
    loads[3].wait()
    weave(norms(1, 0, acts.at[0]))
    weave(ups(1, 0), downs(0, 1))
    start_rows(0, 0, acts.at[0], acts_all)
    weave(norms(1, 1, acts.at[0]))
    weave(ups(1, 1), down_backs(1, 0))

    weave(down_backs(1, 1))
    down_grad(g.at[1], dv, weight_grads.at[1, 0])
    hand_over(1, 0)
    up_grad(adapted.at[1], slope.at[1], weight_grads.at[1, 1])
    hand_over(1, 1)
    weave(norm_backs(1, 0))
    weave(norm_backs(1, 1), conv_backs(1, 0))
    adder(1, add_pair, *[(1, 0, p) for p in range(PARTS)])
    weave(conv_backs(1, 1), down_backs(0, 0))
    start_rows(1, 1, grads.at[1], grads_all)
    adder(1, add_pair, *[(1, 1, p) for p in range(PARTS)])
    weave(down_backs(0, 1))
    for p in range(PARTS):
        down_grad(g.at[0], dv, weight_grads.at[0, 0], (2 * p, 2 * p + 1))
        hand_over(0, 0, (p,))
    for p in range(PARTS):
        up_grad(adapted.at[0], slope.at[0], weight_grads.at[0, 1], (2 * p, 2 * p + 1))
        hand_over(0, 1, (p,))
        adder(0, add_pair, (0, 0, p))
    adder(0, add_pair, *[(0, 1, p) for p in range(PARTS)])
    adder(1, add_line, *[(1, p) for p in range(PARTS)])
    weave(norm_backs(0, 0))
    weave(norm_backs(0, 1), conv_backs(0, 0))
    weave(conv_backs(0, 1), downs(1, 0), downs(1, 1))
    start_rows(0, 1, grads.at[0], grads_all)
    start_rows(1, 0, acts.at[1], acts_all)
    for b in range(2):
        small_grads(
            small_sums.at[b], g_taps.at[b], g_cbias.at[b], g_table.at[b], g_dbias.at[b], g_gamma.at[b], g_ubias.at[b]
        )

    def eighth(index):
        return pl.ds(pl.multiple_of(index * 8, 8), 8)

    def small_out():
        made = []
        for i in range(1, 8):
            distance = i // 2
            b = 1 - section if i % 2 else section
            to = crossed(0, distance) if i % 2 else peer(0, distance)
            src = small_sums.at[b, eighth(along(0, distance))]
            made.append(remote(src, small_got.at[i - 1], small_send.at[i - 1], small_recv.at[i - 1], to))
        return made

    def small_plane():
        return [
            remote(small_sum, plane_small.at[j], small_send.at[7], small_recv.at[7], plane_peer(0, u, v))
            for j, (u, v) in enumerate(plane)
        ]

    def small_plane_wait(sems):
        return pltpu.make_async_copy(plane_small, plane_small, sems.at[7])

    def small_back():
        kept = small_held.at[eighth(coords[0])]
        return [remote(kept, kept, small_send.at[7 + d], small_recv.at[7 + d], peer(0, d)) for d in (1, 2, 3)]

    start(small_out())
    adder(1, add_plane, *every)
    adder(0, add_line, *[(0, p) for p in range(PARTS)])
    arrived(small_out())
    total = small_sums[section, eighth(coords[0]), :]
    for i in range(7):
        total = total + small_got[i]
    small_sum[...] = total
    start(small_plane())
    adder(0, add_plane, *every)
    small_plane_wait(small_recv).wait()
    total = small_sum[...]
    for j in range(15):
        total = total + plane_small[j]
    small_held[eighth(coords[0]), :] = total
    start(small_back())
    adder(1, send_line, *every)
    adder(0, send_line, *every)
    adder(0, pass_on, *every)
    arrived(small_back())
    small_keep = pltpu.make_async_copy(small_held, small_all, store_sems.at[7])
    small_keep.start()
    adder(1, pass_on, *every)
    for p in range(PARTS):
        store_part(p)

    for swap in swaps:
        swap.wait_send()
    for b in range(2):
        finish_rows(b, 0, acts.at[b], acts_all)
        finish_rows(b, 1, grads.at[b], grads_all)

        @pl.when(section == b)
        def _():
            for h in range(2):
                for p in range(PARTS):
                    to_adder(b, h, p).wait_send()

        @pl.when(section != b)
        def _():
            for h in range(2):
                for p in range(PARTS):
                    for copy in line(b, h, p):
                        copy.wait_send()

    for p in range(PARTS):
        for name in LAST:
            last(p, name).wait_send()
        fifteen(p, plane_send).wait()
        fifteen(p, plane_back_send).wait()
        keep(p).wait()
    for copy in small_out() + small_back():
        copy.wait_send()
    small_plane_wait(small_send).wait()
    small_keep.wait()


def train(*arrays):
    smem = pl.BlockSpec(memory_space=pltpu.SMEM)
    hbm = pl.BlockSpec(memory_space=pl.ANY)
    return pl.pallas_call(
        train_kernel,
        out_shape=[
            jax.ShapeDtypeStruct((2 * M, D), BF),
            jax.ShapeDtypeStruct((2 * M, D), BF),
            jax.ShapeDtypeStruct((2, FF, D), BF),
            jax.ShapeDtypeStruct((SMALL, D), F32),
        ],
        in_specs=[smem, smem] + [hbm] * 11,
        out_specs=[hbm] * 4,
        scratch_shapes=[
            pltpu.VMEM(shape, F32)
            for shape in ((7, 1, D), (1, D), (1, 4, D), (1, 4, D), (1, D), (1, D), (1, FF))
        ]
        + [
            pltpu.VMEM((M, D), BF),
            pltpu.VMEM((M, D), BF),
            pltpu.VMEM((2, 24, D), F32),
            pltpu.VMEM((2, D, FF), BF),
            pltpu.VMEM((2, FF, D), BF),
            pltpu.VMEM((2, M, D), BF),
            pltpu.VMEM((2, M, D), BF),
            pltpu.VMEM((2, 2, FF, D), BF),
            pltpu.VMEM((2, SMALL, D), F32),
            pltpu.VMEM((ROWS, 4, PADDED, 128), F32),
            pltpu.VMEM((ROWS, 6, SPAN, 128), F32),
            pltpu.VMEM((M, 128), BF),
            pltpu.VMEM((2, 128, 2 * D), BF),
            pltpu.VMEM((2, M, D), F32),
            pltpu.VMEM((2, M, 128), F32),
            pltpu.VMEM((2, M, D), BF),
            pltpu.VMEM((2, M, FF), BF),
            pltpu.VMEM((2, M, FF), BF),
            pltpu.VMEM((2, 8, 2 * D), F32),
            pltpu.VMEM((2, 7, 8, D), F32),
            pltpu.VMEM((2, 8, D), F32),
            pltpu.VMEM((2, 8, D), F32),
            pltpu.VMEM((2, 8, FF), F32),
            pltpu.VMEM((2, 8, D), F32),
            pltpu.VMEM((2, FF, D), BF),
            pltpu.VMEM((2, FF, D), BF),
            pltpu.VMEM((2, PARTS, 3, QUARTER, D), BF),
            pltpu.VMEM((PARTS, 15, 2) + PIECE, BF),
            pltpu.VMEM((2, PARTS, QUARTER, D), BF),
            pltpu.VMEM((7, 8, D), F32),
            pltpu.VMEM((8, D), F32),
            pltpu.VMEM((15, 8, D), F32),
            pltpu.VMEM((SMALL, D), F32),
        ]
        + [pltpu.SemaphoreType.DMA((n,)) for n in (11, 8, 3, 3, 6, 6, 4, 4, 18, 18, 3, 3, 3, 3, 21, 21, 11, 11)],
        compiler_params=pltpu.CompilerParams(collective_id=0, has_side_effects=True, vmem_limit_bytes=63 * MIB),
        cost_estimate=pl.CostEstimate(flops=24 * M * D * FF, bytes_accessed=24 * MIB, transcendentals=4 * M * FF),
    )(*arrays)


def finish_kernel(
    acts, grads, weights, small,
    acts_out, grads_out, g_taps, g_cbias, g_scale, g_shift, g_up, g_ubias, g_down, g_dbias, g_gamma,
    h_taps, h_cbias, h_scale, h_shift, h_ubias, h_dbias, h_gamma,
    held_small, held, half_grads, half_weights, full_grads, full_weights, load_sems, store_sems,
):
    loads = [pltpu.make_async_copy(small, held_small, load_sems.at[0])]
    for i in range(4):
        rows = at(i * D, D)
        loads.append(pltpu.make_async_copy(grads.at[rows], half_grads.at[rows], load_sems.at[1 + i]))
    for i in range(6):
        rows = at(i * D, D)
        loads.append(
            pltpu.make_async_copy(weights.at[i // 3, at(i % 3 * D, D)], half_weights.at[rows], load_sems.at[5 + i])
        )
    for i in range(4):
        rows = at(i * D, D)
        loads.append(pltpu.make_async_copy(acts.at[rows], held.at[rows], load_sems.at[11 + i]))
    for load in loads:
        load.start()
    stores = []

    def store(src, dst):
        copy = pltpu.make_async_copy(src, dst, store_sems.at[len(stores)])
        copy.start()
        stores.append(copy)

    for i in range(10):
        rows = at((i if i < 4 else i - 4) * D, D)
        loads[1 + i].wait()
        if i < 4:
            full_grads[rows, :] = half_grads[rows, :].astype(F32)
            store(full_grads.at[rows], grads_out.at[0, rows])
        else:
            full_weights[rows, :] = half_weights[rows, :].astype(F32)
            store(full_weights.at[rows], g_down.at[0, rows] if i < 7 else g_up.at[0, :, at((i - 7) * D, D)])
        if i == 0:
            loads[0].wait()
            h_taps[...] = jnp.concatenate([held_small[TAPS + k : TAPS + k + 1, :][None] for k in range(7)], axis=0)
            h_cbias[...] = held_small[CBIAS : CBIAS + 1, :]
            h_scale[0] = held_small[SCALE : SCALE + 4, :]
            h_shift[0] = held_small[SHIFT : SHIFT + 4, :]
            h_dbias[...] = held_small[DBIAS : DBIAS + 1, :]
            h_gamma[...] = held_small[GAMMA : GAMMA + 1, :]
            for k in range(3):
                h_ubias[:, at(k * D, D)] = held_small[UBIAS + k : UBIAS + k + 1, :]
            held_outs = (h_taps, h_cbias, h_scale, h_shift, h_ubias, h_dbias, h_gamma)
            for src, dst in zip(held_outs, (g_taps, g_cbias, g_scale, g_shift, g_ubias, g_dbias, g_gamma)):
                store(src, dst)
    for i in range(4):
        loads[11 + i].wait()
        rows = at(i * D, D)
        store(held.at[rows], acts_out.at[0, rows])
    for copy in stores:
        copy.wait()


def finish(acts, grads, weights, small):
    hbm = pl.BlockSpec(memory_space=pl.ANY)
    shapes = ((7, 1, D), (1, D), (1, 4, D), (1, 4, D), (1, FF), (1, D), (1, D))

    def out(*shape, kind=F32):
        return jax.ShapeDtypeStruct(shape, kind)

    return pl.pallas_call(
        finish_kernel,
        out_shape=[
            out(1, 2 * M, D, kind=BF), out(1, 2 * M, D), out(7, 1, D), out(1, D), out(1, 4, D), out(1, 4, D),
            out(1, D, FF), out(1, FF), out(1, FF, D), out(1, D), out(1, D),
        ],
        in_specs=[hbm] * 4,
        out_specs=[hbm] * 11,
        scratch_shapes=[pltpu.VMEM(shape, F32) for shape in shapes]
        + [
            pltpu.VMEM((SMALL, D), F32),
            pltpu.VMEM((2 * M, D), BF),
            pltpu.VMEM((2 * M, D), BF),
            pltpu.VMEM((GRADS, D), BF),
            pltpu.VMEM((2 * M, D), F32),
            pltpu.VMEM((GRADS, D), F32),
            pltpu.SemaphoreType.DMA((15,)),
            pltpu.SemaphoreType.DMA((21,)),
        ],
        compiler_params=pltpu.CompilerParams(vmem_limit_bytes=60 * MIB),
    )(acts, grads, weights, small)


def shards(
    frames, cotangent, lengths, bw_ids, conv_weight, conv_bias, scale_table, shift_table,
    w_up, b_up, w_down, b_down, layer_scale,
):
    acts, grads, weights, small = train(
        lengths, bw_ids, jnp.transpose(conv_weight, (1, 0, 2)), conv_bias, scale_table, shift_table, b_down, layer_scale, b_up,
        frames, cotangent, w_up[0], w_down[0],
    )
    outs = list(finish(acts, grads, weights, small))
    outs[2] = jnp.transpose(outs[2], (1, 0, 2))
    return tuple(outs)


def solution(mesh):
    rows = P("dp", None)
    matrix, vector = P("section", None, None), P("section", None)
    in_specs = (rows,) * 4 + (matrix, vector, matrix, matrix, matrix, vector, matrix, vector, vector)
    stacked = P("section", "dp", None)
    out_specs = (stacked, stacked, matrix, vector, matrix, matrix, matrix, vector, matrix, vector, vector)
    return jax.shard_map(shards, mesh=mesh, in_specs=in_specs, out_specs=out_specs, check_vma=False)
```

```python
import functools
import math

import jax
import jax.numpy as jnp
import numpy as np
from jax import lax
from jax.experimental import pallas as pl
from jax.experimental.pallas import tpu as pltpu
from jax.sharding import PartitionSpec as P

BF = jnp.bfloat16
F32 = jnp.float32
MESH = pl.DeviceIdType.MESH
MIB = 2**20

SPAN = 512
D = 512
FF = 1536
ROWS = 2
M = ROWS * SPAN
HALO = 8
PADDED = SPAN + 2 * HALO
STEP = 64
TILE = 256
GRADS = 2 * FF
SMALL = 32
EXP_SCALE = -0.5 * math.log2(math.e)
PDF_SCALE = 1.0 / math.sqrt(2.0 * math.pi)
ERF_SCALE = 1.0 / math.sqrt(2.0)
TAPS, CBIAS, SCALE, SHIFT, DBIAS, GAMMA, UBIAS = 0, 7, 8, 12, 16, 17, 18
SMALL_ROWS = 21
OFFSETS = (0, 1, 2, 4, 5, 6)


def at(start, size):
    return slice(start, start + size) if isinstance(start, int) else pl.ds(start, size)


def times(index, size):
    return index * size if isinstance(index, int) else pl.multiple_of(index * size, size)


def over_rows(value):
    return jnp.sum(value.reshape(value.shape[0] // 8, 8, value.shape[1]), axis=0)


def dot(a, b, dims):
    return lax.dot_general(a, b, (dims, ((), ())), preferred_element_type=F32)


def clip_tables(first, lengths, ids, clip_of, masks, hot):
    for r in range(ROWS):
        row = first + r
        ends = [lengths[row, 0]]
        for c in (1, 2):
            ends.append(ends[-1] + lengths[row, c])
        band_of = [ids[row, c] for c in range(4)]
        clip_of[0:HALO] = jnp.full((HALO, 128), -1.0, F32)
        clip_of[HALO + SPAN :] = jnp.full((HALO, 128), -1.0, F32)
        lane = lax.broadcasted_iota(jnp.int32, (STEP, 128), 1)
        for i in range(SPAN // STEP):
            frame = lax.broadcasted_iota(jnp.int32, (STEP, 128), 0) + i * STEP
            late = [frame >= end for end in ends]
            clip = jnp.where(late[0], 1.0, 0.0) + jnp.where(late[1], 1.0, 0.0) + jnp.where(late[2], 1.0, 0.0)
            clip_of[at(HALO + i * STEP, STEP), :] = clip
            band = jnp.where(late[0], band_of[1], band_of[0])
            band = jnp.where(late[1], band_of[2], band)
            band = jnp.where(late[2], band_of[3], band)
            one = (lane == band) | (lane == band + 4)
            hot[at(r * SPAN + i * STEP, STEP), :] = jnp.where(one, 1.0, 0.0).astype(BF)
        for i in range(SPAN // STEP):
            here = clip_of[at(HALO + i * STEP, STEP), :]
            for q, k in enumerate(OFFSETS):
                there = clip_of[at(HALO + i * STEP + k - 3, STEP), :]
                masks[r, q, at(i * STEP, STEP), :] = jnp.where(there == here, 1.0, 0.0)


def band_table(small, table):
    table[...] = jnp.zeros_like(table)
    for half, first in enumerate((SCALE, SHIFT)):
        whole = small[first : first + 4, :]
        upper = whole.astype(BF).astype(F32)
        both = jnp.concatenate([upper, whole - upper], axis=0)
        table[0:8, half * D : (half + 1) * D] = both.astype(BF)


def weave(*lists):
    order = [((i + 0.5) / len(steps), n, step) for n, steps in enumerate(lists) for i, step in enumerate(steps)]
    for _, _, step in sorted(order, key=lambda entry: entry[:2]):
        step()


def conv_norm(r, x, padded, masks, hot, table, small, normed, rstd_out, adapted):
    def widen():
        for j in range(4):
            padded[r, j, 0:HALO] = jnp.zeros((HALO, 128), F32)
            padded[r, j, HALO + SPAN :] = jnp.zeros((HALO, 128), F32)
            padded[r, j, HALO : HALO + SPAN] = x[r * SPAN : (r + 1) * SPAN, 128 * j : 128 * (j + 1)].astype(F32)

    def tile(i):
        here = at(i * STEP, STEP)
        hidden = []
        for j in range(4):
            c = slice(128 * j, 128 * (j + 1))
            total = small[CBIAS : CBIAS + 1, c] + padded[r, j, at(i * STEP + HALO, STEP), :] * small[3:4, c]
            for q, k in enumerate(OFFSETS):
                moved = padded[r, j, at(i * STEP + (HALO + k - 3), STEP), :]
                total = total + moved * masks[r, q, here, :] * small[k : k + 1, c]
            hidden.append(total)
        mean = jnp.sum(hidden[0] + hidden[1] + hidden[2] + hidden[3], axis=1, keepdims=True) * (1.0 / D)
        center = [h - mean for h in hidden]
        square = [c * c for c in center]
        spread = jnp.sum(square[0] + square[1] + square[2] + square[3], axis=1, keepdims=True) * (1.0 / D)
        rstd = lax.rsqrt(spread + 1e-6)
        rows = at(r * SPAN + i * STEP, STEP)
        tables = dot(hot[rows, :], table[...], ((1,), (0,)))
        rstd_out[rows, :] = jnp.broadcast_to(rstd, (STEP, 128))
        for j in range(4):
            c = slice(128 * j, 128 * (j + 1))
            n = center[j] * rstd
            normed[rows, c] = n
            adapted[rows, c] = (n * tables[:, c] + tables[:, D + 128 * j : D + 128 * (j + 1)]).astype(BF)

    return [widen] + [functools.partial(tile, i) for i in range(SPAN // STEP)]


def up_gelu(r, adapted, w_up, small, g, slope):
    def tile(i, c):
        rows, cols = at(i * TILE, TILE), at(c * TILE, TILE)
        bias = small[UBIAS + c // 2 : UBIAS + c // 2 + 1, at((c % 2) * TILE, TILE)]
        u = dot(adapted[rows, :], w_up[:, cols], ((1,), (0,))) + bias
        pdf = jnp.exp2((u * EXP_SCALE) * u) * PDF_SCALE
        cdf = 0.5 + 0.5 * lax.erf(u * ERF_SCALE)
        g[rows, cols] = (u * cdf).astype(BF)
        slope[rows, cols] = (cdf + u * pdf).astype(BF)

    return [functools.partial(tile, i, c) for i in (2 * r, 2 * r + 1) for c in range(FF // TILE)]


def down(r, x, g, w_down, small, out, upstream, v_out, g_gamma):
    def tile(i, c):
        rows, cols = at(i * TILE, TILE), at(c * TILE, TILE)
        v = dot(g[rows, :], w_down[:, cols], ((1,), (0,))) + small[DBIAS : DBIAS + 1, cols]
        out[rows, cols] = (x[rows, cols].astype(F32) + small[GAMMA : GAMMA + 1, cols] * v).astype(BF)
        if v_out is not None:
            v_out[rows, cols] = v.astype(BF)
        if upstream is not None:
            g_gamma[:, cols] += over_rows(upstream[rows, cols].astype(F32) * v)

    return [functools.partial(tile, i, c) for i in (2 * r, 2 * r + 1) for c in range(2)]


def down_back(r, upstream, w_down, small, slope, dv_out, g_dbias, g_ubias, v, g_gamma):
    def scaled(i):
        rows = at(i * TILE, TILE)
        dy = upstream[rows, :].astype(F32)
        dv = small[GAMMA : GAMMA + 1, :] * dy
        g_dbias[...] += over_rows(dv)
        if v is not None:
            g_gamma[...] += over_rows(dy * v[rows, :].astype(F32))
        dv_out[rows, :] = dv.astype(BF)

    def tile(i, c):
        rows, cols = at(i * TILE, TILE), at(c * TILE, TILE)
        du = dot(dv_out[rows, :], w_down[cols, :], ((1,), (1,))) * slope[rows, cols].astype(F32)
        slope[rows, cols] = du.astype(BF)
        g_ubias[:, cols] += over_rows(du)

    steps = []
    for i in (2 * r, 2 * r + 1):
        steps.append(functools.partial(scaled, i))
        steps += [functools.partial(tile, i, c) for c in range(FF // TILE)]
    return steps


def down_grad(g, dv, out, tiles=range(FF // TILE)):
    for c in tiles:
        cols = at(c * TILE, TILE)
        out[cols, :] = dot(g[:, cols], dv[...], ((0,), (0,))).astype(BF)


def up_grad(adapted, du, out, tiles=range(FF // TILE)):
    for c in tiles:
        place = (at((c // 2) * D, D), at((c % 2) * TILE, TILE))
        out[place] = dot(adapted[...], du[:, at(c * TILE, TILE)], ((0,), (0,))).astype(BF)


def norm_back(r, du, w_up, hot, table, normed, rstd, d_hidden, g_table):
    def tile(i):
        rows = at(i * TILE, TILE)
        da = dot(du[rows, :], w_up[...], ((1,), (1,)))
        n = normed[rows, :]
        dan = da * n
        ones = hot[rows, 0:16]
        g_table[:, 0:D] += dot(ones, dan.astype(BF), ((0,), (0,)))[0:8]
        g_table[:, D:] += dot(ones, da.astype(BF), ((0,), (0,)))[0:8]
        scale = dot(hot[rows, :], table[:, 0:D], ((1,), (0,)))
        dn = da * scale
        mean = jnp.sum(dn, axis=1, keepdims=True) * (1.0 / D)
        along = jnp.sum(dan * scale, axis=1, keepdims=True) * (1.0 / D)
        dh = (dn - mean - n * along) * rstd[rows, 0:1]
        first = i * TILE % SPAN
        for j in range(4):
            d_hidden[r, j, at(HALO + first, TILE), :] = dh[:, 128 * j : 128 * (j + 1)]

    return [functools.partial(tile, i) for i in (2 * r, 2 * r + 1)]


def conv_back(r, x, upstream, d_hidden, masks, small, g_taps, g_cbias, out):
    def edges():
        for j in range(4):
            d_hidden[r, j, 0:HALO] = jnp.zeros((HALO, 128), F32)
            d_hidden[r, j, HALO + SPAN :] = jnp.zeros((HALO, 128), F32)

    def tile(i):
        rows = at(r * SPAN + i * STEP, STEP)
        here = at(i * STEP, STEP)
        for j in range(4):
            c = slice(128 * j, 128 * (j + 1))
            value = x[rows, c].astype(F32)
            dh = d_hidden[r, j, at(i * STEP + HALO, STEP), :]
            total = upstream[rows, c].astype(F32) + dh * small[3:4, c]
            g_cbias[:, c] += over_rows(dh)
            g_taps[3, :, c] += over_rows(value * dh)
            for q, k in enumerate(OFFSETS):
                part = d_hidden[r, j, at(i * STEP + (HALO + k - 3), STEP), :] * masks[r, q, here, :]
                total = total + part * small[6 - k : 7 - k, c]
                g_taps[6 - k, :, c] += over_rows(value * part)
            out[rows, c] = total.astype(out.dtype)

    return [edges] + [functools.partial(tile, i) for i in range(SPAN // STEP)]


def small_grads(out, g_taps, g_cbias, g_table, g_dbias, g_gamma, g_ubias):
    def whole(value):
        return jnp.sum(value, axis=0, keepdims=True)

    rows = [whole(g_taps[k]) for k in range(7)] + [whole(g_cbias[...])]
    rows += [g_table[0:4, 0:D], g_table[0:4, D:], whole(g_dbias[...]), whole(g_gamma[...])]
    rows += [whole(g_ubias[:, k * D : (k + 1) * D]) for k in range(3)]
    rows.append(jnp.zeros((SMALL - SMALL_ROWS, D), F32))
    out[...] = jnp.concatenate(rows, axis=0)


PARTS = 3
PART_ROWS = FF // PARTS
QUARTER = PART_ROWS // 4
PIECE = (16, 256)
STRIDES = (16, 4, 1)
LAST = ("first+", "first-", "second+", "second-", "own", "pass+", "pass-")


def train_kernel(
    lengths, ids, conv_weight, conv_bias, scale_table, shift_table, b_down, layer_scale, b_up,
    frames, cotangent, own_up, own_down,
    acts_all, grads_all, weight_all, small_all,
    h_taps, h_cbias, h_scale, h_shift, h_dbias, h_gamma, h_ubias,
    x0, cot, small, w_up, w_down, acts, grads, weight_grads, small_sums,
    padded, masks, hot, table, normed, rstd, adapted, g, slope,
    g_table, g_taps, g_cbias, g_dbias, g_ubias, g_gamma,
    pair, final, line_got, plane_got, line_sum, small_got, small_sum, plane_small, small_held,
    load_sems, store_sems, swap_send, swap_recv, pair_send, pair_recv, row_send, row_recv,
    line_send, line_recv, plane_send, plane_recv, plane_back_send, plane_back_recv, line_back_send, line_back_recv,
    small_send, small_recv,
):
    section = lax.axis_index("section")
    dp = lax.axis_index("dp")
    coords = (dp // 16, (dp // 4) % 4, dp % 4)
    other = {"dp": dp, "section": 1 - section}
    mine = pl.ds(pl.multiple_of(section * M, M), M)
    v0, dv = acts.at[1], grads.at[0]

    ring = [[lax.rem(coords[axis] + distance, 4) for distance in range(4)] for axis in range(3)]
    step = [[(ring[axis][d] - coords[axis]) * STRIDES[axis] for d in range(4)] for axis in range(3)]
    line_dp = [[dp + step[axis][d] for d in range(4)] for axis in range(3)]

    def along(axis, distance):
        return ring[axis][distance]

    def peer(axis, distance):
        return {"dp": line_dp[axis][distance], "section": section}

    def crossed(axis, distance):
        return {"dp": line_dp[axis][distance], "section": 1 - section}

    plane_dp = [[[line_dp[(p + 1) % 3][u] + step[(p + 2) % 3][v] for v in range(4)] for u in range(4)] for p in range(3)]

    def plane_peer(p, u, v):
        return {"dp": plane_dp[p][u][v], "section": section}

    plane = [(u, v) for u in range(4) for v in range(4) if u or v]

    def remote(src, dst, send_sem, recv_sem, device):
        return pltpu.make_async_remote_copy(
            src_ref=src, dst_ref=dst, send_sem=send_sem, recv_sem=recv_sem, device_id=device, device_id_type=MESH
        )

    loads = [
        pltpu.make_async_copy(frames.at[mine], x0, load_sems.at[0]),
        pltpu.make_async_copy(own_up, w_up.at[section], load_sems.at[1]),
        pltpu.make_async_copy(own_down, w_down.at[section], load_sems.at[2]),
        pltpu.make_async_copy(cotangent.at[mine], cot, load_sems.at[3]),
    ]
    given = (conv_weight, conv_bias, scale_table, shift_table, b_down, layer_scale, b_up)
    packs = [
        pltpu.make_async_copy(src, dst, load_sems.at[4 + i])
        for i, (src, dst) in enumerate(zip(given, (h_taps, h_cbias, h_scale, h_shift, h_dbias, h_gamma, h_ubias)))
    ]
    for load in packs + loads:
        load.start()
    barrier = pltpu.get_barrier_semaphore()
    pl.semaphore_signal(barrier, inc=1, device_id=other, device_id_type=MESH)
    for axis in range(3):
        for distance in (1, 2, 3):
            pl.semaphore_signal(barrier, inc=1, device_id=peer(axis, distance), device_id_type=MESH)
            pl.semaphore_signal(barrier, inc=1, device_id=crossed(axis, distance), device_id_type=MESH)
        for u, v in plane:
            if u and v:
                pl.semaphore_signal(barrier, inc=1, device_id=plane_peer(axis, u, v), device_id_type=MESH)
    for load in packs:
        load.wait()
    rows = [h_taps[k] for k in range(7)] + [h_cbias[...], h_scale[0], h_shift[0], h_dbias[...], h_gamma[...]]
    rows += [h_ubias[:, k * D : (k + 1) * D] for k in range(3)] + [jnp.zeros((24 - SMALL_ROWS, D), F32)]
    small[section] = jnp.concatenate(rows, axis=0)
    pl.semaphore_wait(barrier, 46)
    swaps = [
        remote(small.at[section], small.at[section], swap_send.at[0], swap_recv.at[0], other),
        remote(own_up, w_up.at[section], swap_send.at[1], swap_recv.at[1], other),
        remote(own_down, w_down.at[section], swap_send.at[2], swap_recv.at[2], other),
    ]
    for swap in swaps:
        swap.start()

    def part_rows(p):
        return at(p * PART_ROWS, PART_ROWS)

    def to_adder(b, h, p):
        rows, i = part_rows(p), h * PARTS + p
        return remote(weight_grads.at[b, h, rows], pair.at[h, rows], pair_send.at[i], pair_recv.at[i], other)

    def kept_rows(b, kind, source, target):
        return pltpu.make_async_copy(source, target.at[mine], store_sems.at[2 * kind + b])

    def sent_rows(b, kind, source, target):
        i = 2 * kind + b
        return remote(source, target.at[mine], row_send.at[i], row_recv.at[i], other)

    def start_rows(b, *what):
        @pl.when(section == b)
        def _():
            kept_rows(b, *what).start()

        @pl.when(section != b)
        def _():
            sent_rows(b, *what).start()

    def finish_rows(b, *what):
        @pl.when(section == b)
        def _():
            kept_rows(b, *what).wait()
            sent_rows(b, *what).wait_recv()

        @pl.when(section != b)
        def _():
            sent_rows(b, *what).wait_send()

    def quarter(p, distance):
        first = p * PART_ROWS + along(p, distance) * QUARTER
        return pl.ds(pl.multiple_of(first, QUARTER), QUARTER)

    def piece(first, p, u, v):
        i, j = along((p + 1) % 3, u), along((p + 2) % 3, v)
        rows = pl.ds(pl.multiple_of(first + i * 32 + (j // 2) * 16, 16), 16)
        return rows, pl.ds(pl.multiple_of(lax.rem(j, 2) * 256, 256), 256)

    def own_piece(p):
        return piece(p * PART_ROWS + coords[p] * QUARTER, p, 0, 0)

    def line(b, h, p):
        made = []
        for distance in (1, 2, 3):
            i = (h * PARTS + p) * 3 + distance - 1
            src, dst = weight_grads.at[b, h, quarter(p, distance)], line_got.at[h, p, distance - 1]
            made.append(remote(src, dst, line_send.at[i], line_recv.at[i], peer(p, distance)))
        return made

    HALVES = (at(0, 256), at(256, 256))

    def last(p, name):
        i = LAST.index(name) + p * len(LAST)
        if name == "own":
            rows = quarter(p, 0)
            src, dst, to = pair.at[:, rows], final.at[:, rows], other
        elif name in ("pass+", "pass-"):
            away, half, towards = (3, 0, 1) if name == "pass+" else (1, 1, 3)
            src = dst = final.at[:, quarter(p, away), HALVES[half]]
            to = peer(p, towards)
        else:
            towards = 1 if name[-1] == "+" else 3
            half = {"first+": 0, "second+": 1, "first-": 1, "second-": 0}[name]
            rows = quarter(p, 0)
            src, dst, to = pair.at[:, rows, HALVES[half]], final.at[:, rows, HALVES[half]], crossed(p, towards)
        return remote(src, dst, line_back_send.at[i], line_back_recv.at[i], to)

    def spread(p):
        made = []
        for j, (u, v) in enumerate(plane):
            rows, cols = piece(0, p, u, v)
            src = line_sum.at[:, p, rows, cols]
            made.append(remote(src, plane_got.at[p, j], plane_send.at[p], plane_recv.at[p], plane_peer(p, u, v)))
        return made

    def spread_back(p):
        rows, cols = own_piece(p)
        kept = pair.at[:, rows, cols]
        return [remote(kept, kept, plane_back_send.at[p], plane_back_recv.at[p], plane_peer(p, u, v)) for u, v in plane]

    def fifteen(p, sems):
        return pltpu.make_async_copy(plane_got.at[p], plane_got.at[p], sems.at[p])

    def start(copies):
        for copy in copies:
            copy.start()

    def arrived(copies):
        for copy in copies:
            copy.wait_recv()

    def keep(p):
        rows = part_rows(p)
        return pltpu.make_async_copy(final.at[:, rows], weight_all.at[:, rows], store_sems.at[4 + p])

    def add_pair(b, h, p):
        to_adder(b, h, p).wait_recv()
        rows = part_rows(p)
        weight_grads[b, h, rows, :] = weight_grads[b, h, rows, :] + pair[h, rows, :]
        start(line(b, h, p))

    def add_line(b, p):
        for h in range(2):
            arrived(line(b, h, p))
            total = weight_grads[b, h, quarter(p, 0), :].astype(F32)
            for d in range(3):
                total = total + line_got[h, p, d].astype(F32)
            line_sum[h, p] = total.astype(BF)
        start(spread(p))

    def add_plane(p):
        fifteen(p, plane_recv).wait()
        rows, cols = piece(0, p, 0, 0)
        total = line_sum[:, p, rows, cols].astype(F32)
        for j in range(15):
            total = total + plane_got[p, j].astype(F32)
        rows, cols = own_piece(p)
        pair[:, rows, cols] = total.astype(BF)
        start(spread_back(p))

    def send_line(p):
        fifteen(p, plane_back_recv).wait()
        start([last(p, name) for name in LAST[:5]])

    def pass_on(p):
        for sign in "+-":
            last(p, "first" + sign).wait_recv()
            last(p, "pass" + sign).start()

    def store_part(p):
        arrived([last(p, name) for name in LAST[2:]])
        keep(p).start()

    def adder(b, act, *todo):
        @pl.when(section != b)
        def _():
            for what in todo:
                act(*what)

    every = [(p,) for p in range(PARTS)]

    def hand_over(b, h, parts=range(PARTS)):
        @pl.when(section == b)
        def _():
            for p in parts:
                to_adder(b, h, p).start()

    clip_tables(section * ROWS, lengths, ids, padded.at[0, 0], masks, hot)
    for ref in (g_table, g_taps, g_cbias, g_dbias, g_ubias, g_gamma):
        ref[...] = jnp.zeros_like(ref)
    def needs(b, *parts):
        @pl.when(section == b)
        def _():
            for i in parts:
                if i:
                    loads[i].wait()

        @pl.when(section != b)
        def _():
            for i in parts:
                swaps[i].wait_recv()

    needs(0, 0)
    band_table(small.at[0], table.at[0])
    loads[0].wait()

    def norms(b, r, x):
        return conv_norm(
            r, x, padded, masks, hot, table.at[b], small.at[b], normed.at[b], rstd.at[b], adapted.at[b]
        )

    def ups(b, r):
        return up_gelu(r, adapted.at[b], w_up.at[b], small.at[b], g.at[b], slope.at[b])

    def downs(b, r):
        if b == 0:
            return down(r, x0, g.at[0], w_down.at[0], small.at[0], acts.at[0], None, v0, None)
        return down(r, acts.at[0], g.at[1], w_down.at[1], small.at[1], acts.at[1], cot, None, g_gamma.at[1])

    def down_backs(b, r):
        dy, v = ((grads.at[1], v0), (cot, None))[b]
        return down_back(
            r, dy, w_down.at[b], small.at[b], slope.at[b], dv, g_dbias.at[b], g_ubias.at[b], v, g_gamma.at[b]
        )

    def norm_backs(b, r):
        return norm_back(
            r, slope.at[b], w_up.at[b], hot, table.at[b], normed.at[b], rstd.at[b], padded, g_table.at[b]
        )

    def conv_backs(b, r):
        x, dy = ((x0, grads.at[1]), (acts.at[0], cot))[b]
        return conv_back(r, x, dy, padded, masks, small.at[b], g_taps.at[b], g_cbias.at[b], grads.at[b])

    weave(norms(0, 0, x0))
    needs(0, 1)
    weave(norms(0, 1, x0), ups(0, 0))
    needs(0, 2)
    weave(ups(0, 1), downs(0, 0))
    needs(1, 0, 1, 2)
    band_table(small.at[1], table.at[1])
    loads[3].wait()
    weave(norms(1, 0, acts.at[0]))
    weave(ups(1, 0), downs(0, 1))
    start_rows(0, 0, acts.at[0], acts_all)
    weave(norms(1, 1, acts.at[0]))
    weave(ups(1, 1), down_backs(1, 0))

    weave(down_backs(1, 1))
    down_grad(g.at[1], dv, weight_grads.at[1, 0])
    hand_over(1, 0)
    up_grad(adapted.at[1], slope.at[1], weight_grads.at[1, 1])
    hand_over(1, 1)
    weave(norm_backs(1, 0))
    weave(norm_backs(1, 1), conv_backs(1, 0))
    adder(1, add_pair, *[(1, 0, p) for p in range(PARTS)])
    weave(conv_backs(1, 1), down_backs(0, 0))
    start_rows(1, 1, grads.at[1], grads_all)
    adder(1, add_pair, *[(1, 1, p) for p in range(PARTS)])
    weave(down_backs(0, 1))
    for p in range(PARTS):
        down_grad(g.at[0], dv, weight_grads.at[0, 0], (2 * p, 2 * p + 1))
        hand_over(0, 0, (p,))
    for p in range(PARTS):
        up_grad(adapted.at[0], slope.at[0], weight_grads.at[0, 1], (2 * p, 2 * p + 1))
        hand_over(0, 1, (p,))
        adder(0, add_pair, (0, 0, p))
    adder(0, add_pair, *[(0, 1, p) for p in range(PARTS)])
    adder(1, add_line, *[(1, p) for p in range(PARTS)])
    weave(norm_backs(0, 0))
    weave(norm_backs(0, 1), conv_backs(0, 0))
    weave(conv_backs(0, 1), downs(1, 0), downs(1, 1))
    start_rows(0, 1, grads.at[0], grads_all)
    start_rows(1, 0, acts.at[1], acts_all)
    for b in range(2):
        small_grads(
            small_sums.at[b], g_taps.at[b], g_cbias.at[b], g_table.at[b], g_dbias.at[b], g_gamma.at[b], g_ubias.at[b]
        )

    def eighth(index):
        return pl.ds(pl.multiple_of(index * 8, 8), 8)

    def small_out():
        made = []
        for i in range(1, 8):
            distance = i // 2
            b = 1 - section if i % 2 else section
            to = crossed(0, distance) if i % 2 else peer(0, distance)
            src = small_sums.at[b, eighth(along(0, distance))]
            made.append(remote(src, small_got.at[i - 1], small_send.at[i - 1], small_recv.at[i - 1], to))
        return made

    def small_plane():
        return [
            remote(small_sum, plane_small.at[j], small_send.at[7], small_recv.at[7], plane_peer(0, u, v))
            for j, (u, v) in enumerate(plane)
        ]

    def small_plane_wait(sems):
        return pltpu.make_async_copy(plane_small, plane_small, sems.at[7])

    def small_back():
        kept = small_held.at[eighth(coords[0])]
        return [remote(kept, kept, small_send.at[7 + d], small_recv.at[7 + d], peer(0, d)) for d in (1, 2, 3)]

    start(small_out())
    adder(1, add_plane, *every)
    adder(0, add_line, *[(0, p) for p in range(PARTS)])
    arrived(small_out())
    total = small_sums[section, eighth(coords[0]), :]
    for i in range(7):
        total = total + small_got[i]
    small_sum[...] = jnp.concatenate([total[:, 0:256], total[:, 256:]], axis=0).astype(BF)
    start(small_plane())
    adder(0, add_plane, *every)
    small_plane_wait(small_recv).wait()
    total = small_sum[...].astype(F32)
    for j in range(15):
        total = total + plane_small[j].astype(F32)
    small_held[eighth(coords[0]), :] = jnp.concatenate([total[0:8], total[8:16]], axis=1)
    start(small_back())
    adder(1, send_line, *every)
    adder(0, send_line, *every)
    adder(0, pass_on, *every)
    arrived(small_back())
    small_keep = pltpu.make_async_copy(small_held, small_all, store_sems.at[7])
    small_keep.start()
    adder(1, pass_on, *every)
    for p in range(PARTS):
        store_part(p)

    for swap in swaps:
        swap.wait_send()
    for b in range(2):
        finish_rows(b, 0, acts.at[b], acts_all)
        finish_rows(b, 1, grads.at[b], grads_all)

        @pl.when(section == b)
        def _():
            for h in range(2):
                for p in range(PARTS):
                    to_adder(b, h, p).wait_send()

        @pl.when(section != b)
        def _():
            for h in range(2):
                for p in range(PARTS):
                    for copy in line(b, h, p):
                        copy.wait_send()

    for p in range(PARTS):
        for name in LAST:
            last(p, name).wait_send()
        fifteen(p, plane_send).wait()
        fifteen(p, plane_back_send).wait()
        keep(p).wait()
    for copy in small_out() + small_back():
        copy.wait_send()
    small_plane_wait(small_send).wait()
    small_keep.wait()


def train(*arrays):
    smem = pl.BlockSpec(memory_space=pltpu.SMEM)
    hbm = pl.BlockSpec(memory_space=pl.ANY)
    return pl.pallas_call(
        train_kernel,
        out_shape=[
            jax.ShapeDtypeStruct((2 * M, D), BF),
            jax.ShapeDtypeStruct((2 * M, D), BF),
            jax.ShapeDtypeStruct((2, FF, D), BF),
            jax.ShapeDtypeStruct((SMALL, D), F32),
        ],
        in_specs=[smem, smem] + [hbm] * 11,
        out_specs=[hbm] * 4,
        scratch_shapes=[
            pltpu.VMEM(shape, F32)
            for shape in ((7, 1, D), (1, D), (1, 4, D), (1, 4, D), (1, D), (1, D), (1, FF))
        ]
        + [
            pltpu.VMEM((M, D), BF),
            pltpu.VMEM((M, D), BF),
            pltpu.VMEM((2, 24, D), F32),
            pltpu.VMEM((2, D, FF), BF),
            pltpu.VMEM((2, FF, D), BF),
            pltpu.VMEM((2, M, D), BF),
            pltpu.VMEM((2, M, D), BF),
            pltpu.VMEM((2, 2, FF, D), BF),
            pltpu.VMEM((2, SMALL, D), F32),
            pltpu.VMEM((ROWS, 4, PADDED, 128), F32),
            pltpu.VMEM((ROWS, 6, SPAN, 128), F32),
            pltpu.VMEM((M, 128), BF),
            pltpu.VMEM((2, 128, 2 * D), BF),
            pltpu.VMEM((2, M, D), F32),
            pltpu.VMEM((2, M, 128), F32),
            pltpu.VMEM((2, M, D), BF),
            pltpu.VMEM((2, M, FF), BF),
            pltpu.VMEM((2, M, FF), BF),
            pltpu.VMEM((2, 8, 2 * D), F32),
            pltpu.VMEM((2, 7, 8, D), F32),
            pltpu.VMEM((2, 8, D), F32),
            pltpu.VMEM((2, 8, D), F32),
            pltpu.VMEM((2, 8, FF), F32),
            pltpu.VMEM((2, 8, D), F32),
            pltpu.VMEM((2, FF, D), BF),
            pltpu.VMEM((2, FF, D), BF),
            pltpu.VMEM((2, PARTS, 3, QUARTER, D), BF),
            pltpu.VMEM((PARTS, 15, 2) + PIECE, BF),
            pltpu.VMEM((2, PARTS, QUARTER, D), BF),
            pltpu.VMEM((7, 8, D), F32),
            pltpu.VMEM((16, 256), BF),
            pltpu.VMEM((15, 16, 256), BF),
            pltpu.VMEM((SMALL, D), F32),
        ]
        + [pltpu.SemaphoreType.DMA((n,)) for n in (11, 8, 3, 3, 6, 6, 4, 4, 18, 18, 3, 3, 3, 3, 21, 21, 11, 11)],
        compiler_params=pltpu.CompilerParams(collective_id=0, has_side_effects=True, vmem_limit_bytes=63 * MIB),
        cost_estimate=pl.CostEstimate(flops=24 * M * D * FF, bytes_accessed=24 * MIB, transcendentals=4 * M * FF),
    )(*arrays)


def finish_kernel(
    acts, grads, weights, small,
    acts_out, grads_out, g_taps, g_cbias, g_scale, g_shift, g_up, g_ubias, g_down, g_dbias, g_gamma,
    h_taps, h_cbias, h_scale, h_shift, h_ubias, h_dbias, h_gamma,
    held_small, held, half_grads, half_weights, full_grads, full_weights, load_sems, store_sems,
):
    loads = [pltpu.make_async_copy(small, held_small, load_sems.at[0])]
    for i in range(4):
        rows = at(i * D, D)
        loads.append(pltpu.make_async_copy(grads.at[rows], half_grads.at[rows], load_sems.at[1 + i]))
    for i in range(6):
        rows = at(i * D, D)
        loads.append(
            pltpu.make_async_copy(weights.at[i // 3, at(i % 3 * D, D)], half_weights.at[rows], load_sems.at[5 + i])
        )
    for i in range(4):
        rows = at(i * D, D)
        loads.append(pltpu.make_async_copy(acts.at[rows], held.at[rows], load_sems.at[11 + i]))
    for load in loads:
        load.start()
    stores = []

    def store(src, dst):
        copy = pltpu.make_async_copy(src, dst, store_sems.at[len(stores)])
        copy.start()
        stores.append(copy)

    for i in range(10):
        rows = at((i if i < 4 else i - 4) * D, D)
        loads[1 + i].wait()
        if i < 4:
            full_grads[rows, :] = half_grads[rows, :].astype(F32)
            store(full_grads.at[rows], grads_out.at[0, rows])
        else:
            full_weights[rows, :] = half_weights[rows, :].astype(F32)
            store(full_weights.at[rows], g_down.at[0, rows] if i < 7 else g_up.at[0, :, at((i - 7) * D, D)])
        if i == 0:
            loads[0].wait()
            h_taps[...] = jnp.concatenate([held_small[TAPS + k : TAPS + k + 1, :][None] for k in range(7)], axis=0)
            h_cbias[...] = held_small[CBIAS : CBIAS + 1, :]
            h_scale[0] = held_small[SCALE : SCALE + 4, :]
            h_shift[0] = held_small[SHIFT : SHIFT + 4, :]
            h_dbias[...] = held_small[DBIAS : DBIAS + 1, :]
            h_gamma[...] = held_small[GAMMA : GAMMA + 1, :]
            for k in range(3):
                h_ubias[:, at(k * D, D)] = held_small[UBIAS + k : UBIAS + k + 1, :]
            held_outs = (h_taps, h_cbias, h_scale, h_shift, h_ubias, h_dbias, h_gamma)
            for src, dst in zip(held_outs, (g_taps, g_cbias, g_scale, g_shift, g_ubias, g_dbias, g_gamma)):
                store(src, dst)
    for i in range(4):
        loads[11 + i].wait()
        rows = at(i * D, D)
        store(held.at[rows], acts_out.at[0, rows])
    for copy in stores:
        copy.wait()


def finish(acts, grads, weights, small):
    hbm = pl.BlockSpec(memory_space=pl.ANY)
    shapes = ((7, 1, D), (1, D), (1, 4, D), (1, 4, D), (1, FF), (1, D), (1, D))

    def out(*shape, kind=F32):
        return jax.ShapeDtypeStruct(shape, kind)

    return pl.pallas_call(
        finish_kernel,
        out_shape=[
            out(1, 2 * M, D, kind=BF), out(1, 2 * M, D), out(7, 1, D), out(1, D), out(1, 4, D), out(1, 4, D),
            out(1, D, FF), out(1, FF), out(1, FF, D), out(1, D), out(1, D),
        ],
        in_specs=[hbm] * 4,
        out_specs=[hbm] * 11,
        scratch_shapes=[pltpu.VMEM(shape, F32) for shape in shapes]
        + [
            pltpu.VMEM((SMALL, D), F32),
            pltpu.VMEM((2 * M, D), BF),
            pltpu.VMEM((2 * M, D), BF),
            pltpu.VMEM((GRADS, D), BF),
            pltpu.VMEM((2 * M, D), F32),
            pltpu.VMEM((GRADS, D), F32),
            pltpu.SemaphoreType.DMA((15,)),
            pltpu.SemaphoreType.DMA((21,)),
        ],
        compiler_params=pltpu.CompilerParams(vmem_limit_bytes=60 * MIB),
    )(acts, grads, weights, small)


def shards(
    frames, cotangent, lengths, bw_ids, conv_weight, conv_bias, scale_table, shift_table,
    w_up, b_up, w_down, b_down, layer_scale,
):
    acts, grads, weights, small = train(
        lengths, bw_ids, jnp.transpose(conv_weight, (1, 0, 2)), conv_bias, scale_table, shift_table, b_down, layer_scale, b_up,
        frames, cotangent, w_up[0], w_down[0],
    )
    outs = list(finish(acts, grads, weights, small))
    outs[2] = jnp.transpose(outs[2], (1, 0, 2))
    return tuple(outs)


def solution(mesh):
    rows = P("dp", None)
    matrix, vector = P("section", None, None), P("section", None)
    in_specs = (rows,) * 4 + (matrix, vector, matrix, matrix, matrix, vector, matrix, vector, vector)
    stacked = P("section", "dp", None)
    out_specs = (stacked, stacked, matrix, vector, matrix, matrix, matrix, vector, matrix, vector, vector)
    return jax.shard_map(shards, mesh=mesh, in_specs=in_specs, out_specs=out_specs, check_vma=False)
```
